32 devices in a mesh: az: 8 (over y, x, core), rad: 4 (over z).
Axes of the slice: x: 2, y: 2, z: 4, core: 2. Of those that a mesh axis runs over, the one named last changes fastest.
Arguments:
- velocity: float32 [3, 128, 512, 128], P(None, 'rad', 'az'), may hold values from -6 to 6
- dumbbells: float32 [3, 4, 8, 4096], P(None, 'rad', 'az'), may hold values from -1.6 to 1.6
- cell_ids: int32 [2, 4, 8, 4096], P(None, 'rad', 'az'), may hold values from 0 to 2047, as said below
- brownian: float32 [3, 4, 8, 4096], P(None, 'rad', 'az'), may hold values from -5 to 5
- stencil_coef: float32 [9, 128], P(None, 'rad'), may hold values from -3 to 3
- block_inverse: float32 [128, 32], P('rad'), may hold values from -1 to 4, as said below
- azim_coef: float32 [128], P('rad'), may hold values from 1e-05 to 10
Outputs:
- velocity_next: float32 [3, 128, 512, 128], P(None, 'rad', 'az')
- dumbbells_next: float32 [3, 4, 8, 4096], P(None, 'rad', 'az')
The draws below stay inside these ranges and needn't reach their ends.
Inputs may be any that keep to these rules, and one draw needn't show every extreme that they name: cell_ids[0] is local radius times 64 plus local azimuth within the block, below 2048; cell_ids[1] is below 128. `block_inverse`: row r holds the weights that map the stencil sums of its radial block to the derivative at r.
All inputs are finite; a program needn't handle non-finite values.
Results may differ from the reference program's by a relative error of at most 0.000064.
Values sent between devices are 32-bit elements; how exact they have to be, the bound alone decides.
No kernel may reach another device: no remote copies, remote signals or barrier semaphores. Data moves between devices by JAX's collectives and lax.ppermute only.
A program may use at most 192 MiB of HBM per device.

```python
import math
import jax
import jax.numpy as jnp
from jax import lax

NT = 512
CR = 32
ZW = 128
PD = 4096
NR = 128
CT = 64
N_AZ = 8
N_RAD = 4


def draw_cell_ids(key, part):
    key = jax.random.fold_in(key, 11)
    plane_key, axial_key = jax.random.split(key)
    plane_cell = jax.random.randint(plane_key, (N_RAD, N_AZ, PD), 0, CR * CT)
    axial_cell = jax.random.randint(axial_key, (N_RAD, N_AZ, PD), 0, ZW)
    plane_cell = plane_cell.at[:, :, 0].set(CR * CT - 1)
    plane_cell = plane_cell.at[:, :, 2].set(0)
    axial_cell = axial_cell.at[:, :, 1].set(ZW - 1)
    axial_cell = axial_cell.at[:, :, 3].set(0)
    return jnp.stack([plane_cell, axial_cell]).astype(jnp.int32)


def draw_block_inverse(key, part):
    key = jax.random.fold_in(key, 23)
    ratio_key, spread_key = jax.random.split(key)
    row_index = (jnp.arange(NR, dtype=jnp.int32) % CR)[:, None]
    col_index = jnp.arange(CR, dtype=jnp.int32)[None, :]
    distance = jnp.abs(row_index - col_index)
    parity = (1 - 2 * (distance % 2)).astype(jnp.float32)
    decay_ratio = jax.random.uniform(ratio_key, (NR, 1), minval=0.2, maxval=0.35)
    spread = 0.15 * jax.random.normal(spread_key, (NR, CR))
    spread = jnp.clip(spread, -0.3, 0.3)
    magnitude = jnp.exp(distance.astype(jnp.float32) * jnp.log(decay_ratio))
    diagonal = jnp.where(distance == 0, 2.5, 1.0)
    value = parity * magnitude * diagonal * (1.0 + spread)
    return value.astype(jnp.float32)


def block_levels(key, extent, cuts, low, top_value):
    def one(dim, blocks):
        steps = jax.random.uniform(jax.random.fold_in(jax.random.fold_in(key, 6), dim), (blocks,), jnp.float32, low / len(cuts), top_value / len(cuts))
        return jnp.repeat(jnp.exp(steps), extent[dim] // blocks).reshape((-1,) + (1,) * (len(extent) - dim - 1))

    gain = one(*cuts[0])
    for cut in cuts[1:]:
        gain = gain * one(*cut)
    return gain


def scatter_about(rng, extent, width, limit, cuts=(), kind=jnp.bfloat16):
    values = jax.random.normal(rng, extent, jnp.float32) * width
    if len(cuts) > 0:
        values = block_levels(rng, extent, cuts, -0.22, 0.18) * values
    return jnp.clip(values, min=-limit, max=limit).astype(kind)


def setup_inputs(seed: int = 0) -> dict:
    keys = jax.random.split(jax.random.key(seed), 8)
    velocity = scatter_about(keys[0], (3, NR, NT, ZW), 1.0, 6.0, ((1, 4), (2, 8)), jnp.float32)
    dumbbells = jnp.clip(jax.random.uniform(keys[1], (3, N_RAD, N_AZ, PD), jnp.float32, -1.6, 1.6) * block_levels(keys[1], (3, N_RAD, N_AZ, PD), ((1, 4), (2, 8)), -0.4, 0.0), -1.6, 1.6)
    cell_ids = draw_cell_ids(jax.random.fold_in(keys[7], 71), 0)
    brownian = scatter_about(keys[3], (3, N_RAD, N_AZ, PD), 1.0, 5.0, ((1, 4), (2, 8)), jnp.float32)
    stencil_coef = scatter_about(keys[4], (9, NR), 0.5, 3.0, ((1, 4),), jnp.float32)
    block_inverse = draw_block_inverse(jax.random.fold_in(keys[7], 71), 0)
    azim_coef = jnp.clip(jnp.exp(math.log(10.0) - 13.815511 * jax.random.uniform(keys[6], (NR,), jnp.float32) ** block_levels(keys[6], (NR,), ((0, 4),), -0.2, 0.2)), 9.999999747378752e-06, 10.0)
    return dict(velocity=velocity, dumbbells=dumbbells, cell_ids=cell_ids, brownian=brownian, stencil_coef=stencil_coef, block_inverse=block_inverse, azim_coef=azim_coef)


TIME_STEP = 0.05
MAX_STRETCH = 10.0
STRESS_SCALE = 4.0
PRECISE = lax.Precision.HIGHEST

def radial_derivative(field, stencil_coef, block_inverse):
    inverse = block_inverse.reshape(N_RAD, CR, CR)

    def one_component(component):
        padded = jnp.pad(component, ((4, 4), (0, 0), (0, 0)))
        stencil_sum = stencil_coef[0][:, None, None] * padded[0:NR]
        for offset in range(1, 9):
            stencil_sum = stencil_sum + stencil_coef[offset][:, None, None] * padded[offset:offset + NR]
        blocks = stencil_sum.reshape(N_RAD, CR, NT, ZW)
        result = jnp.einsum('bij,bjtz->bitz', inverse, blocks, precision=PRECISE)
        return result.reshape(NR, NT, ZW)
    return lax.map(one_component, field)

def azimuth_solve(velocity, azim_coef):
    wave_numbers = jnp.arange(NT // 2 + 1).astype(jnp.float32)
    damping = 1.0 / (1.0 + azim_coef[:, None] * wave_numbers[None, :] * wave_numbers[None, :])

    def one_component(component):
        spectrum = jnp.fft.rfft(component, axis=1)
        return jnp.fft.irfft(spectrum * damping[:, :, None], n=NT, axis=1)
    return lax.map(one_component, velocity)

def reference(velocity, dumbbells, cell_ids, brownian, stencil_coef, block_inverse, azim_coef):
    radial_grad = radial_derivative(velocity, stencil_coef, block_inverse)
    block_rad = jnp.arange(N_RAD, dtype=jnp.int32)[:, None, None]
    block_az = jnp.arange(N_AZ, dtype=jnp.int32)[None, :, None]
    plane_cell = cell_ids[0]
    axial_cell = cell_ids[1]
    radius = block_rad * CR + plane_cell // CT
    azimuth = block_az * CT + plane_cell % CT
    flat_cell = ((radius * NT + azimuth) * ZW + axial_cell).reshape(-1).astype(jnp.int32)
    spring = dumbbells.reshape(3, -1)
    noise = brownian.reshape(3, -1)
    shear = jnp.take(radial_grad.reshape(3, -1), flat_cell, axis=1)
    stretch_sq = lax.optimization_barrier(jnp.sum(spring * spring, axis=0))
    fene_factor = 1.0 / (1.0 - stretch_sq / MAX_STRETCH)
    moved = spring + TIME_STEP * (shear * spring[0] - 0.5 * fene_factor * spring) + math.sqrt(TIME_STEP) * noise
    weighted = STRESS_SCALE * fene_factor * spring[0] * spring
    stress = jnp.zeros((3, NR * NT * ZW), weighted.dtype).at[:, flat_cell].add(weighted)
    stress = stress.reshape(3, NR, NT, ZW)
    polymer_force = radial_derivative(stress, stencil_coef, block_inverse)
    smooth = azimuth_solve(velocity, azim_coef)
    velocity_next = smooth + TIME_STEP * polymer_force
    return (velocity_next, moved.reshape(dumbbells.shape))
```

```python
import functools
import math

import jax
import jax.numpy as jnp
import numpy as np
from jax import lax
from jax.experimental import pallas as pl
from jax.experimental.pallas import tpu as pltpu
from jax.sharding import PartitionSpec as P

TIME_STEP = 0.05
MAX_STRETCH = 10.0
STRESS_SCALE = 4.0
PRECISE = lax.Precision.HIGHEST
HALO = 4
SUB = 8
VMEM_LIMIT = 56 * 1024 * 1024
F32 = jnp.float32
BF16 = jnp.bfloat16


def split(value):
    high = value.astype(BF16)
    return high, (value - high.astype(F32)).astype(BF16)


def dot(a, b):
    return jnp.dot(a, b, preferred_element_type=F32)


def dot3(a_high, a_low, b_high, b_low):
    return dot(a_high, b_high) + dot(a_high, b_low) + dot(a_low, b_high)


def derivative_matrix(stencil_coef, block_inverse):
    rows = stencil_coef.shape[1]
    wide = rows + 2 * HALO
    offset = lax.broadcasted_iota(jnp.int32, (rows, wide), 1) - lax.broadcasted_iota(
        jnp.int32, (rows, wide), 0
    )
    band = jnp.zeros((rows, wide), F32)
    for s in range(2 * HALO + 1):
        band = band + jnp.where(offset == s, stencil_coef[s][:, None], 0.0)
    small = jnp.dot(block_inverse, band, precision=PRECISE)
    big = jnp.repeat(jnp.repeat(small, SUB, axis=0), SUB, axis=1)
    row = lax.broadcasted_iota(jnp.int32, big.shape, 0)
    col = lax.broadcasted_iota(jnp.int32, big.shape, 1)
    return jnp.where(row % SUB == col % SUB, big, 0.0)


def widened_rows(low_ref, own_ref, high_ref, c, angles):
    parts = [ref[c, :, angles, :] for ref in (low_ref, own_ref, high_ref)]
    value = jnp.concatenate(parts, axis=0)
    return value.reshape(value.shape[0] * SUB, value.shape[2])


def deposit_kernel(ids_ref, spring_ref, stress_ref, weight_ref):
    step = pl.program_id(0)
    count = ids_ref.shape[3]
    axial = stress_ref.shape[3]

    @pl.when(step == 0)
    def _():
        q = [spring_ref[c, 0] for c in range(3)]
        stretch_sq = q[0] * q[0] + q[1] * q[1] + q[2] * q[2]
        factor = 1.0 / (1.0 - stretch_sq / MAX_STRETCH)
        here = lax.broadcasted_iota(jnp.int32, (axial, count), 0) == ids_ref[1, 0]
        for c in range(3):
            weight = STRESS_SCALE * factor * q[0] * q[c]
            high = weight.astype(BF16).astype(F32)
            weight_ref[c * axial : (c + 1) * axial, :] = jnp.where(here, high, 0.0).astype(BF16)
            weight_ref[(3 + c) * axial : (4 + c) * axial, :] = jnp.where(
                here, weight - high, 0.0
            ).astype(BF16)

    radii, angles = stress_ref.shape[1], stress_ref.shape[2]
    rows = radii * angles
    plane = lax.broadcasted_iota(jnp.int32, (rows, count), 0) + step * rows
    hot = jnp.where(plane == ids_ref[0, 0], 1.0, 0.0).astype(BF16)
    both = lax.dot_general(
        hot, weight_ref[...], (((1,), (1,)), ((), ())), preferred_element_type=F32
    )
    for c in range(3):
        total = (
            both[:, c * axial : (c + 1) * axial] + both[:, (3 + c) * axial : (4 + c) * axial]
        )
        stress_ref[c] = total.reshape(radii, angles, axial)


def deposit(ids, spring, shape):
    _, radii, angles, axial = shape
    count = ids.shape[3]
    part = max(1, min(radii, 512 // angles))
    return pl.pallas_call(
        deposit_kernel,
        grid=(radii // part,),
        in_specs=[
            pl.BlockSpec(ids.shape, lambda i: (0, 0, 0, 0)),
            pl.BlockSpec(spring.shape, lambda i: (0, 0, 0, 0)),
        ],
        out_specs=pl.BlockSpec((3, part, angles, axial), lambda i: (0, i, 0, 0)),
        out_shape=jax.ShapeDtypeStruct(shape, F32),
        scratch_shapes=[pltpu.VMEM((6 * axial, count), BF16)],
        compiler_params=pltpu.CompilerParams(vmem_limit_bytes=VMEM_LIMIT),
        cost_estimate=pl.CostEstimate(
            flops=12 * radii * angles * count * axial,
            bytes_accessed=12 * radii * angles * axial,
            transcendentals=0,
        ),
        name="deposit",
    )(ids, spring)


def move_kernel(
    matrix_ref, low_ref, own_ref, high_ref, ids_ref, spring_ref, noise_ref, moved_ref, grad_ref
):
    radii, angles, axial = own_ref.shape[1:]
    group = radii * SUB
    matrix_high, matrix_low = split(matrix_ref[...])

    def grad_step(i, carry):
        at = pl.ds(pl.multiple_of(i * SUB, SUB), SUB)
        field = jnp.concatenate(
            [widened_rows(low_ref, own_ref, high_ref, c, at) for c in range(3)], axis=1
        )
        field_high, field_low = split(field)
        grad = dot3(matrix_high, matrix_low, field_high, field_low)
        turned_high, turned_low = split(grad.T)
        cols = pl.ds(pl.multiple_of(i * group, group), group)
        grad_ref[: 3 * axial, cols] = turned_high
        grad_ref[3 * axial :, cols] = turned_low
        return carry

    lax.fori_loop(0, angles // SUB, grad_step, 0)

    count = ids_ref.shape[3]
    part = min(count, 512)

    def read_step(i, carry):
        at = pl.ds(pl.multiple_of(i * part, part), part)
        plane = ids_ref[0, 0, :, at]
        radius, angle = plane // angles, plane % angles
        column = (angle // SUB) * group + radius * SUB + angle % SUB
        row_ids = lax.broadcasted_iota(jnp.int32, (radii * angles, part), 0)
        hot = jnp.where(row_ids == column, 1.0, 0.0).astype(BF16)
        picked = dot(grad_ref[...], hot)
        here = lax.broadcasted_iota(jnp.int32, (axial, part), 0) == ids_ref[1, 0, :, at]
        q = [spring_ref[c, 0, :, at] for c in range(3)]
        stretch_sq = q[0] * q[0] + q[1] * q[1] + q[2] * q[2]
        factor = 1.0 / (1.0 - stretch_sq / MAX_STRETCH)
        for c in range(3):
            value = (
                picked[c * axial : (c + 1) * axial] + picked[(3 + c) * axial : (4 + c) * axial]
            )
            shear = jnp.sum(jnp.where(here, value, 0.0), axis=0, keepdims=True)
            moved_ref[c, 0, :, at] = (
                q[c]
                + TIME_STEP * (shear * q[0] - 0.5 * factor * q[c])
                + math.sqrt(TIME_STEP) * noise_ref[c, 0, :, at]
            )
        return carry

    lax.fori_loop(0, count // part, read_step, 0)


def move(matrix, low, velocity, high, ids, spring, noise):
    radii, angles, axial = velocity.shape[1:]
    count = ids.shape[3]
    return pl.pallas_call(
        move_kernel,
        out_shape=jax.ShapeDtypeStruct(spring.shape, F32),
        scratch_shapes=[pltpu.VMEM((6 * axial, radii * angles), BF16)],
        compiler_params=pltpu.CompilerParams(vmem_limit_bytes=VMEM_LIMIT),
        cost_estimate=pl.CostEstimate(
            flops=12 * radii * angles * count * axial,
            bytes_accessed=15 * radii * angles * axial,
            transcendentals=0,
        ),
        name="move",
    )(matrix, low, velocity, high, ids, spring, noise)


def force_kernel(matrix_ref, low_ref, own_ref, high_ref, out_ref):
    radii, angles, axial = own_ref.shape[1:]
    matrix_high, matrix_low = split(matrix_ref[...])
    for i in range(angles // SUB):
        at = pl.ds(i * SUB, SUB)
        field = jnp.concatenate(
            [widened_rows(low_ref, own_ref, high_ref, c, at) for c in range(3)], axis=1
        )
        field_high, field_low = split(field)
        force = TIME_STEP * dot3(matrix_high, matrix_low, field_high, field_low)
        for c in range(3):
            out_ref[c, :, at, :] = force[:, c * axial : (c + 1) * axial].reshape(radii, SUB, axial)


def force_term(matrix, low, stress, high):
    _, radii, angles, axial = stress.shape
    part = 2 * SUB

    def block(count):
        return pl.BlockSpec((3, count, part, axial), lambda i: (0, 0, i, 0))

    return pl.pallas_call(
        force_kernel,
        grid=(angles // part,),
        in_specs=[
            pl.BlockSpec(matrix.shape, lambda i: (0, 0)),
            block(HALO),
            block(radii),
            block(HALO),
        ],
        out_specs=block(radii),
        out_shape=jax.ShapeDtypeStruct(stress.shape, F32),
        compiler_params=pltpu.CompilerParams(vmem_limit_bytes=VMEM_LIMIT),
        cost_estimate=pl.CostEstimate(
            flops=18 * matrix.shape[0] * matrix.shape[1] * angles * axial // SUB,
            bytes_accessed=27 * radii * angles * axial,
            transcendentals=0,
        ),
        name="force",
    )(matrix, low, stress, high)


def fourier_table(all_angles):
    half = all_angles // 2
    row = np.arange(all_angles)
    wave = np.where(row <= half, row, row - half)
    phase = (wave[:, None] * row[None, :]) % all_angles
    angle = phase * (2.0 * math.pi / all_angles)
    table = np.where((row <= half)[:, None], np.cos(angle), np.sin(angle)).astype(np.float32)
    high = table.astype(BF16)
    low = (table - high.astype(np.float32)).astype(BF16)
    return high, low


def solve_kernel(coef_ref, first_ref, fh_ref, fl_ref, bh_ref, bl_ref, in_ref, out_ref):
    blocks, rows, angles, axial = in_ref.shape
    all_angles = blocks * angles
    half = all_angles // 2
    row_ids = lax.broadcasted_iota(jnp.int32, (all_angles, axial), 0)
    wave = jnp.where(row_ids <= half, row_ids, row_ids - half).astype(F32)
    weight = jnp.where((row_ids == 0) | (row_ids == half), 1.0 / all_angles, 2.0 / all_angles)
    base = first_ref[0] + pl.program_id(0) * rows
    field = jnp.concatenate(
        [in_ref[:, q].reshape(all_angles, axial) for q in range(rows)], axis=1
    )
    field_high, field_low = split(field)
    spectrum = dot3(fh_ref[...], fl_ref[...], field_high, field_low)
    scale = []
    for q in range(rows):
        coef = coef_ref[lax.rem(base + q, coef_ref.shape[0])]
        scale.append(weight / (1.0 + coef * (wave * wave)))
    spectrum_high, spectrum_low = split(spectrum * jnp.concatenate(scale, axis=1))
    result = dot3(bh_ref[...], bl_ref[...], spectrum_high, spectrum_low)
    for q in range(rows):
        out_ref[:, q] = result[:, q * axial : (q + 1) * axial].reshape(blocks, angles, axial)


def solve(coef, first, field):
    blocks, rows, angles, axial = field.shape
    all_angles = blocks * angles
    high, low = fourier_table(all_angles)
    tables = [high, low, np.ascontiguousarray(high.T), np.ascontiguousarray(low.T)]
    part = 2 if rows % 2 == 0 else 1
    table_spec = pl.BlockSpec((all_angles, all_angles), lambda i: (0, 0))
    field_spec = pl.BlockSpec((blocks, part, angles, axial), lambda i: (0, i, 0, 0))
    smem = pl.BlockSpec(memory_space=pltpu.SMEM)
    return pl.pallas_call(
        solve_kernel,
        grid=(rows // part,),
        in_specs=[smem, smem, table_spec, table_spec, table_spec, table_spec, field_spec],
        out_specs=field_spec,
        out_shape=jax.ShapeDtypeStruct(field.shape, F32),
        compiler_params=pltpu.CompilerParams(vmem_limit_bytes=VMEM_LIMIT),
        cost_estimate=pl.CostEstimate(
            flops=12 * all_angles * all_angles * rows * axial,
            bytes_accessed=8 * all_angles * rows * axial,
            transcendentals=0,
        ),
        name="solve",
    )(coef, first, *[jnp.asarray(t) for t in tables], field)


def halos(block):
    count = lax.axis_size("rad")
    forward = [(i, i + 1) for i in range(count - 1)]
    backward = [(target, source) for source, target in forward]
    radii = block.shape[1]
    low = lax.ppermute(block[:, radii - HALO :], "rad", forward)
    high = lax.ppermute(block[:, :HALO], "rad", backward)
    return low, high


def per_device(velocity, dumbbells, cell_ids, brownian, stencil_coef, block_inverse, azim_coef):
    _, radii, angles, axial = velocity.shape
    az = lax.axis_size("az")
    rows = 3 * radii // az
    pieces = velocity.reshape(az, rows, angles, axial)
    gathered = lax.all_to_all(pieces, "az", 0, 0, tiled=True)
    low, high = halos(velocity)
    stress = deposit(cell_ids, dumbbells, velocity.shape)
    stress_low, stress_high = halos(stress)
    matrix = derivative_matrix(stencil_coef, block_inverse)
    moved = move(matrix, low, velocity, high, cell_ids, dumbbells, brownian)
    first = (lax.axis_index("az") * rows).astype(jnp.int32).reshape(1)
    solved = solve(azim_coef, first, gathered)
    smooth = lax.all_to_all(solved, "az", 0, 0, tiled=True).reshape(velocity.shape)
    force = force_term(matrix, stress_low, stress, stress_high)
    return smooth + force, moved


def solution(mesh):
    placed = (
        P(None, "rad", "az", None),
        P(None, "rad", "az", None),
        P(None, "rad", "az", None),
        P(None, "rad", "az", None),
        P(None, "rad"),
        P("rad", None),
        P("rad"),
    )
    return jax.shard_map(
        per_device,
        mesh=mesh,
        in_specs=placed,
        out_specs=(P(None, "rad", "az", None), P(None, "rad", "az", None)),
        check_vma=False,
    )
```

```python
import functools
import math

import jax
import jax.numpy as jnp
import numpy as np
from jax import lax
from jax.experimental import pallas as pl
from jax.experimental.pallas import tpu as pltpu
from jax.sharding import PartitionSpec as P

TIME_STEP = 0.05
MAX_STRETCH = 10.0
STRESS_SCALE = 4.0
PRECISE = lax.Precision.HIGHEST
HALO = 4
SUB = 8
VMEM_LIMIT = 56 * 1024 * 1024
F32 = jnp.float32
BF16 = jnp.bfloat16


def split(value):
    high = value.astype(BF16)
    return high, (value - high.astype(F32)).astype(BF16)


def dot(a, b):
    return jnp.dot(a, b, preferred_element_type=F32)


def dot3(stacked, b_high, b_low):
    rows = stacked.shape[0] // 2
    both = dot(stacked, b_high)
    return both[:rows] + both[rows:] + dot(stacked[:rows], b_low)

def iota(shape, dim):
    return lax.broadcasted_iota(jnp.int32, shape, dim)


def deposit_kernel(
    ids_ref, spring_ref, first_ref, last_ref, stress_ref, low_ref, high_ref, total_ref, weight_ref
):
    _, radii, angles, axial = stress_ref.shape
    count = spring_ref.shape[3]
    cells = radii * angles
    low_ref[0] = first_ref[...]
    high_ref[0] = last_ref[...]

    chunk = 64

    def clear(i, carry):
        total_ref[pl.ds(i * chunk, chunk)] = jnp.zeros((chunk, SUB, axial), F32)
        return carry

    lax.fori_loop(0, cells // chunk, clear, 0)

    q = [spring_ref[c, 0] for c in range(3)]
    stretch_sq = q[0] * q[0] + q[1] * q[1] + q[2] * q[2]
    factor = 1.0 / (1.0 - stretch_sq / MAX_STRETCH)
    for c in range(3):
        weight_ref[c : c + 1, :] = STRESS_SCALE * factor * q[0] * q[c]
    weight_ref[3:SUB, :] = jnp.zeros((SUB - 3, count), F32)

    lane = iota((SUB, axial), 1)
    batch = 4

    def block(i, carry):
        start = pl.multiple_of(i * axial, axial)
        tile = weight_ref[:, pl.ds(start, axial)]
        for g in range(axial // batch):
            cell, added = [], []
            for j in range(batch):
                at = g * batch + j
                place = ids_ref[1, 0, 0, start + at]
                turned = pltpu.roll(tile, (place + (axial - at)) & (axial - 1), axis=1)
                cell.append(ids_ref[0, 0, 0, start + at])
                added.append(jnp.where(lane == place, turned, 0.0))
            sums = []
            for j in range(batch):
                value = added[j]
                for k in range(j):
                    value = value + jnp.where(cell[k] == cell[j], added[k], 0.0)
                sums.append(value)
            old = [total_ref[cell[j]] for j in range(batch)]
            for j in range(batch):
                total_ref[cell[j]] = old[j] + sums[j]
        return carry

    lax.fori_loop(0, count // axial, block, 0)

    flat = total_ref.reshape(cells * SUB, axial)

    def unpack(r, carry):
        for i in range(angles // SUB):
            for c in range(3):
                at = (r * angles + i * SUB) * SUB + c
                stress_ref[c, r, i * SUB : (i + 1) * SUB, :] = flat[pl.ds(at, SUB, stride=SUB), :]
        return carry

    lax.fori_loop(0, radii, unpack, 0)
    low_ref[1] = stress_ref[:, :HALO]
    high_ref[1] = stress_ref[:, radii - HALO :]


def deposit(ids, spring, velocity):
    _, radii, angles, axial = velocity.shape
    count = ids.shape[3]
    edge = (2, 3, HALO, angles, axial)
    edge_block = (3, HALO, angles, axial)
    whole = pl.BlockSpec(memory_space=pltpu.VMEM)
    return pl.pallas_call(
        deposit_kernel,
        grid=(1,),
        in_specs=[
            pl.BlockSpec(memory_space=pltpu.SMEM),
            whole,
            pl.BlockSpec(edge_block, lambda i: (0, 0, 0, 0)),
            pl.BlockSpec(edge_block, lambda i: (0, radii // HALO - 1, 0, 0)),
        ],
        out_specs=[whole, whole, whole],
        out_shape=[
            jax.ShapeDtypeStruct(velocity.shape, F32),
            jax.ShapeDtypeStruct(edge, F32),
            jax.ShapeDtypeStruct(edge, F32),
        ],
        scratch_shapes=[
            pltpu.VMEM((radii * angles, SUB, axial), F32),
            pltpu.VMEM((SUB, count), F32),
        ],
        compiler_params=pltpu.CompilerParams(vmem_limit_bytes=VMEM_LIMIT),
        cost_estimate=pl.CostEstimate(
            flops=8 * radii * angles * count * axial,
            bytes_accessed=12 * radii * angles * axial,
            transcendentals=0,
        ),
        name="deposit",
    )(ids, spring, velocity, velocity)


def derivative_matrix(stencil_ref, inverse_ref):
    rows = inverse_ref.shape[1]
    wide = rows + 2 * HALO
    offset = iota((wide, rows), 0) - iota((wide, rows), 1)
    band = jnp.zeros((wide, rows), F32)
    for s in range(2 * HALO + 1):
        band = band + jnp.where(offset == s, stencil_ref[s : s + 1, :], 0.0)
    small = lax.dot_general(
        inverse_ref[...],
        band,
        (((1,), (1,)), ((), ())),
        precision=PRECISE,
        preferred_element_type=F32,
    )
    tall = jnp.where(iota((rows * SUB, rows), 0) // SUB == iota((rows * SUB, rows), 1), 1.0, 0.0)
    flat = jnp.where(iota((wide, wide * SUB), 1) // SUB == iota((wide, wide * SUB), 0), 1.0, 0.0)
    big = (rows * SUB, wide * SUB)
    same = iota(big, 0) % SUB == iota(big, 1) % SUB
    parts = []
    for part in split(small):
        spread = dot(dot(tall.astype(BF16), part).astype(BF16), flat.astype(BF16))
        parts.append(jnp.where(same, spread, 0.0).astype(BF16))
    return jnp.concatenate(parts, axis=0)


def move_kernel(
    stencil_ref,
    inverse_ref,
    low_ref,
    velocity_ref,
    stress_ref,
    high_ref,
    ids_ref,
    spring_ref,
    noise_ref,
    moved_ref,
    force_ref,
    grad_ref,
    matrix_ref,
):
    radii, angles, axial = velocity_ref.shape[1:]
    matrix_ref[...] = derivative_matrix(stencil_ref, inverse_ref)
    flat = grad_ref.reshape(radii * angles * SUB, axial)

    def derive(i, carry):
        at = pl.ds(pl.multiple_of(i * SUB, SUB), SUB)
        columns = []
        for f, own_ref in enumerate((velocity_ref, stress_ref)):
            for c in range(3):
                value = jnp.concatenate(
                    [low_ref[f, c, :, at, :], own_ref[c, :, at, :], high_ref[f, c, :, at, :]],
                    axis=0,
                )
                columns.append(value.reshape((radii + 2 * HALO) * SUB, axial))
        field_high, field_low = split(jnp.concatenate(columns, axis=1))
        result = dot3(matrix_ref[...], field_high, field_low)
        for c in range(3):
            force = TIME_STEP * result[:, (3 + c) * axial : (4 + c) * axial]
            force_ref[c, :, at, :] = force.reshape(radii, SUB, axial)
            for r in range(radii):
                place = (r * angles + i * SUB) * SUB + c
                flat[pl.ds(place, SUB, stride=SUB), :] = result[
                    r * SUB : (r + 1) * SUB, c * axial : (c + 1) * axial
                ]
        return carry

    lax.fori_loop(0, angles // SUB, derive, 0)

    lane = iota((SUB, axial), 1)

    def read(i, carry):
        start = pl.multiple_of(i * axial, axial)
        kept = [jnp.zeros((SUB, axial), F32) for _ in range(4)]
        for j in range(axial):
            tile = grad_ref[ids_ref[0, 0, 0, start + j]]
            turn = (axial + j - ids_ref[1, 0, 0, start + j]) & (axial - 1)
            kept[j % 4] = jnp.where(lane == j, pltpu.roll(tile, turn, axis=1), kept[j % 4])
        shear = (kept[0] + kept[1]) + (kept[2] + kept[3])
        at = pl.ds(start, axial)
        q = [spring_ref[c, 0, :, at] for c in range(3)]
        stretch_sq = q[0] * q[0] + q[1] * q[1] + q[2] * q[2]
        factor = 1.0 / (1.0 - stretch_sq / MAX_STRETCH)
        for c in range(3):
            moved_ref[c, 0, :, at] = (
                q[c]
                + TIME_STEP * (shear[c : c + 1] * q[0] - 0.5 * factor * q[c])
                + math.sqrt(TIME_STEP) * noise_ref[c, 0, :, at]
            )
        return carry

    lax.fori_loop(0, spring_ref.shape[3] // axial, read, 0)


def move(stencil, inverse, low, velocity, stress, high, ids, spring, noise):
    radii, angles, axial = velocity.shape[1:]
    whole = pl.BlockSpec(memory_space=pltpu.VMEM)
    return pl.pallas_call(
        move_kernel,
        in_specs=[whole] * 6 + [pl.BlockSpec(memory_space=pltpu.SMEM)] + [whole] * 2,
        out_specs=[whole, whole],
        out_shape=[
            jax.ShapeDtypeStruct(spring.shape, F32),
            jax.ShapeDtypeStruct(velocity.shape, F32),
        ],
        scratch_shapes=[
            pltpu.VMEM((radii * angles, SUB, axial), F32),
            pltpu.VMEM((2 * radii * SUB, (radii + 2 * HALO) * SUB), BF16),
        ],
        compiler_params=pltpu.CompilerParams(vmem_limit_bytes=VMEM_LIMIT),
        cost_estimate=pl.CostEstimate(
            flops=10 * radii * angles * spring.shape[3] * axial,
            bytes_accessed=40 * radii * angles * axial,
            transcendentals=0,
        ),
        name="move",
    )(stencil, inverse, low, velocity, stress, high, ids, spring, noise)


def fourier_tables(all_angles):
    half = all_angles // 2
    row = np.arange(half)
    quarter = half // 2
    waves = [
        np.where(row <= quarter, 2 * row, 2 * (row - quarter)),
        np.where(row < quarter, 2 * row + 1, 2 * (row - quarter) + 1),
    ]
    cosine = [row <= quarter, row < quarter]
    tables, squares = [], []
    for wave, even in zip(waves, cosine):
        phase = (wave[:, None] * row[None, :]) % all_angles
        angle = phase * (2.0 * math.pi / all_angles)
        table = np.where(even[:, None], np.cos(angle), np.sin(angle))
        weight = np.where((wave == 0) | (wave == half), 1.0, 2.0) / all_angles
        for value in (table, table.T * weight[None, :]):
            value = value.astype(np.float32)
            high = value.astype(BF16)
            low = (value - high.astype(np.float32)).astype(BF16)
            tables.append(np.concatenate([high, low], axis=0))
        squares.append(wave.astype(np.float32) ** 2)
    return np.stack(tables), np.stack(squares)


def solve_kernel(coef_ref, first_ref, table_ref, square_ref, in_ref, out_ref):
    blocks, rows, angles, axial = in_ref.shape
    half = blocks * angles // 2
    base = first_ref[0] + pl.program_id(0) * rows
    scale = [
        coef_ref[lax.rem(base + q, coef_ref.shape[0])] for q in range(rows)
    ]
    near = [in_ref[: blocks // 2, q].reshape(half, axial) for q in range(rows)]
    far = [in_ref[blocks // 2 :, q].reshape(half, axial) for q in range(rows)]
    results = []
    for odd in range(2):
        field = jnp.concatenate(
            [a - b if odd else a + b for a, b in zip(near, far)], axis=1
        )
        spectrum = dot3(table_ref[2 * odd], *split(field))
        square = square_ref[odd]
        damped = spectrum / (1.0 + jnp.concatenate([s * square for s in scale], axis=1))
        results.append(dot3(table_ref[2 * odd + 1], *split(damped)))
    for q in range(rows):
        even, odd = [value[:, q * axial : (q + 1) * axial] for value in results]
        out_ref[: blocks // 2, q] = (even + odd).reshape(blocks // 2, angles, axial)
        out_ref[blocks // 2 :, q] = (even - odd).reshape(blocks // 2, angles, axial)


def solve(coef, first, field):
    blocks, rows, angles, axial = field.shape
    all_angles = blocks * angles
    tables, squares = fourier_tables(all_angles)
    squares = jnp.broadcast_to(squares[:, :, None], squares.shape + (axial,))
    part = 2 if rows % 2 == 0 else 1
    field_spec = pl.BlockSpec((blocks, part, angles, axial), lambda i: (0, i, 0, 0))
    smem = pl.BlockSpec(memory_space=pltpu.SMEM)
    whole = pl.BlockSpec(memory_space=pltpu.VMEM)
    return pl.pallas_call(
        solve_kernel,
        grid=(rows // part,),
        in_specs=[smem, smem, whole, whole, field_spec],
        out_specs=field_spec,
        out_shape=jax.ShapeDtypeStruct(field.shape, F32),
        compiler_params=pltpu.CompilerParams(vmem_limit_bytes=VMEM_LIMIT),
        cost_estimate=pl.CostEstimate(
            flops=12 * all_angles * all_angles * rows * axial,
            bytes_accessed=8 * all_angles * rows * axial,
            transcendentals=0,
        ),
        name="solve",
    )(coef, first, jnp.asarray(tables), squares, field)


def add_kernel(force_ref, smooth_ref, out_ref):
    out_ref[...] = force_ref[...] + smooth_ref[...]


def add_part(force, smooth, first_row):
    rows, angles, axial = smooth.shape
    part = math.gcd(math.gcd(rows, first_row), 16)
    shifted = pl.BlockSpec((part, angles, axial), lambda i: (i + first_row // part, 0, 0))
    return pl.pallas_call(
        add_kernel,
        grid=(rows // part,),
        in_specs=[shifted, pl.BlockSpec((part, angles, axial), lambda i: (i, 0, 0))],
        out_specs=shifted,
        out_shape=jax.ShapeDtypeStruct(force.shape, F32),
        input_output_aliases={0: 0},
        compiler_params=pltpu.CompilerParams(vmem_limit_bytes=VMEM_LIMIT),
        cost_estimate=pl.CostEstimate(
            flops=rows * angles * axial,
            bytes_accessed=12 * rows * angles * axial,
            transcendentals=0,
        ),
        name="add",
    )(force, smooth)


def from_neighbours(low_edge, high_edge):
    count = lax.axis_size("rad")
    forward = [(i, i + 1) for i in range(count - 1)]
    backward = [(target, source) for source, target in forward]
    low = lax.ppermute(high_edge, "rad", forward)
    high = lax.ppermute(low_edge, "rad", backward)
    return low, high


PARTS = 2


def per_device(velocity, dumbbells, cell_ids, brownian, stencil_coef, block_inverse, azim_coef):
    _, radii, angles, axial = velocity.shape
    az = lax.axis_size("az")
    total = 3 * radii
    size = total // PARTS
    rows = size // az
    lines = velocity.reshape(total, angles, axial)
    gathered = []
    for part in range(PARTS):
        pieces = lines[part * size : (part + 1) * size].reshape(az, rows, angles, axial)
        gathered.append(lax.all_to_all(pieces, "az", 0, 0, tiled=True))
    stress, low_edge, high_edge = deposit(cell_ids, dumbbells, velocity)
    low, high = from_neighbours(low_edge, high_edge)
    moved, force = move(
        stencil_coef, block_inverse, low, velocity, stress, high, cell_ids, dumbbells, brownian
    )
    result = force.reshape(lines.shape)
    for part in range(PARTS):
        first = (lax.axis_index("az") * rows + part * size).astype(jnp.int32).reshape(1)
        solved = solve(azim_coef, first, gathered[part])
        smooth = lax.all_to_all(solved, "az", 0, 0, tiled=True)
        result = add_part(result, smooth.reshape(size, angles, axial), part * size)
    return result.reshape(velocity.shape), moved


def solution(mesh):
    placed = (
        P(None, "rad", "az", None),
        P(None, "rad", "az", None),
        P(None, "rad", "az", None),
        P(None, "rad", "az", None),
        P(None, "rad"),
        P("rad", None),
        P("rad"),
    )
    return jax.shard_map(
        per_device,
        mesh=mesh,
        in_specs=placed,
        out_specs=(P(None, "rad", "az", None), P(None, "rad", "az", None)),
        check_vma=False,
    )
```

```python
import functools
import math

import jax
import jax.numpy as jnp
import numpy as np
from jax import lax
from jax.experimental import pallas as pl
from jax.experimental.pallas import tpu as pltpu
from jax.sharding import PartitionSpec as P

TIME_STEP = 0.05
MAX_STRETCH = 10.0
STRESS_SCALE = 4.0
PRECISE = lax.Precision.HIGHEST
HALO = 4
SUB = 8
VMEM_LIMIT = 56 * 1024 * 1024
F32 = jnp.float32
BF16 = jnp.bfloat16


def split(value):
    high = value.astype(BF16)
    return high, (value - high.astype(F32)).astype(BF16)


def dot(a, b):
    return jnp.dot(a, b, preferred_element_type=F32)


def dot3(stacked, b_high, b_low):
    rows = stacked.shape[0] // 2
    both = dot(stacked, b_high)
    return both[:rows] + both[rows:] + dot(stacked[:rows], b_low)

def iota(shape, dim):
    return lax.broadcasted_iota(jnp.int32, shape, dim)


def deposit_kernel(
    ids_ref, spring_ref, first_ref, last_ref, stress_ref, low_ref, high_ref, weight_ref
):
    step = pl.program_id(0)
    count = spring_ref.shape[3]
    axial = stress_ref.shape[3]

    @pl.when(step == 0)
    def _():
        low_ref[0] = first_ref[...]
        high_ref[0] = last_ref[...]
        q = [spring_ref[c, 0] for c in range(3)]
        stretch_sq = q[0] * q[0] + q[1] * q[1] + q[2] * q[2]
        factor = 1.0 / (1.0 - stretch_sq / MAX_STRETCH)
        here = iota((axial, count), 0) == ids_ref[1, 0]
        for c in range(3):
            weight = STRESS_SCALE * factor * q[0] * q[c]
            high = weight.astype(BF16).astype(F32)
            weight_ref[c * axial : (c + 1) * axial, :] = jnp.where(here, high, 0.0).astype(BF16)
            weight_ref[(3 + c) * axial : (4 + c) * axial, :] = jnp.where(
                here, weight - high, 0.0
            ).astype(BF16)

    radii, angles = stress_ref.shape[1], stress_ref.shape[2]
    rows = radii * angles
    hot = jnp.where(iota((rows, count), 0) + step * rows == ids_ref[0, 0], 1.0, 0.0).astype(BF16)
    both = lax.dot_general(
        hot, weight_ref[...], (((1,), (1,)), ((), ())), preferred_element_type=F32
    )
    for c in range(3):
        total = (
            both[:, c * axial : (c + 1) * axial] + both[:, (3 + c) * axial : (4 + c) * axial]
        )
        stress_ref[c] = total.reshape(radii, angles, axial)

    @pl.when(step == 0)
    def _():
        low_ref[1] = stress_ref[:, :HALO]

    @pl.when(step == pl.num_programs(0) - 1)
    def _():
        high_ref[1] = stress_ref[:, radii - HALO :]


def deposit(ids, spring, velocity):
    _, radii, angles, axial = velocity.shape
    count = ids.shape[3]
    part = max(HALO, min(radii, 512 // angles))
    edge = (2, 3, HALO, angles, axial)
    edge_block = (3, HALO, angles, axial)
    whole = pl.BlockSpec(memory_space=pltpu.VMEM)
    return pl.pallas_call(
        deposit_kernel,
        grid=(radii // part,),
        in_specs=[
            whole,
            whole,
            pl.BlockSpec(edge_block, lambda i: (0, 0, 0, 0)),
            pl.BlockSpec(edge_block, lambda i: (0, radii // HALO - 1, 0, 0)),
        ],
        out_specs=[
            pl.BlockSpec((3, part, angles, axial), lambda i: (0, i, 0, 0)),
            pl.BlockSpec(edge, lambda i: (0, 0, 0, 0, 0)),
            pl.BlockSpec(edge, lambda i: (0, 0, 0, 0, 0)),
        ],
        out_shape=[
            jax.ShapeDtypeStruct(velocity.shape, F32),
            jax.ShapeDtypeStruct(edge, F32),
            jax.ShapeDtypeStruct(edge, F32),
        ],
        scratch_shapes=[pltpu.VMEM((6 * axial, count), BF16)],
        compiler_params=pltpu.CompilerParams(vmem_limit_bytes=VMEM_LIMIT),
        cost_estimate=pl.CostEstimate(
            flops=12 * radii * angles * count * axial,
            bytes_accessed=12 * radii * angles * axial,
            transcendentals=0,
        ),
        name="deposit",
    )(ids, spring, velocity, velocity)


def derivative_matrix(stencil_ref, inverse_ref):
    rows = inverse_ref.shape[1]
    wide = rows + 2 * HALO
    offset = iota((wide, rows), 0) - iota((wide, rows), 1)
    band = jnp.zeros((wide, rows), F32)
    for s in range(2 * HALO + 1):
        band = band + jnp.where(offset == s, stencil_ref[s : s + 1, :], 0.0)
    small = lax.dot_general(
        inverse_ref[...],
        band,
        (((1,), (1,)), ((), ())),
        precision=PRECISE,
        preferred_element_type=F32,
    )
    tall = jnp.where(iota((rows * SUB, rows), 0) // SUB == iota((rows * SUB, rows), 1), 1.0, 0.0)
    flat = jnp.where(iota((wide, wide * SUB), 1) // SUB == iota((wide, wide * SUB), 0), 1.0, 0.0)
    big = (rows * SUB, wide * SUB)
    same = iota(big, 0) % SUB == iota(big, 1) % SUB
    parts = []
    for part in split(small):
        spread = dot(dot(tall.astype(BF16), part).astype(BF16), flat.astype(BF16))
        parts.append(jnp.where(same, spread, 0.0).astype(BF16))
    return jnp.concatenate(parts, axis=0)


def move_kernel(
    stencil_ref,
    inverse_ref,
    low_ref,
    velocity_ref,
    stress_ref,
    high_ref,
    ids_ref,
    spring_ref,
    noise_ref,
    moved_ref,
    force_ref,
    grad_ref,
    matrix_ref,
):
    radii, angles, axial = velocity_ref.shape[1:]
    matrix_ref[...] = derivative_matrix(stencil_ref, inverse_ref)
    group = radii * SUB

    def derive(i, carry):
        at = pl.ds(pl.multiple_of(i * SUB, SUB), SUB)
        columns = []
        for f, own_ref in enumerate((velocity_ref, stress_ref)):
            for c in range(3):
                value = jnp.concatenate(
                    [low_ref[f, c, :, at, :], own_ref[c, :, at, :], high_ref[f, c, :, at, :]],
                    axis=0,
                )
                columns.append(value.reshape((radii + 2 * HALO) * SUB, axial))
        field_high, field_low = split(jnp.concatenate(columns, axis=1))
        result = dot3(matrix_ref[...], field_high, field_low)
        for c in range(3):
            force = TIME_STEP * result[:, (3 + c) * axial : (4 + c) * axial]
            force_ref[c, :, at, :] = force.reshape(radii, SUB, axial)
        turned_high, turned_low = split(result[:, : 3 * axial].T)
        cols = pl.ds(pl.multiple_of(i * group, group), group)
        grad_ref[: 3 * axial, cols] = turned_high
        grad_ref[3 * axial :, cols] = turned_low
        return carry

    lax.fori_loop(0, angles // SUB, derive, 0)

    count = spring_ref.shape[3]
    part = min(count, 512)

    def read(i, carry):
        at = pl.ds(pl.multiple_of(i * part, part), part)
        plane = ids_ref[0, 0, :, at]
        radius, angle = plane // angles, plane % angles
        column = (angle // SUB) * group + radius * SUB + angle % SUB
        hot = jnp.where(iota((radii * angles, part), 0) == column, 1.0, 0.0).astype(BF16)
        picked = dot(grad_ref[...], hot)
        here = iota((axial, part), 0) == ids_ref[1, 0, :, at]
        q = [spring_ref[c, 0, :, at] for c in range(3)]
        stretch_sq = q[0] * q[0] + q[1] * q[1] + q[2] * q[2]
        factor = 1.0 / (1.0 - stretch_sq / MAX_STRETCH)
        for c in range(3):
            value = (
                picked[c * axial : (c + 1) * axial] + picked[(3 + c) * axial : (4 + c) * axial]
            )
            shear = jnp.sum(jnp.where(here, value, 0.0), axis=0, keepdims=True)
            moved_ref[c, 0, :, at] = (
                q[c]
                + TIME_STEP * (shear * q[0] - 0.5 * factor * q[c])
                + math.sqrt(TIME_STEP) * noise_ref[c, 0, :, at]
            )
        return carry

    lax.fori_loop(0, count // part, read, 0)


def move(stencil, inverse, low, velocity, stress, high, ids, spring, noise):
    radii, angles, axial = velocity.shape[1:]
    whole = pl.BlockSpec(memory_space=pltpu.VMEM)
    return pl.pallas_call(
        move_kernel,
        in_specs=[whole] * 9,
        out_specs=[whole, whole],
        out_shape=[
            jax.ShapeDtypeStruct(spring.shape, F32),
            jax.ShapeDtypeStruct(velocity.shape, F32),
        ],
        scratch_shapes=[
            pltpu.VMEM((6 * axial, radii * angles), BF16),
            pltpu.VMEM((2 * radii * SUB, (radii + 2 * HALO) * SUB), BF16),
        ],
        compiler_params=pltpu.CompilerParams(vmem_limit_bytes=VMEM_LIMIT),
        cost_estimate=pl.CostEstimate(
            flops=14 * radii * angles * spring.shape[3] * axial,
            bytes_accessed=40 * radii * angles * axial,
            transcendentals=0,
        ),
        name="move",
    )(stencil, inverse, low, velocity, stress, high, ids, spring, noise)


def fourier_tables(all_angles):
    half = all_angles // 2
    row = np.arange(half)
    quarter = half // 2
    waves = [
        np.where(row <= quarter, 2 * row, 2 * (row - quarter)),
        np.where(row < quarter, 2 * row + 1, 2 * (row - quarter) + 1),
    ]
    cosine = [row <= quarter, row < quarter]
    tables = []
    for wave, even in zip(waves, cosine):
        phase = (wave[:, None] * row[None, :]) % all_angles
        angle = phase * (2.0 * math.pi / all_angles)
        table = np.where(even[:, None], np.cos(angle), np.sin(angle))
        weight = np.where((wave == 0) | (wave == half), 1.0, 2.0) / all_angles
        for value in (table, table.T * weight[None, :]):
            tables.append(value.astype(np.float32))
    return np.stack(tables)


def solve_kernel(coef_ref, first_ref, float_ref, in_ref, out_ref, table_ref):
    blocks, rows, angles, axial = in_ref.shape
    half = blocks * angles // 2
    quarter = half // 2

    @pl.when(pl.program_id(0) == 0)
    def _():
        for i in range(4):
            high, low = split(float_ref[i])
            table_ref[i, :half] = high
            table_ref[i, half:] = low

    row = iota((half, axial), 0)
    waves = [
        jnp.where(row <= quarter, 2 * row, 2 * (row - quarter)),
        jnp.where(row < quarter, 2 * row + 1, 2 * (row - quarter) + 1),
    ]
    base = first_ref[0] + pl.program_id(0) * rows
    scale = [coef_ref[lax.rem(base + q, coef_ref.shape[0])] for q in range(rows)]
    near = [in_ref[: blocks // 2, q].reshape(half, axial) for q in range(rows)]
    far = [in_ref[blocks // 2 :, q].reshape(half, axial) for q in range(rows)]
    results = []
    for odd in range(2):
        field = jnp.concatenate(
            [a - b if odd else a + b for a, b in zip(near, far)], axis=1
        )
        spectrum = dot3(table_ref[2 * odd], *split(field))
        square = (waves[odd] * waves[odd]).astype(F32)
        damped = spectrum / (1.0 + jnp.concatenate([s * square for s in scale], axis=1))
        results.append(dot3(table_ref[2 * odd + 1], *split(damped)))
    for q in range(rows):
        even, odd = [value[:, q * axial : (q + 1) * axial] for value in results]
        out_ref[: blocks // 2, q] = (even + odd).reshape(blocks // 2, angles, axial)
        out_ref[blocks // 2 :, q] = (even - odd).reshape(blocks // 2, angles, axial)


def solve(coef, first, field):
    blocks, rows, angles, axial = field.shape
    all_angles = blocks * angles
    tables = fourier_tables(all_angles)
    half = all_angles // 2
    part = 2 if rows % 2 == 0 else 1
    field_spec = pl.BlockSpec((blocks, part, angles, axial), lambda i: (0, i, 0, 0))
    smem = pl.BlockSpec(memory_space=pltpu.SMEM)
    whole = pl.BlockSpec(memory_space=pltpu.VMEM)
    return pl.pallas_call(
        solve_kernel,
        grid=(rows // part,),
        in_specs=[smem, smem, whole, field_spec],
        out_specs=field_spec,
        out_shape=jax.ShapeDtypeStruct(field.shape, F32),
        scratch_shapes=[pltpu.VMEM((4, 2 * half, half), BF16)],
        compiler_params=pltpu.CompilerParams(vmem_limit_bytes=VMEM_LIMIT),
        cost_estimate=pl.CostEstimate(
            flops=12 * all_angles * all_angles * rows * axial,
            bytes_accessed=8 * all_angles * rows * axial,
            transcendentals=0,
        ),
        name="solve",
    )(coef, first, jnp.asarray(tables), field)


def add_kernel(force_ref, smooth_ref, out_ref):
    out_ref[...] = force_ref[...] + smooth_ref[...]


def add_part(force, smooth, first_row):
    rows, angles, axial = smooth.shape
    part = math.gcd(math.gcd(rows, first_row), 8)
    shifted = pl.BlockSpec((part, angles, axial), lambda i: (i + first_row // part, 0, 0))
    return pl.pallas_call(
        add_kernel,
        grid=(rows // part,),
        in_specs=[shifted, pl.BlockSpec((part, angles, axial), lambda i: (i, 0, 0))],
        out_specs=shifted,
        out_shape=jax.ShapeDtypeStruct(force.shape, F32),
        input_output_aliases={0: 0},
        compiler_params=pltpu.CompilerParams(vmem_limit_bytes=VMEM_LIMIT),
        cost_estimate=pl.CostEstimate(
            flops=rows * angles * axial,
            bytes_accessed=12 * rows * angles * axial,
            transcendentals=0,
        ),
        name="add",
    )(force, smooth)


def from_neighbours(low_edge, high_edge):
    count = lax.axis_size("rad")
    forward = [(i, i + 1) for i in range(count - 1)]
    backward = [(target, source) for source, target in forward]
    low = lax.ppermute(high_edge, "rad", forward)
    high = lax.ppermute(low_edge, "rad", backward)
    return low, high


PARTS = 1


def per_device(velocity, dumbbells, cell_ids, brownian, stencil_coef, block_inverse, azim_coef):
    _, radii, angles, axial = velocity.shape
    az = lax.axis_size("az")
    total = 3 * radii
    size = total // PARTS
    rows = size // az
    lines = velocity.reshape(total, angles, axial)
    gathered = []
    for part in range(PARTS):
        pieces = lines[part * size : (part + 1) * size].reshape(az, rows, angles, axial)
        gathered.append(lax.all_to_all(pieces, "az", 0, 0, tiled=True))
    stress, low_edge, high_edge = deposit(cell_ids, dumbbells, velocity)
    low, high = from_neighbours(low_edge, high_edge)
    moved, force = move(
        stencil_coef, block_inverse, low, velocity, stress, high, cell_ids, dumbbells, brownian
    )
    result = force.reshape(lines.shape)
    for part in range(PARTS):
        first = (lax.axis_index("az") * rows + part * size).astype(jnp.int32).reshape(1)
        solved = solve(azim_coef, first, gathered[part])
        smooth = lax.all_to_all(solved, "az", 0, 0, tiled=True)
        result = add_part(result, smooth.reshape(size, angles, axial), part * size)
    return result.reshape(velocity.shape), moved


def solution(mesh):
    placed = (
        P(None, "rad", "az", None),
        P(None, "rad", "az", None),
        P(None, "rad", "az", None),
        P(None, "rad", "az", None),
        P(None, "rad"),
        P("rad", None),
        P("rad"),
    )
    return jax.shard_map(
        per_device,
        mesh=mesh,
        in_specs=placed,
        out_specs=(P(None, "rad", "az", None), P(None, "rad", "az", None)),
        check_vma=False,
    )
```

```python
import functools
import math

import jax
import jax.numpy as jnp
import numpy as np
from jax import lax
from jax.experimental import pallas as pl
from jax.experimental.pallas import tpu as pltpu
from jax.sharding import PartitionSpec as P

TIME_STEP = 0.05
MAX_STRETCH = 10.0
STRESS_SCALE = 4.0
PRECISE = lax.Precision.HIGHEST
HALO = 4
SUB = 8
MIB = 1024 * 1024
F32 = jnp.float32
BF16 = jnp.bfloat16


def split(value):
    high = value.astype(BF16)
    return high, (value - high.astype(F32)).astype(BF16)


def dot(a, b):
    return jnp.dot(a, b, preferred_element_type=F32)


def dot3(stacked, b_high, b_low):
    rows = stacked.shape[0] // 2
    both = dot(stacked, b_high)
    return both[:rows] + both[rows:] + dot(stacked[:rows], b_low)

def iota(shape, dim):
    return lax.broadcasted_iota(jnp.int32, shape, dim)


def deposit_kernel(
    ids_ref, spring_ref, first_ref, last_ref, stress_ref, low_ref, high_ref, weight_ref
):
    step = pl.program_id(0)
    count = spring_ref.shape[3]
    axial = stress_ref.shape[3]

    @pl.when(step == 0)
    def _():
        low_ref[0] = first_ref[...]
        high_ref[0] = last_ref[...]
        q = [spring_ref[c, 0] for c in range(3)]
        stretch_sq = q[0] * q[0] + q[1] * q[1] + q[2] * q[2]
        factor = 1.0 / (1.0 - stretch_sq / MAX_STRETCH)
        here = iota((axial, count), 0) == ids_ref[1, 0]
        for c in range(3):
            weight = STRESS_SCALE * factor * q[0] * q[c]
            high = weight.astype(BF16).astype(F32)
            weight_ref[c * axial : (c + 1) * axial, :] = jnp.where(here, high, 0.0).astype(BF16)
            weight_ref[(3 + c) * axial : (4 + c) * axial, :] = jnp.where(
                here, weight - high, 0.0
            ).astype(BF16)

    radii, angles = stress_ref.shape[1], stress_ref.shape[2]
    rows = radii * angles
    hot = jnp.where(iota((rows, count), 0) + step * rows == ids_ref[0, 0], 1.0, 0.0).astype(BF16)
    both = lax.dot_general(
        hot, weight_ref[...], (((1,), (1,)), ((), ())), preferred_element_type=F32
    )
    for c in range(3):
        total = (
            both[:, c * axial : (c + 1) * axial] + both[:, (3 + c) * axial : (4 + c) * axial]
        )
        stress_ref[c] = total.reshape(radii, angles, axial)

    @pl.when(step == 0)
    def _():
        low_ref[1] = stress_ref[:, :HALO]

    @pl.when(step == pl.num_programs(0) - 1)
    def _():
        high_ref[1] = stress_ref[:, radii - HALO :]


def deposit(ids, spring, velocity):
    _, radii, angles, axial = velocity.shape
    count = ids.shape[3]
    part = max(HALO, min(radii, 512 // angles))
    edge = (2, 3, HALO, angles, axial)
    edge_block = (3, HALO, angles, axial)
    whole = pl.BlockSpec(memory_space=pltpu.VMEM)
    return pl.pallas_call(
        deposit_kernel,
        grid=(radii // part,),
        in_specs=[
            whole,
            whole,
            pl.BlockSpec(edge_block, lambda i: (0, 0, 0, 0)),
            pl.BlockSpec(edge_block, lambda i: (0, radii // HALO - 1, 0, 0)),
        ],
        out_specs=[
            pl.BlockSpec((3, part, angles, axial), lambda i: (0, i, 0, 0)),
            pl.BlockSpec(edge, lambda i: (0, 0, 0, 0, 0)),
            pl.BlockSpec(edge, lambda i: (0, 0, 0, 0, 0)),
        ],
        out_shape=[
            jax.ShapeDtypeStruct(velocity.shape, F32),
            jax.ShapeDtypeStruct(edge, F32),
            jax.ShapeDtypeStruct(edge, F32),
        ],
        scratch_shapes=[pltpu.VMEM((6 * axial, count), BF16)],
        compiler_params=pltpu.CompilerParams(vmem_limit_bytes=24 * MIB),
        cost_estimate=pl.CostEstimate(
            flops=12 * radii * angles * count * axial,
            bytes_accessed=12 * radii * angles * axial,
            transcendentals=0,
        ),
        name="deposit",
    )(ids, spring, velocity, velocity)


def derivative_matrix(stencil_ref, inverse_ref):
    rows = inverse_ref.shape[1]
    wide = rows + 2 * HALO
    offset = iota((wide, rows), 0) - iota((wide, rows), 1)
    band = jnp.zeros((wide, rows), F32)
    for s in range(2 * HALO + 1):
        band = band + jnp.where(offset == s, stencil_ref[s : s + 1, :], 0.0)
    small = lax.dot_general(
        inverse_ref[...],
        band,
        (((1,), (1,)), ((), ())),
        precision=PRECISE,
        preferred_element_type=F32,
    )
    tall = jnp.where(iota((rows * SUB, rows), 0) // SUB == iota((rows * SUB, rows), 1), 1.0, 0.0)
    flat = jnp.where(iota((wide, wide * SUB), 1) // SUB == iota((wide, wide * SUB), 0), 1.0, 0.0)
    big = (rows * SUB, wide * SUB)
    same = iota(big, 0) % SUB == iota(big, 1) % SUB
    parts = []
    for part in split(small):
        spread = dot(dot(tall.astype(BF16), part).astype(BF16), flat.astype(BF16))
        parts.append(jnp.where(same, spread, 0.0).astype(BF16))
    return jnp.concatenate(parts, axis=0)


def move_kernel(
    stencil_ref,
    inverse_ref,
    low_ref,
    velocity_ref,
    stress_ref,
    high_ref,
    ids_ref,
    spring_ref,
    noise_ref,
    moved_ref,
    force_ref,
    grad_ref,
    matrix_ref,
):
    radii, angles, axial = velocity_ref.shape[1:]
    matrix_ref[...] = derivative_matrix(stencil_ref, inverse_ref)
    group = radii * SUB

    def derive(i, carry):
        at = pl.ds(pl.multiple_of(i * SUB, SUB), SUB)
        columns = []
        for f, own_ref in enumerate((velocity_ref, stress_ref)):
            for c in range(3):
                value = jnp.concatenate(
                    [low_ref[f, c, :, at, :], own_ref[c, :, at, :], high_ref[f, c, :, at, :]],
                    axis=0,
                )
                columns.append(value.reshape((radii + 2 * HALO) * SUB, axial))
        field_high, field_low = split(jnp.concatenate(columns, axis=1))
        result = dot3(matrix_ref[...], field_high, field_low)
        for c in range(3):
            force = TIME_STEP * result[:, (3 + c) * axial : (4 + c) * axial]
            force_ref[c, :, at, :] = force.reshape(radii, SUB, axial)
        turned_high, turned_low = split(result[:, : 3 * axial].T)
        cols = pl.ds(pl.multiple_of(i * group, group), group)
        grad_ref[: 3 * axial, cols] = turned_high
        grad_ref[3 * axial :, cols] = turned_low
        return carry

    lax.fori_loop(0, angles // SUB, derive, 0)

    count = spring_ref.shape[3]
    part = min(count, 512)

    def read(i, carry):
        at = pl.ds(pl.multiple_of(i * part, part), part)
        plane = ids_ref[0, 0, :, at]
        radius, angle = plane // angles, plane % angles
        column = (angle // SUB) * group + radius * SUB + angle % SUB
        hot = jnp.where(iota((radii * angles, part), 0) == column, 1.0, 0.0).astype(BF16)
        picked = dot(grad_ref[...], hot)
        here = iota((axial, part), 0) == ids_ref[1, 0, :, at]
        q = [spring_ref[c, 0, :, at] for c in range(3)]
        stretch_sq = q[0] * q[0] + q[1] * q[1] + q[2] * q[2]
        factor = 1.0 / (1.0 - stretch_sq / MAX_STRETCH)
        for c in range(3):
            value = (
                picked[c * axial : (c + 1) * axial] + picked[(3 + c) * axial : (4 + c) * axial]
            )
            shear = jnp.sum(jnp.where(here, value, 0.0), axis=0, keepdims=True)
            moved_ref[c, 0, :, at] = (
                q[c]
                + TIME_STEP * (shear * q[0] - 0.5 * factor * q[c])
                + math.sqrt(TIME_STEP) * noise_ref[c, 0, :, at]
            )
        return carry

    lax.fori_loop(0, count // part, read, 0)


def move(stencil, inverse, low, velocity, stress, high, ids, spring, noise):
    radii, angles, axial = velocity.shape[1:]
    whole = pl.BlockSpec(memory_space=pltpu.VMEM)
    return pl.pallas_call(
        move_kernel,
        in_specs=[whole] * 9,
        out_specs=[whole, whole],
        out_shape=[
            jax.ShapeDtypeStruct(spring.shape, F32),
            jax.ShapeDtypeStruct(velocity.shape, F32),
        ],
        scratch_shapes=[
            pltpu.VMEM((6 * axial, radii * angles), BF16),
            pltpu.VMEM((2 * radii * SUB, (radii + 2 * HALO) * SUB), BF16),
        ],
        compiler_params=pltpu.CompilerParams(vmem_limit_bytes=28 * MIB),
        cost_estimate=pl.CostEstimate(
            flops=14 * radii * angles * spring.shape[3] * axial,
            bytes_accessed=40 * radii * angles * axial,
            transcendentals=0,
        ),
        name="move",
    )(stencil, inverse, low, velocity, stress, high, ids, spring, noise)


def fourier_tables(all_angles):
    half = all_angles // 2
    row = np.arange(half)
    quarter = half // 2
    waves = [
        np.where(row <= quarter, 2 * row, 2 * (row - quarter)),
        np.where(row < quarter, 2 * row + 1, 2 * (row - quarter) + 1),
    ]
    cosine = [row <= quarter, row < quarter]
    tables = []
    for wave, even in zip(waves, cosine):
        phase = (wave[:, None] * row[None, :]) % all_angles
        angle = phase * (2.0 * math.pi / all_angles)
        table = np.where(even[:, None], np.cos(angle), np.sin(angle))
        weight = np.where((wave == 0) | (wave == half), 1.0, 2.0) / all_angles
        for value in (table, table.T * weight[None, :]):
            tables.append(value.astype(np.float32))
    return np.stack(tables)


def solve_kernel(coef_ref, first_ref, float_ref, after_ref, in_ref, out_ref, table_ref):
    blocks, rows, angles, axial = in_ref.shape
    half = blocks * angles // 2
    quarter = half // 2

    @pl.when(pl.program_id(0) == 0)
    def _():
        for i in range(4):
            high, low = split(float_ref[i])
            table_ref[i, :half] = high
            table_ref[i, half:] = low

    row = iota((half, axial), 0)
    waves = [
        jnp.where(row <= quarter, 2 * row, 2 * (row - quarter)),
        jnp.where(row < quarter, 2 * row + 1, 2 * (row - quarter) + 1),
    ]
    base = first_ref[0] + pl.program_id(0) * rows
    scale = [coef_ref[lax.rem(base + q, coef_ref.shape[0])] for q in range(rows)]
    near = [in_ref[: blocks // 2, q].reshape(half, axial) for q in range(rows)]
    far = [in_ref[blocks // 2 :, q].reshape(half, axial) for q in range(rows)]
    results = []
    for odd in range(2):
        field = jnp.concatenate(
            [a - b if odd else a + b for a, b in zip(near, far)], axis=1
        )
        spectrum = dot3(table_ref[2 * odd], *split(field))
        square = (waves[odd] * waves[odd]).astype(F32)
        damped = spectrum / (1.0 + jnp.concatenate([s * square for s in scale], axis=1))
        results.append(dot3(table_ref[2 * odd + 1], *split(damped)))
    for q in range(rows):
        even, odd = [value[:, q * axial : (q + 1) * axial] for value in results]
        out_ref[: blocks // 2, q] = (even + odd).reshape(blocks // 2, angles, axial)
        out_ref[blocks // 2 :, q] = (even - odd).reshape(blocks // 2, angles, axial)


def solve(coef, first, field, after):
    blocks, rows, angles, axial = field.shape
    all_angles = blocks * angles
    tables = fourier_tables(all_angles)
    half = all_angles // 2
    part = 2 if rows % 2 == 0 else 1
    field_spec = pl.BlockSpec((blocks, part, angles, axial), lambda i: (0, i, 0, 0))
    smem = pl.BlockSpec(memory_space=pltpu.SMEM)
    whole = pl.BlockSpec(memory_space=pltpu.VMEM)
    return pl.pallas_call(
        solve_kernel,
        grid=(rows // part,),
        in_specs=[smem, smem, whole, pl.BlockSpec(memory_space=pl.ANY), field_spec],
        out_specs=field_spec,
        out_shape=jax.ShapeDtypeStruct(field.shape, F32),
        scratch_shapes=[pltpu.VMEM((4, 2 * half, half), BF16)],
        compiler_params=pltpu.CompilerParams(vmem_limit_bytes=14 * MIB),
        cost_estimate=pl.CostEstimate(
            flops=12 * all_angles * all_angles * rows * axial,
            bytes_accessed=8 * all_angles * rows * axial,
            transcendentals=0,
        ),
        name="solve",
    )(coef, first, jnp.asarray(tables), after, field)


def from_neighbours(low_edge, high_edge):
    count = lax.axis_size("rad")
    forward = [(i, i + 1) for i in range(count - 1)]
    backward = [(target, source) for source, target in forward]
    low = lax.ppermute(high_edge, "rad", forward)
    high = lax.ppermute(low_edge, "rad", backward)
    return low, high


def per_device(velocity, dumbbells, cell_ids, brownian, stencil_coef, block_inverse, azim_coef):
    _, radii, angles, axial = velocity.shape
    az = lax.axis_size("az")
    rows = 3 * radii // az
    pieces = velocity.reshape(az, rows, angles, axial)
    gathered = lax.all_to_all(pieces, "az", 0, 0, tiled=True)
    stress, low_edge, high_edge = deposit(cell_ids, dumbbells, velocity)
    low, high = from_neighbours(low_edge, high_edge)
    first = (lax.axis_index("az") * rows).astype(jnp.int32).reshape(1)
    solved = solve(azim_coef, first, gathered, low_edge)
    smooth = lax.all_to_all(solved, "az", 0, 0, tiled=True).reshape(velocity.shape)
    moved, force = move(
        stencil_coef, block_inverse, low, velocity, stress, high, cell_ids, dumbbells, brownian
    )
    return smooth + force, moved


def solution(mesh):
    placed = (
        P(None, "rad", "az", None),
        P(None, "rad", "az", None),
        P(None, "rad", "az", None),
        P(None, "rad", "az", None),
        P(None, "rad"),
        P("rad", None),
        P("rad"),
    )
    return jax.shard_map(
        per_device,
        mesh=mesh,
        in_specs=placed,
        out_specs=(P(None, "rad", "az", None), P(None, "rad", "az", None)),
        check_vma=False,
    )
```

```python
import functools
import math

import jax
import jax.numpy as jnp
import numpy as np
from jax import lax
from jax.experimental import pallas as pl
from jax.experimental.pallas import tpu as pltpu
from jax.sharding import PartitionSpec as P

TIME_STEP = 0.05
MAX_STRETCH = 10.0
STRESS_SCALE = 4.0
PRECISE = lax.Precision.HIGHEST
HALO = 4
SUB = 8
MIB = 1024 * 1024
F32 = jnp.float32
BF16 = jnp.bfloat16


def split(value):
    high = value.astype(BF16)
    return high, (value - high.astype(F32)).astype(BF16)


def dot(a, b):
    return jnp.dot(a, b, preferred_element_type=F32)


def dot3(stacked, b_high, b_low):
    rows = stacked.shape[0] // 2
    both = dot(stacked, b_high)
    return both[:rows] + both[rows:] + dot(stacked[:rows], b_low)

def in_hbm(value):
    return pltpu.with_memory_space_constraint(value, pltpu.HBM)


def in_vmem(value):
    return pltpu.with_memory_space_constraint(value, pltpu.VMEM)


def iota(shape, dim):
    return lax.broadcasted_iota(jnp.int32, shape, dim)


def deposit_kernel(
    ids_ref, spring_ref, first_ref, last_ref, stress_ref, low_ref, high_ref, weight_ref
):
    step = pl.program_id(0)
    count = spring_ref.shape[3]
    axial = stress_ref.shape[3]

    @pl.when(step == 0)
    def _():
        low_ref[0] = first_ref[...]
        high_ref[0] = last_ref[...]
        q = [spring_ref[c, 0] for c in range(3)]
        stretch_sq = q[0] * q[0] + q[1] * q[1] + q[2] * q[2]
        factor = 1.0 / (1.0 - stretch_sq / MAX_STRETCH)
        here = iota((axial, count), 0) == ids_ref[1, 0]
        for c in range(3):
            weight = STRESS_SCALE * factor * q[0] * q[c]
            high = weight.astype(BF16).astype(F32)
            weight_ref[c * axial : (c + 1) * axial, :] = jnp.where(here, high, 0.0).astype(BF16)
            weight_ref[(3 + c) * axial : (4 + c) * axial, :] = jnp.where(
                here, weight - high, 0.0
            ).astype(BF16)

    radii, angles = stress_ref.shape[1], stress_ref.shape[2]
    rows = radii * angles
    hot = jnp.where(iota((rows, count), 0) + step * rows == ids_ref[0, 0], 1.0, 0.0).astype(BF16)
    both = lax.dot_general(
        hot, weight_ref[...], (((1,), (1,)), ((), ())), preferred_element_type=F32
    )
    for c in range(3):
        total = (
            both[:, c * axial : (c + 1) * axial] + both[:, (3 + c) * axial : (4 + c) * axial]
        )
        stress_ref[c] = total.reshape(radii, angles, axial)

    @pl.when(step == 0)
    def _():
        low_ref[1] = stress_ref[:, :HALO]

    @pl.when(step == pl.num_programs(0) - 1)
    def _():
        high_ref[1] = stress_ref[:, radii - HALO :]


def deposit(ids, spring, velocity):
    _, radii, angles, axial = velocity.shape
    count = ids.shape[3]
    part = max(HALO, min(radii, 512 // angles))
    edge = (2, 3, HALO, angles, axial)
    edge_block = (3, HALO, angles, axial)
    whole = pl.BlockSpec(memory_space=pltpu.VMEM)
    return pl.pallas_call(
        deposit_kernel,
        grid=(radii // part,),
        in_specs=[
            whole,
            whole,
            pl.BlockSpec(edge_block, lambda i: (0, 0, 0, 0)),
            pl.BlockSpec(edge_block, lambda i: (0, radii // HALO - 1, 0, 0)),
        ],
        out_specs=[
            pl.BlockSpec((3, part, angles, axial), lambda i: (0, i, 0, 0)),
            pl.BlockSpec(edge, lambda i: (0, 0, 0, 0, 0)),
            pl.BlockSpec(edge, lambda i: (0, 0, 0, 0, 0)),
        ],
        out_shape=[
            pltpu.HBM(velocity.shape, F32),
            pltpu.HBM(edge, F32),
            pltpu.HBM(edge, F32),
        ],
        scratch_shapes=[pltpu.VMEM((6 * axial, count), BF16)],
        compiler_params=pltpu.CompilerParams(vmem_limit_bytes=24 * MIB),
        cost_estimate=pl.CostEstimate(
            flops=12 * radii * angles * count * axial,
            bytes_accessed=12 * radii * angles * axial,
            transcendentals=0,
        ),
        name="deposit",
    )(ids, spring, in_hbm(velocity), in_hbm(velocity))


def derivative_matrix(stencil_ref, inverse_ref):
    rows = inverse_ref.shape[1]
    wide = rows + 2 * HALO
    offset = iota((wide, rows), 0) - iota((wide, rows), 1)
    band = jnp.zeros((wide, rows), F32)
    for s in range(2 * HALO + 1):
        band = band + jnp.where(offset == s, stencil_ref[s : s + 1, :], 0.0)
    small = lax.dot_general(
        inverse_ref[...],
        band,
        (((1,), (1,)), ((), ())),
        precision=PRECISE,
        preferred_element_type=F32,
    )
    tall = jnp.where(iota((rows * SUB, rows), 0) // SUB == iota((rows * SUB, rows), 1), 1.0, 0.0)
    flat = jnp.where(iota((wide, wide * SUB), 1) // SUB == iota((wide, wide * SUB), 0), 1.0, 0.0)
    big = (rows * SUB, wide * SUB)
    same = iota(big, 0) % SUB == iota(big, 1) % SUB
    parts = []
    for part in split(small):
        spread = dot(dot(tall.astype(BF16), part).astype(BF16), flat.astype(BF16))
        parts.append(jnp.where(same, spread, 0.0).astype(BF16))
    return jnp.concatenate(parts, axis=0)


def move_kernel(
    stencil_ref,
    inverse_ref,
    low_ref,
    velocity_ref,
    stress_ref,
    high_ref,
    ids_ref,
    spring_ref,
    noise_ref,
    moved_ref,
    force_ref,
    grad_ref,
    matrix_ref,
):
    radii, angles, axial = velocity_ref.shape[1:]
    matrix_ref[...] = derivative_matrix(stencil_ref, inverse_ref)
    group = radii * SUB

    def derive(i, carry):
        at = pl.ds(pl.multiple_of(i * SUB, SUB), SUB)
        columns = []
        for f, own_ref in enumerate((velocity_ref, stress_ref)):
            for c in range(3):
                value = jnp.concatenate(
                    [low_ref[f, c, :, at, :], own_ref[c, :, at, :], high_ref[f, c, :, at, :]],
                    axis=0,
                )
                columns.append(value.reshape((radii + 2 * HALO) * SUB, axial))
        field_high, field_low = split(jnp.concatenate(columns, axis=1))
        result = dot3(matrix_ref[...], field_high, field_low)
        for c in range(3):
            force = TIME_STEP * result[:, (3 + c) * axial : (4 + c) * axial]
            force_ref[c, :, at, :] = force.reshape(radii, SUB, axial)
        turned_high, turned_low = split(result[:, : 3 * axial].T)
        cols = pl.ds(pl.multiple_of(i * group, group), group)
        grad_ref[: 3 * axial, cols] = turned_high
        grad_ref[3 * axial :, cols] = turned_low
        return carry

    lax.fori_loop(0, angles // SUB, derive, 0)

    count = spring_ref.shape[3]
    part = min(count, 512)

    def read(i, carry):
        at = pl.ds(pl.multiple_of(i * part, part), part)
        plane = ids_ref[0, 0, :, at]
        radius, angle = plane // angles, plane % angles
        column = (angle // SUB) * group + radius * SUB + angle % SUB
        hot = jnp.where(iota((radii * angles, part), 0) == column, 1.0, 0.0).astype(BF16)
        picked = dot(grad_ref[...], hot)
        here = iota((axial, part), 0) == ids_ref[1, 0, :, at]
        q = [spring_ref[c, 0, :, at] for c in range(3)]
        stretch_sq = q[0] * q[0] + q[1] * q[1] + q[2] * q[2]
        factor = 1.0 / (1.0 - stretch_sq / MAX_STRETCH)
        for c in range(3):
            value = (
                picked[c * axial : (c + 1) * axial] + picked[(3 + c) * axial : (4 + c) * axial]
            )
            shear = jnp.sum(jnp.where(here, value, 0.0), axis=0, keepdims=True)
            moved_ref[c, 0, :, at] = (
                q[c]
                + TIME_STEP * (shear * q[0] - 0.5 * factor * q[c])
                + math.sqrt(TIME_STEP) * noise_ref[c, 0, :, at]
            )
        return carry

    lax.fori_loop(0, count // part, read, 0)


def move(stencil, inverse, low, velocity, stress, high, ids, spring, noise):
    radii, angles, axial = velocity.shape[1:]
    whole = pl.BlockSpec(memory_space=pltpu.VMEM)
    return pl.pallas_call(
        move_kernel,
        in_specs=[whole] * 9,
        out_specs=[whole, whole],
        out_shape=[
            jax.ShapeDtypeStruct(spring.shape, F32),
            pltpu.VMEM(velocity.shape, F32),
        ],
        scratch_shapes=[
            pltpu.VMEM((6 * axial, radii * angles), BF16),
            pltpu.VMEM((2 * radii * SUB, (radii + 2 * HALO) * SUB), BF16),
        ],
        compiler_params=pltpu.CompilerParams(vmem_limit_bytes=28 * MIB),
        cost_estimate=pl.CostEstimate(
            flops=14 * radii * angles * spring.shape[3] * axial,
            bytes_accessed=40 * radii * angles * axial,
            transcendentals=0,
        ),
        name="move",
    )(
        stencil,
        inverse,
        in_vmem(low),
        in_hbm(velocity),
        in_hbm(stress),
        in_vmem(high),
        ids,
        spring,
        noise,
    )


def fourier_tables(all_angles):
    half = all_angles // 2
    row = np.arange(half)
    quarter = half // 2
    waves = [
        np.where(row <= quarter, 2 * row, 2 * (row - quarter)),
        np.where(row < quarter, 2 * row + 1, 2 * (row - quarter) + 1),
    ]
    cosine = [row <= quarter, row < quarter]
    tables = []
    for wave, even in zip(waves, cosine):
        phase = (wave[:, None] * row[None, :]) % all_angles
        angle = phase * (2.0 * math.pi / all_angles)
        table = np.where(even[:, None], np.cos(angle), np.sin(angle))
        weight = np.where((wave == 0) | (wave == half), 1.0, 2.0) / all_angles
        for value in (table, table.T * weight[None, :]):
            tables.append(value.astype(np.float32))
    return np.stack(tables)


def solve_kernel(coef_ref, first_ref, float_ref, low_ref, high_ref, in_ref, out_ref, table_ref):
    blocks, rows, angles, axial = in_ref.shape
    half = blocks * angles // 2
    quarter = half // 2

    @pl.when(pl.program_id(0) == 0)
    def _():
        for i in range(4):
            high, low = split(float_ref[i])
            table_ref[i, :half] = high
            table_ref[i, half:] = low

    row = iota((half, axial), 0)
    waves = [
        jnp.where(row <= quarter, 2 * row, 2 * (row - quarter)),
        jnp.where(row < quarter, 2 * row + 1, 2 * (row - quarter) + 1),
    ]
    base = first_ref[0] + pl.program_id(0) * rows
    scale = [coef_ref[lax.rem(base + q, coef_ref.shape[0])] for q in range(rows)]
    near = [in_ref[: blocks // 2, q].reshape(half, axial) for q in range(rows)]
    far = [in_ref[blocks // 2 :, q].reshape(half, axial) for q in range(rows)]
    results = []
    for odd in range(2):
        field = jnp.concatenate(
            [a - b if odd else a + b for a, b in zip(near, far)], axis=1
        )
        spectrum = dot3(table_ref[2 * odd], *split(field))
        square = (waves[odd] * waves[odd]).astype(F32)
        damped = spectrum / (1.0 + jnp.concatenate([s * square for s in scale], axis=1))
        results.append(dot3(table_ref[2 * odd + 1], *split(damped)))
    for q in range(rows):
        even, odd = [value[:, q * axial : (q + 1) * axial] for value in results]
        out_ref[: blocks // 2, q] = (even + odd).reshape(blocks // 2, angles, axial)
        out_ref[blocks // 2 :, q] = (even - odd).reshape(blocks // 2, angles, axial)


def solve(coef, first, field, low, high):
    blocks, rows, angles, axial = field.shape
    all_angles = blocks * angles
    tables = fourier_tables(all_angles)
    half = all_angles // 2
    part = 2 if rows % 2 == 0 else 1
    field_spec = pl.BlockSpec((blocks, part, angles, axial), lambda i: (0, i, 0, 0))
    smem = pl.BlockSpec(memory_space=pltpu.SMEM)
    whole = pl.BlockSpec(memory_space=pltpu.VMEM)
    unread = pl.BlockSpec(memory_space=pl.ANY)
    return pl.pallas_call(
        solve_kernel,
        grid=(rows // part,),
        in_specs=[smem, smem, whole, unread, unread, field_spec],
        out_specs=field_spec,
        out_shape=pltpu.HBM(field.shape, F32),
        scratch_shapes=[pltpu.VMEM((4, 2 * half, half), BF16)],
        compiler_params=pltpu.CompilerParams(vmem_limit_bytes=14 * MIB),
        cost_estimate=pl.CostEstimate(
            flops=12 * all_angles * all_angles * rows * axial,
            bytes_accessed=8 * all_angles * rows * axial,
            transcendentals=0,
        ),
        name="solve",
    )(coef, first, in_hbm(jnp.asarray(tables)), in_vmem(low), in_vmem(high), in_vmem(field))


def join_kernel(force_ref, smooth_ref, out_ref, sum_ref, sems):
    parts = sems.shape[0]
    part = force_ref.shape[0] // parts
    copies = []
    for i in range(parts):
        at = pl.ds(i * part, part)
        sum_ref[at] = force_ref[at] + smooth_ref[at]
        copies.append(pltpu.make_async_copy(sum_ref.at[at], out_ref.at[at], sems.at[i]))
        copies[-1].start()
    for copy in copies:
        copy.wait()


def join(force, smooth):
    whole = pl.BlockSpec(memory_space=pltpu.VMEM)
    return pl.pallas_call(
        join_kernel,
        in_specs=[whole, whole],
        out_specs=pl.BlockSpec(memory_space=pl.ANY),
        out_shape=pltpu.HBM(force.shape, F32),
        scratch_shapes=[
            pltpu.VMEM(force.shape, F32),
            pltpu.SemaphoreType.DMA((math.gcd(force.shape[0], 8),)),
        ],
        compiler_params=pltpu.CompilerParams(vmem_limit_bytes=14 * MIB),
        cost_estimate=pl.CostEstimate(
            flops=force.size, bytes_accessed=12 * force.size, transcendentals=0
        ),
        name="join",
    )(in_vmem(force), in_vmem(smooth))


def from_neighbours(low_edge, high_edge):
    count = lax.axis_size("rad")
    forward = [(i, i + 1) for i in range(count - 1)]
    backward = [(target, source) for source, target in forward]
    low = lax.ppermute(high_edge, "rad", forward)
    high = lax.ppermute(low_edge, "rad", backward)
    return low, high


def per_device(velocity, dumbbells, cell_ids, brownian, stencil_coef, block_inverse, azim_coef):
    _, radii, angles, axial = velocity.shape
    az = lax.axis_size("az")
    rows = 3 * radii // az
    pieces = velocity.reshape(az, rows, angles, axial)
    gathered = lax.all_to_all(pieces, "az", 0, 0, tiled=True)
    stress, low_edge, high_edge = deposit(cell_ids, dumbbells, velocity)
    low, high = from_neighbours(low_edge, high_edge)
    first = (lax.axis_index("az") * rows).astype(jnp.int32).reshape(1)
    solved = solve(azim_coef, first, gathered, low, high)
    smooth = lax.all_to_all(solved, "az", 0, 0, tiled=True)
    moved, force = move(
        stencil_coef, block_inverse, low, velocity, stress, high, cell_ids, dumbbells, brownian
    )
    lines = (3 * radii, angles, axial)
    result = join(force.reshape(lines), smooth.reshape(lines))
    return result.reshape(velocity.shape), moved


def solution(mesh):
    placed = (
        P(None, "rad", "az", None),
        P(None, "rad", "az", None),
        P(None, "rad", "az", None),
        P(None, "rad", "az", None),
        P(None, "rad"),
        P("rad", None),
        P("rad"),
    )
    return jax.shard_map(
        per_device,
        mesh=mesh,
        in_specs=placed,
        out_specs=(P(None, "rad", "az", None), P(None, "rad", "az", None)),
        check_vma=False,
    )
```

```python
import functools
import functools
import math

import jax
import jax.numpy as jnp
import numpy as np
from jax import lax
from jax.experimental import pallas as pl
from jax.experimental.pallas import tpu as pltpu
from jax.sharding import PartitionSpec as P

TIME_STEP = 0.05
MAX_STRETCH = 10.0
STRESS_SCALE = 4.0
PRECISE = lax.Precision.HIGHEST
HALO = 4
SUB = 8
MIB = 1024 * 1024
F32 = jnp.float32
BF16 = jnp.bfloat16


def split(value):
    high = value.astype(BF16)
    return high, (value - high.astype(F32)).astype(BF16)


def dot(a, b):
    return jnp.dot(a, b, preferred_element_type=F32)


def dot3(stacked, b_high, b_low):
    rows = stacked.shape[0] // 2
    both = dot(stacked, b_high)
    return both[:rows] + both[rows:] + dot(stacked[:rows], b_low)

def in_hbm(value):
    return pltpu.with_memory_space_constraint(value, pltpu.HBM)


def in_vmem(value):
    return pltpu.with_memory_space_constraint(value, pltpu.VMEM)


def iota(shape, dim):
    return lax.broadcasted_iota(jnp.int32, shape, dim)


def weigh(ids_ref, spring_ref, weight_ref):
    axial = weight_ref.shape[0] // 6
    count = weight_ref.shape[1]
    q = [spring_ref[c, 0] for c in range(3)]
    stretch_sq = q[0] * q[0] + q[1] * q[1] + q[2] * q[2]
    factor = 1.0 / (1.0 - stretch_sq / MAX_STRETCH)
    here = iota((axial, count), 0) == ids_ref[1, 0]
    for c in range(3):
        weight = STRESS_SCALE * factor * q[0] * q[c]
        high = weight.astype(BF16).astype(F32)
        weight_ref[c * axial : (c + 1) * axial, :] = jnp.where(here, high, 0.0).astype(BF16)
        weight_ref[(3 + c) * axial : (4 + c) * axial, :] = jnp.where(
            here, weight - high, 0.0
        ).astype(BF16)


def gather_rows(ids_ref, weight_ref, first_row, rows):
    axial = weight_ref.shape[0] // 6
    count = weight_ref.shape[1]
    hot = jnp.where(iota((rows, count), 0) + first_row == ids_ref[0, 0], 1.0, 0.0).astype(BF16)
    both = lax.dot_general(
        hot, weight_ref[...], (((1,), (1,)), ((), ())), preferred_element_type=F32
    )
    return [
        both[:, c * axial : (c + 1) * axial] + both[:, (3 + c) * axial : (4 + c) * axial]
        for c in range(3)
    ]


def edge_kernel(ids_ref, spring_ref, first_ref, last_ref, low_ref, high_ref, weight_ref, *, radii):
    _, _, _, angles, axial = low_ref.shape
    weigh(ids_ref, spring_ref, weight_ref)
    for field_ref, out_ref, radius in (
        (first_ref, low_ref, 0),
        (last_ref, high_ref, radii - HALO),
    ):
        out_ref[0] = field_ref[...]
        values = gather_rows(ids_ref, weight_ref, radius * angles, HALO * angles)
        for c in range(3):
            out_ref[1, c] = values[c].reshape(HALO, angles, axial)


def middle_kernel(ids_ref, spring_ref, stress_ref, weight_ref):
    step = pl.program_id(0)
    _, radii, angles, axial = stress_ref.shape

    @pl.when(step == 0)
    def _():
        weigh(ids_ref, spring_ref, weight_ref)

    rows = radii * angles
    values = gather_rows(ids_ref, weight_ref, HALO * angles + step * rows, rows)
    for c in range(3):
        stress_ref[c] = values[c].reshape(radii, angles, axial)


def deposit_edges(ids, spring, velocity):
    _, radii, angles, axial = velocity.shape
    count = ids.shape[3]
    edge = (2, 3, HALO, angles, axial)
    edge_block = (3, HALO, angles, axial)
    whole = pl.BlockSpec(memory_space=pltpu.VMEM)
    return pl.pallas_call(
        functools.partial(edge_kernel, radii=radii),
        grid=(1,),
        in_specs=[
            whole,
            whole,
            pl.BlockSpec(edge_block, lambda i: (0, 0, 0, 0)),
            pl.BlockSpec(edge_block, lambda i: (0, radii // HALO - 1, 0, 0)),
        ],
        out_specs=[pl.BlockSpec(edge, lambda i: (0, 0, 0, 0, 0))] * 2,
        out_shape=[pltpu.HBM(edge, F32)] * 2,
        scratch_shapes=[pltpu.VMEM((6 * axial, count), BF16)],
        compiler_params=pltpu.CompilerParams(vmem_limit_bytes=28 * MIB),
        cost_estimate=pl.CostEstimate(
            flops=24 * HALO * angles * count * axial,
            bytes_accessed=96 * HALO * angles * axial,
            transcendentals=0,
        ),
        name="deposit_edges",
    )(ids, spring, in_hbm(velocity), in_hbm(velocity))


def deposit_middle(ids, spring, low_edge, shape):
    _, radii, angles, axial = shape
    count = ids.shape[3]
    inner = radii - 2 * HALO
    part = math.gcd(inner, max(1, 512 // angles))
    whole = pl.BlockSpec(memory_space=pltpu.VMEM)
    return pl.pallas_call(
        lambda ids_ref, spring_ref, _, *refs: middle_kernel(ids_ref, spring_ref, *refs),
        grid=(inner // part,),
        in_specs=[whole, whole, pl.BlockSpec(memory_space=pl.ANY)],
        out_specs=pl.BlockSpec((3, part, angles, axial), lambda i: (0, i, 0, 0)),
        out_shape=pltpu.HBM((3, inner, angles, axial), F32),
        scratch_shapes=[pltpu.VMEM((6 * axial, count), BF16)],
        compiler_params=pltpu.CompilerParams(vmem_limit_bytes=28 * MIB),
        cost_estimate=pl.CostEstimate(
            flops=12 * inner * angles * count * axial,
            bytes_accessed=12 * inner * angles * axial,
            transcendentals=0,
        ),
        name="deposit_middle",
    )(ids, spring, in_hbm(low_edge))


def derivative_matrix(stencil_ref, inverse_ref):
    rows = inverse_ref.shape[1]
    wide = rows + 2 * HALO
    offset = iota((wide, rows), 0) - iota((wide, rows), 1)
    band = jnp.zeros((wide, rows), F32)
    for s in range(2 * HALO + 1):
        band = band + jnp.where(offset == s, stencil_ref[s : s + 1, :], 0.0)
    small = lax.dot_general(
        inverse_ref[...],
        band,
        (((1,), (1,)), ((), ())),
        precision=PRECISE,
        preferred_element_type=F32,
    )
    tall = jnp.where(iota((rows * SUB, rows), 0) // SUB == iota((rows * SUB, rows), 1), 1.0, 0.0)
    flat = jnp.where(iota((wide, wide * SUB), 1) // SUB == iota((wide, wide * SUB), 0), 1.0, 0.0)
    big = (rows * SUB, wide * SUB)
    same = iota(big, 0) % SUB == iota(big, 1) % SUB
    parts = []
    for part in split(small):
        spread = dot(dot(tall.astype(BF16), part).astype(BF16), flat.astype(BF16))
        parts.append(jnp.where(same, spread, 0.0).astype(BF16))
    return jnp.concatenate(parts, axis=0)


def move_kernel(
    stencil_ref,
    inverse_ref,
    low_ref,
    velocity_ref,
    low_edge_ref,
    middle_ref,
    high_edge_ref,
    high_ref,
    ids_ref,
    spring_ref,
    noise_ref,
    moved_ref,
    force_ref,
    grad_ref,
    matrix_ref,
):
    radii, angles, axial = velocity_ref.shape[1:]
    matrix_ref[...] = derivative_matrix(stencil_ref, inverse_ref)
    group = radii * SUB

    def derive(i, carry):
        at = pl.ds(pl.multiple_of(i * SUB, SUB), SUB)
        columns = []
        own = [
            [velocity_ref],
            [low_edge_ref.at[1], middle_ref, high_edge_ref.at[1]],
        ]
        for f in range(2):
            refs = [low_ref.at[f]] + own[f] + [high_ref.at[f]]
            for c in range(3):
                value = jnp.concatenate([ref[c, :, at, :] for ref in refs], axis=0)
                columns.append(value.reshape((radii + 2 * HALO) * SUB, axial))
        field_high, field_low = split(jnp.concatenate(columns, axis=1))
        result = dot3(matrix_ref[...], field_high, field_low)
        for c in range(3):
            force = TIME_STEP * result[:, (3 + c) * axial : (4 + c) * axial]
            force_ref[c, :, at, :] = force.reshape(radii, SUB, axial)
        turned_high, turned_low = split(result[:, : 3 * axial].T)
        cols = pl.ds(pl.multiple_of(i * group, group), group)
        grad_ref[: 3 * axial, cols] = turned_high
        grad_ref[3 * axial :, cols] = turned_low
        return carry

    lax.fori_loop(0, angles // SUB, derive, 0)

    count = spring_ref.shape[3]
    part = min(count, 512)

    def read(i, carry):
        at = pl.ds(pl.multiple_of(i * part, part), part)
        plane = ids_ref[0, 0, :, at]
        radius, angle = plane // angles, plane % angles
        column = (angle // SUB) * group + radius * SUB + angle % SUB
        hot = jnp.where(iota((radii * angles, part), 0) == column, 1.0, 0.0).astype(BF16)
        picked = dot(grad_ref[...], hot)
        here = iota((axial, part), 0) == ids_ref[1, 0, :, at]
        q = [spring_ref[c, 0, :, at] for c in range(3)]
        stretch_sq = q[0] * q[0] + q[1] * q[1] + q[2] * q[2]
        factor = 1.0 / (1.0 - stretch_sq / MAX_STRETCH)
        for c in range(3):
            value = (
                picked[c * axial : (c + 1) * axial] + picked[(3 + c) * axial : (4 + c) * axial]
            )
            shear = jnp.sum(jnp.where(here, value, 0.0), axis=0, keepdims=True)
            moved_ref[c, 0, :, at] = (
                q[c]
                + TIME_STEP * (shear * q[0] - 0.5 * factor * q[c])
                + math.sqrt(TIME_STEP) * noise_ref[c, 0, :, at]
            )
        return carry

    lax.fori_loop(0, count // part, read, 0)


def move(stencil, inverse, low, velocity, stress, high, ids, spring, noise):
    low_edge, middle, high_edge = stress
    radii, angles, axial = velocity.shape[1:]
    whole = pl.BlockSpec(memory_space=pltpu.VMEM)
    return pl.pallas_call(
        move_kernel,
        in_specs=[whole] * 11,
        out_specs=[whole, whole],
        out_shape=[
            jax.ShapeDtypeStruct(spring.shape, F32),
            pltpu.HBM(velocity.shape, F32),
        ],
        scratch_shapes=[
            pltpu.VMEM((6 * axial, radii * angles), BF16),
            pltpu.VMEM((2 * radii * SUB, (radii + 2 * HALO) * SUB), BF16),
        ],
        compiler_params=pltpu.CompilerParams(vmem_limit_bytes=28 * MIB),
        cost_estimate=pl.CostEstimate(
            flops=14 * radii * angles * spring.shape[3] * axial,
            bytes_accessed=40 * radii * angles * axial,
            transcendentals=0,
        ),
        name="move",
    )(
        stencil,
        inverse,
        in_vmem(low),
        in_hbm(velocity),
        in_hbm(low_edge),
        in_hbm(middle),
        in_hbm(high_edge),
        in_vmem(high),
        ids,
        spring,
        noise,
    )


def fourier_tables(all_angles):
    half = all_angles // 2
    row = np.arange(half)
    quarter = half // 2
    waves = [
        np.where(row <= quarter, 2 * row, 2 * (row - quarter)),
        np.where(row < quarter, 2 * row + 1, 2 * (row - quarter) + 1),
    ]
    cosine = [row <= quarter, row < quarter]
    tables = []
    for wave, even in zip(waves, cosine):
        phase = (wave[:, None] * row[None, :]) % all_angles
        angle = phase * (2.0 * math.pi / all_angles)
        table = np.where(even[:, None], np.cos(angle), np.sin(angle))
        weight = np.where((wave == 0) | (wave == half), 1.0, 2.0) / all_angles
        for value in (table, table.T * weight[None, :]):
            value = value.astype(np.float32)
            high = value.astype(BF16)
            low = (value - high.astype(np.float32)).astype(BF16)
            tables.append(np.concatenate([high, low, high], axis=1))
    return np.stack(tables)


def product(table, value):
    high, low = split(value)
    return dot(table, jnp.concatenate([high, high, low], axis=0))


def solve_kernel(coef_ref, first_ref, table_ref, *refs):
    in_ref, out_ref = refs[-2:]
    blocks, rows, angles, axial = in_ref.shape
    half = blocks * angles // 2
    quarter = half // 2
    row = iota((half, axial), 0)
    waves = [
        jnp.where(row <= quarter, 2 * row, 2 * (row - quarter)),
        jnp.where(row < quarter, 2 * row + 1, 2 * (row - quarter) + 1),
    ]
    base = first_ref[0] + pl.program_id(0) * rows
    scale = [coef_ref[lax.rem(base + q, coef_ref.shape[0])] for q in range(rows)]
    near = [in_ref[: blocks // 2, q].reshape(half, axial) for q in range(rows)]
    far = [in_ref[blocks // 2 :, q].reshape(half, axial) for q in range(rows)]
    results = []
    for odd in range(2):
        field = jnp.concatenate(
            [a - b if odd else a + b for a, b in zip(near, far)], axis=1
        )
        spectrum = product(table_ref[2 * odd], field)
        square = (waves[odd] * waves[odd]).astype(F32)
        damped = spectrum / (1.0 + jnp.concatenate([s * square for s in scale], axis=1))
        results.append(product(table_ref[2 * odd + 1], damped))
    for q in range(rows):
        even, odd = [value[:, q * axial : (q + 1) * axial] for value in results]
        out_ref[: blocks // 2, q] = (even + odd).reshape(blocks // 2, angles, axial)
        out_ref[blocks // 2 :, q] = (even - odd).reshape(blocks // 2, angles, axial)


def solve(coef, first, field, after):
    blocks, rows, angles, axial = field.shape
    all_angles = blocks * angles
    tables = fourier_tables(all_angles)
    part = math.gcd(rows, 4)
    field_spec = pl.BlockSpec((blocks, part, angles, axial), lambda i: (0, i, 0, 0))
    smem = pl.BlockSpec(memory_space=pltpu.SMEM)
    whole = pl.BlockSpec(memory_space=pltpu.VMEM)
    unread = pl.BlockSpec(memory_space=pl.ANY)
    return pl.pallas_call(
        solve_kernel,
        grid=(rows // part,),
        in_specs=[smem, smem, whole] + [unread] * len(after) + [field_spec],
        out_specs=field_spec,
        out_shape=pltpu.HBM(field.shape, F32),
        compiler_params=pltpu.CompilerParams(vmem_limit_bytes=24 * MIB),
        cost_estimate=pl.CostEstimate(
            flops=12 * all_angles * all_angles * rows * axial,
            bytes_accessed=8 * all_angles * rows * axial,
            transcendentals=0,
        ),
        name="solve",
    )(
        coef,
        first,
        in_hbm(jnp.asarray(tables)),
        *after,
        in_vmem(field),
    )


def join_kernel(force_ref, smooth_ref, out_ref, sum_ref, in_sems, out_sems):
    parts = in_sems.shape[0]
    part = sum_ref.shape[0] // parts
    spans = [pl.ds(i * part, part) for i in range(parts)]
    reads = [
        pltpu.make_async_copy(force_ref.at[at], sum_ref.at[at], in_sems.at[i])
        for i, at in enumerate(spans)
    ]
    writes = [
        pltpu.make_async_copy(sum_ref.at[at], out_ref.at[at], out_sems.at[i])
        for i, at in enumerate(spans)
    ]
    for copy in reads:
        copy.start()
    for i, at in enumerate(spans):
        reads[i].wait()
        sum_ref[at] = sum_ref[at] + smooth_ref[at]
        writes[i].start()
    for copy in writes:
        copy.wait()


def join(force, smooth):
    whole = pl.BlockSpec(memory_space=pltpu.VMEM)
    return pl.pallas_call(
        join_kernel,
        in_specs=[pl.BlockSpec(memory_space=pl.ANY), whole],
        out_specs=pl.BlockSpec(memory_space=pl.ANY),
        out_shape=pltpu.HBM(force.shape, F32),
        scratch_shapes=[
            pltpu.VMEM(force.shape, F32),
            pltpu.SemaphoreType.DMA((math.gcd(force.shape[0], 8),)),
            pltpu.SemaphoreType.DMA((math.gcd(force.shape[0], 8),)),
        ],
        compiler_params=pltpu.CompilerParams(vmem_limit_bytes=14 * MIB),
        cost_estimate=pl.CostEstimate(
            flops=force.size, bytes_accessed=12 * force.size, transcendentals=0
        ),
        name="join",
    )(in_hbm(force), in_vmem(smooth))


def from_neighbours(low_edge, high_edge):
    count = lax.axis_size("rad")
    forward = [(i, i + 1) for i in range(count - 1)]
    backward = [(target, source) for source, target in forward]
    low = lax.ppermute(high_edge, "rad", forward)
    high = lax.ppermute(low_edge, "rad", backward)
    return low, high


def per_device(velocity, dumbbells, cell_ids, brownian, stencil_coef, block_inverse, azim_coef):
    _, radii, angles, axial = velocity.shape
    az = lax.axis_size("az")
    rows = 3 * radii // az
    pieces = velocity.reshape(az, rows, angles, axial)
    gathered = lax.all_to_all(pieces, "az", 0, 0, tiled=True)
    low_edge, high_edge = deposit_edges(cell_ids, dumbbells, velocity)
    low, high = from_neighbours(low_edge, high_edge)
    middle = deposit_middle(cell_ids, dumbbells, low_edge, velocity.shape)
    stress = (low_edge, middle, high_edge)
    first = (lax.axis_index("az") * rows).astype(jnp.int32).reshape(1)
    solved = solve(azim_coef, first, gathered, (in_vmem(low), in_vmem(high), in_hbm(middle)))
    smooth = lax.all_to_all(solved, "az", 0, 0, tiled=True)
    moved, force = move(
        stencil_coef, block_inverse, low, velocity, stress, high, cell_ids, dumbbells, brownian
    )
    lines = (3 * radii, angles, axial)
    result = join(force.reshape(lines), smooth.reshape(lines))
    return result.reshape(velocity.shape), moved


def solution(mesh):
    placed = (
        P(None, "rad", "az", None),
        P(None, "rad", "az", None),
        P(None, "rad", "az", None),
        P(None, "rad", "az", None),
        P(None, "rad"),
        P("rad", None),
        P("rad"),
    )
    return jax.shard_map(
        per_device,
        mesh=mesh,
        in_specs=placed,
        out_specs=(P(None, "rad", "az", None), P(None, "rad", "az", None)),
        check_vma=False,
    )
```

```python
import functools
import functools
import math

import jax
import jax.numpy as jnp
import numpy as np
from jax import lax
from jax.experimental import pallas as pl
from jax.experimental.pallas import tpu as pltpu
from jax.sharding import PartitionSpec as P

TIME_STEP = 0.05
MAX_STRETCH = 10.0
STRESS_SCALE = 4.0
PRECISE = lax.Precision.HIGHEST
HALO = 4
SUB = 8
MIB = 1024 * 1024
F32 = jnp.float32
BF16 = jnp.bfloat16


def split(value):
    high = value.astype(BF16)
    return high, (value - high.astype(F32)).astype(BF16)


def dot(a, b):
    return jnp.dot(a, b, preferred_element_type=F32)


def dot3(stacked, b_high, b_low):
    rows = stacked.shape[0] // 2
    both = dot(stacked, b_high)
    return both[:rows] + both[rows:] + dot(stacked[:rows], b_low)

def in_hbm(value):
    return pltpu.with_memory_space_constraint(value, pltpu.HBM)


def in_vmem(value):
    return pltpu.with_memory_space_constraint(value, pltpu.VMEM)


def iota(shape, dim):
    return lax.broadcasted_iota(jnp.int32, shape, dim)


def weigh(ids_ref, spring_ref, weight_ref):
    axial = weight_ref.shape[0] // 6
    count = weight_ref.shape[1]
    q = [spring_ref[c, 0] for c in range(3)]
    stretch_sq = q[0] * q[0] + q[1] * q[1] + q[2] * q[2]
    factor = 1.0 / (1.0 - stretch_sq / MAX_STRETCH)
    here = iota((axial, count), 0) == ids_ref[1, 0]
    for c in range(3):
        weight = STRESS_SCALE * factor * q[0] * q[c]
        high = weight.astype(BF16).astype(F32)
        weight_ref[c * axial : (c + 1) * axial, :] = jnp.where(here, high, 0.0).astype(BF16)
        weight_ref[(3 + c) * axial : (4 + c) * axial, :] = jnp.where(
            here, weight - high, 0.0
        ).astype(BF16)


def gather_rows(ids_ref, weight_ref, first_row, rows):
    axial = weight_ref.shape[0] // 6
    count = weight_ref.shape[1]
    hot = jnp.where(iota((rows, count), 0) + first_row == ids_ref[0, 0], 1.0, 0.0).astype(BF16)
    both = lax.dot_general(
        hot, weight_ref[...], (((1,), (1,)), ((), ())), preferred_element_type=F32
    )
    return [
        both[:, c * axial : (c + 1) * axial] + both[:, (3 + c) * axial : (4 + c) * axial]
        for c in range(3)
    ]


def edge_kernel(ids_ref, spring_ref, first_ref, last_ref, low_ref, high_ref, weight_ref, *, radii):
    _, _, _, angles, axial = low_ref.shape
    weigh(ids_ref, spring_ref, weight_ref)
    for field_ref, out_ref, radius in (
        (first_ref, low_ref, 0),
        (last_ref, high_ref, radii - HALO),
    ):
        out_ref[0] = field_ref[...]
        values = gather_rows(ids_ref, weight_ref, radius * angles, HALO * angles)
        for c in range(3):
            out_ref[1, c] = values[c].reshape(HALO, angles, axial)


def middle_kernel(ids_ref, spring_ref, stress_ref, weight_ref):
    step = pl.program_id(0)
    _, radii, angles, axial = stress_ref.shape

    @pl.when(step == 0)
    def _():
        weigh(ids_ref, spring_ref, weight_ref)

    rows = radii * angles
    values = gather_rows(ids_ref, weight_ref, HALO * angles + step * rows, rows)
    for c in range(3):
        stress_ref[c] = values[c].reshape(radii, angles, axial)


def deposit_edges(ids, spring, velocity):
    _, radii, angles, axial = velocity.shape
    count = ids.shape[3]
    edge = (2, 3, HALO, angles, axial)
    edge_block = (3, HALO, angles, axial)
    whole = pl.BlockSpec(memory_space=pltpu.VMEM)
    return pl.pallas_call(
        functools.partial(edge_kernel, radii=radii),
        grid=(1,),
        in_specs=[
            whole,
            whole,
            pl.BlockSpec(edge_block, lambda i: (0, 0, 0, 0)),
            pl.BlockSpec(edge_block, lambda i: (0, radii // HALO - 1, 0, 0)),
        ],
        out_specs=[pl.BlockSpec(edge, lambda i: (0, 0, 0, 0, 0))] * 2,
        out_shape=[pltpu.HBM(edge, F32)] * 2,
        scratch_shapes=[pltpu.VMEM((6 * axial, count), BF16)],
        compiler_params=pltpu.CompilerParams(vmem_limit_bytes=28 * MIB),
        cost_estimate=pl.CostEstimate(
            flops=24 * HALO * angles * count * axial,
            bytes_accessed=96 * HALO * angles * axial,
            transcendentals=0,
        ),
        name="deposit_edges",
    )(ids, spring, in_hbm(velocity), in_hbm(velocity))


def deposit_middle(ids, spring, low_edge, shape):
    _, radii, angles, axial = shape
    count = ids.shape[3]
    inner = radii - 2 * HALO
    part = math.gcd(inner, max(1, 512 // angles))
    whole = pl.BlockSpec(memory_space=pltpu.VMEM)
    return pl.pallas_call(
        lambda ids_ref, spring_ref, _, *refs: middle_kernel(ids_ref, spring_ref, *refs),
        grid=(inner // part,),
        in_specs=[whole, whole, pl.BlockSpec(memory_space=pl.ANY)],
        out_specs=pl.BlockSpec((3, part, angles, axial), lambda i: (0, i, 0, 0)),
        out_shape=pltpu.HBM((3, inner, angles, axial), F32),
        scratch_shapes=[pltpu.VMEM((6 * axial, count), BF16)],
        compiler_params=pltpu.CompilerParams(vmem_limit_bytes=28 * MIB),
        cost_estimate=pl.CostEstimate(
            flops=12 * inner * angles * count * axial,
            bytes_accessed=12 * inner * angles * axial,
            transcendentals=0,
        ),
        name="deposit_middle",
    )(ids, spring, in_hbm(low_edge))


def derivative_matrix(stencil_ref, inverse_ref):
    rows = inverse_ref.shape[1]
    wide = rows + 2 * HALO
    offset = iota((wide, rows), 0) - iota((wide, rows), 1)
    band = jnp.zeros((wide, rows), F32)
    for s in range(2 * HALO + 1):
        band = band + jnp.where(offset == s, stencil_ref[s : s + 1, :], 0.0)
    small = lax.dot_general(
        inverse_ref[...],
        band,
        (((1,), (1,)), ((), ())),
        precision=PRECISE,
        preferred_element_type=F32,
    )
    tall = jnp.where(iota((rows * SUB, rows), 0) // SUB == iota((rows * SUB, rows), 1), 1.0, 0.0)
    flat = jnp.where(iota((wide, wide * SUB), 1) // SUB == iota((wide, wide * SUB), 0), 1.0, 0.0)
    big = (rows * SUB, wide * SUB)
    same = iota(big, 0) % SUB == iota(big, 1) % SUB
    parts = []
    for part in split(small):
        spread = dot(dot(tall.astype(BF16), part).astype(BF16), flat.astype(BF16))
        parts.append(jnp.where(same, spread, 0.0).astype(BF16))
    return jnp.concatenate(parts, axis=0)


def move_kernel(
    stencil_ref,
    inverse_ref,
    low_ref,
    velocity_ref,
    low_edge_ref,
    middle_ref,
    high_edge_ref,
    high_ref,
    ids_ref,
    spring_ref,
    noise_ref,
    moved_ref,
    force_ref,
    grad_ref,
    matrix_ref,
):
    radii, angles, axial = velocity_ref.shape[1:]
    matrix_ref[...] = derivative_matrix(stencil_ref, inverse_ref)
    group = radii * SUB

    def derive(i, carry):
        at = pl.ds(pl.multiple_of(i * SUB, SUB), SUB)
        columns = []
        own = [
            [velocity_ref],
            [low_edge_ref.at[1], middle_ref, high_edge_ref.at[1]],
        ]
        for f in range(2):
            refs = [low_ref.at[f]] + own[f] + [high_ref.at[f]]
            for c in range(3):
                value = jnp.concatenate([ref[c, :, at, :] for ref in refs], axis=0)
                columns.append(value.reshape((radii + 2 * HALO) * SUB, axial))
        field_high, field_low = split(jnp.concatenate(columns, axis=1))
        result = dot3(matrix_ref[...], field_high, field_low)
        for c in range(3):
            force = TIME_STEP * result[:, (3 + c) * axial : (4 + c) * axial]
            force_ref[c, :, at, :] = force.reshape(radii, SUB, axial)
        turned_high, turned_low = split(result[:, : 3 * axial].T)
        cols = pl.ds(pl.multiple_of(i * group, group), group)
        grad_ref[: 3 * axial, cols] = turned_high
        grad_ref[3 * axial :, cols] = turned_low
        return carry

    lax.fori_loop(0, angles // SUB, derive, 0)

    count = spring_ref.shape[3]
    part = min(count, 512)

    def read(i, carry):
        at = pl.ds(pl.multiple_of(i * part, part), part)
        plane = ids_ref[0, 0, :, at]
        radius, angle = plane // angles, plane % angles
        column = (angle // SUB) * group + radius * SUB + angle % SUB
        hot = jnp.where(iota((radii * angles, part), 0) == column, 1.0, 0.0).astype(BF16)
        picked = dot(grad_ref[...], hot)
        here = iota((axial, part), 0) == ids_ref[1, 0, :, at]
        q = [spring_ref[c, 0, :, at] for c in range(3)]
        stretch_sq = q[0] * q[0] + q[1] * q[1] + q[2] * q[2]
        factor = 1.0 / (1.0 - stretch_sq / MAX_STRETCH)
        for c in range(3):
            value = (
                picked[c * axial : (c + 1) * axial] + picked[(3 + c) * axial : (4 + c) * axial]
            )
            shear = jnp.sum(jnp.where(here, value, 0.0), axis=0, keepdims=True)
            moved_ref[c, 0, :, at] = (
                q[c]
                + TIME_STEP * (shear * q[0] - 0.5 * factor * q[c])
                + math.sqrt(TIME_STEP) * noise_ref[c, 0, :, at]
            )
        return carry

    lax.fori_loop(0, count // part, read, 0)


def move(stencil, inverse, low, velocity, stress, high, ids, spring, noise):
    low_edge, middle, high_edge = stress
    radii, angles, axial = velocity.shape[1:]
    whole = pl.BlockSpec(memory_space=pltpu.VMEM)
    return pl.pallas_call(
        move_kernel,
        in_specs=[whole] * 11,
        out_specs=[whole, whole],
        out_shape=[
            jax.ShapeDtypeStruct(spring.shape, F32),
            pltpu.HBM(velocity.shape, F32),
        ],
        scratch_shapes=[
            pltpu.VMEM((6 * axial, radii * angles), BF16),
            pltpu.VMEM((2 * radii * SUB, (radii + 2 * HALO) * SUB), BF16),
        ],
        compiler_params=pltpu.CompilerParams(vmem_limit_bytes=28 * MIB),
        cost_estimate=pl.CostEstimate(
            flops=14 * radii * angles * spring.shape[3] * axial,
            bytes_accessed=40 * radii * angles * axial,
            transcendentals=0,
        ),
        name="move",
    )(
        stencil,
        inverse,
        in_vmem(low),
        in_hbm(velocity),
        in_hbm(low_edge),
        in_hbm(middle),
        in_hbm(high_edge),
        in_vmem(high),
        ids,
        spring,
        noise,
    )


def fourier_tables(all_angles):
    half = all_angles // 2
    row = np.arange(half)
    quarter = half // 2
    waves = [
        np.where(row <= quarter, 2 * row, 2 * (row - quarter)),
        np.where(row < quarter, 2 * row + 1, 2 * (row - quarter) + 1),
    ]
    cosine = [row <= quarter, row < quarter]
    tables = []
    for wave, even in zip(waves, cosine):
        phase = (wave[:, None] * row[None, :]) % all_angles
        angle = phase * (2.0 * math.pi / all_angles)
        table = np.where(even[:, None], np.cos(angle), np.sin(angle))
        weight = np.where((wave == 0) | (wave == half), 1.0, 2.0) / all_angles
        for value in (table, table.T * weight[None, :]):
            value = value.astype(np.float32)
            high = value.astype(BF16)
            low = (value - high.astype(np.float32)).astype(BF16)
            tables.append(np.concatenate([high, low, high], axis=1))
    return np.stack(tables)


def product(table, value):
    high, low = split(value)
    return dot(table, jnp.concatenate([high, high, low], axis=0))


def solve_kernel(coef_ref, first_ref, tables_ref, *refs):
    in_ref, out_ref, table_ref, done_ref, table_sems, out_sems = refs[-6:]
    blocks, rows, angles, axial = in_ref.shape
    half = blocks * angles // 2
    quarter = half // 2
    part = rows // out_sems.shape[0]
    loads = [
        pltpu.make_async_copy(tables_ref.at[i], table_ref.at[i], table_sems.at[i])
        for i in range(4)
    ]
    for copy in loads:
        copy.start()

    base = first_ref[0]
    lane = iota((1, axial), 1)
    coef = jnp.zeros((1, axial), F32)
    for q in range(rows):
        coef = jnp.where(lane == q, coef_ref[lax.rem(base + q, coef_ref.shape[0])], coef)
    row = iota((half, axial), 0)
    waves = [
        jnp.where(row <= quarter, 2 * row, 2 * (row - quarter)),
        jnp.where(row < quarter, 2 * row + 1, 2 * (row - quarter) + 1),
    ]
    damping = [1.0 / (1.0 + coef * (wave * wave).astype(F32)) for wave in waves]

    stores = []
    for g in range(rows // part):
        chosen = range(g * part, (g + 1) * part)
        near = [in_ref[: blocks // 2, q].reshape(half, axial) for q in chosen]
        far = [in_ref[blocks // 2 :, q].reshape(half, axial) for q in chosen]
        results = []
        for odd in range(2):
            field = jnp.concatenate([a - b if odd else a + b for a, b in zip(near, far)], axis=1)
            if g == 0:
                loads[2 * odd].wait()
            spectrum = product(table_ref[2 * odd], field)
            scale = [
                jnp.broadcast_to(damping[odd][:, q : q + 1], (half, axial)) for q in chosen
            ]
            if g == 0:
                loads[2 * odd + 1].wait()
            damped = spectrum * jnp.concatenate(scale, axis=1)
            results.append(product(table_ref[2 * odd + 1], damped))
        for i, q in enumerate(chosen):
            even, odd = [value[:, i * axial : (i + 1) * axial] for value in results]
            done_ref[: blocks // 2, q] = (even + odd).reshape(blocks // 2, angles, axial)
            done_ref[blocks // 2 :, q] = (even - odd).reshape(blocks // 2, angles, axial)
        at = pl.ds(g * part, part)
        stores.append(
            pltpu.make_async_copy(done_ref.at[:, at], out_ref.at[:, at], out_sems.at[g])
        )
        stores[-1].start()
    for copy in stores:
        copy.wait()


def solve(coef, first, field, after):
    blocks, rows, angles, axial = field.shape
    all_angles = blocks * angles
    tables = fourier_tables(all_angles)
    parts = rows // math.gcd(rows, 4)
    smem = pl.BlockSpec(memory_space=pltpu.SMEM)
    whole = pl.BlockSpec(memory_space=pltpu.VMEM)
    unread = pl.BlockSpec(memory_space=pl.ANY)
    return pl.pallas_call(
        solve_kernel,
        in_specs=[smem, smem, unread] + [unread] * len(after) + [whole],
        out_specs=unread,
        out_shape=pltpu.HBM(field.shape, F32),
        scratch_shapes=[
            pltpu.VMEM(tables.shape, BF16),
            pltpu.VMEM(field.shape, F32),
            pltpu.SemaphoreType.DMA((4,)),
            pltpu.SemaphoreType.DMA((parts,)),
        ],
        compiler_params=pltpu.CompilerParams(vmem_limit_bytes=28 * MIB),
        cost_estimate=pl.CostEstimate(
            flops=12 * all_angles * all_angles * rows * axial,
            bytes_accessed=8 * all_angles * rows * axial,
            transcendentals=0,
        ),
        name="solve",
    )(
        coef,
        first,
        in_hbm(jnp.asarray(tables)),
        *after,
        in_vmem(field),
    )


def join_kernel(force_ref, smooth_ref, out_ref, sum_ref, sems):
    parts = sems.shape[0]
    part = force_ref.shape[0] // parts
    copies = []
    for i in range(parts):
        at = pl.ds(i * part, part)
        sum_ref[at] = force_ref[at] + smooth_ref[at]
        copies.append(pltpu.make_async_copy(sum_ref.at[at], out_ref.at[at], sems.at[i]))
        copies[-1].start()
    for copy in copies:
        copy.wait()


def join(force, smooth):
    whole = pl.BlockSpec(memory_space=pltpu.VMEM)
    return pl.pallas_call(
        join_kernel,
        in_specs=[whole, whole],
        out_specs=pl.BlockSpec(memory_space=pl.ANY),
        out_shape=pltpu.HBM(force.shape, F32),
        scratch_shapes=[
            pltpu.VMEM(force.shape, F32),
            pltpu.SemaphoreType.DMA((math.gcd(force.shape[0], 8),)),
        ],
        compiler_params=pltpu.CompilerParams(vmem_limit_bytes=14 * MIB),
        cost_estimate=pl.CostEstimate(
            flops=force.size, bytes_accessed=12 * force.size, transcendentals=0
        ),
        name="join",
    )(in_vmem(force), in_vmem(smooth))


def from_neighbours(low_edge, high_edge):
    count = lax.axis_size("rad")
    forward = [(i, i + 1) for i in range(count - 1)]
    backward = [(target, source) for source, target in forward]
    low = lax.ppermute(high_edge, "rad", forward)
    high = lax.ppermute(low_edge, "rad", backward)
    return low, high


def per_device(velocity, dumbbells, cell_ids, brownian, stencil_coef, block_inverse, azim_coef):
    _, radii, angles, axial = velocity.shape
    az = lax.axis_size("az")
    rows = 3 * radii // az
    pieces = velocity.reshape(az, rows, angles, axial)
    gathered = lax.all_to_all(pieces, "az", 0, 0, tiled=True)
    low_edge, high_edge = deposit_edges(cell_ids, dumbbells, velocity)
    low, high = from_neighbours(low_edge, high_edge)
    middle = deposit_middle(cell_ids, dumbbells, low_edge, velocity.shape)
    stress = (low_edge, middle, high_edge)
    first = (lax.axis_index("az") * rows).astype(jnp.int32).reshape(1)
    solved = solve(azim_coef, first, gathered, (in_vmem(low), in_vmem(high), in_hbm(middle)))
    smooth = lax.all_to_all(solved, "az", 0, 0, tiled=True)
    moved, force = move(
        stencil_coef, block_inverse, low, velocity, stress, high, cell_ids, dumbbells, brownian
    )
    lines = (3 * radii, angles, axial)
    result = join(force.reshape(lines), smooth.reshape(lines))
    return result.reshape(velocity.shape), moved


def solution(mesh):
    placed = (
        P(None, "rad", "az", None),
        P(None, "rad", "az", None),
        P(None, "rad", "az", None),
        P(None, "rad", "az", None),
        P(None, "rad"),
        P("rad", None),
        P("rad"),
    )
    return jax.shard_map(
        per_device,
        mesh=mesh,
        in_specs=placed,
        out_specs=(P(None, "rad", "az", None), P(None, "rad", "az", None)),
        check_vma=False,
    )
```

```python
import functools
import functools
import math

import jax
import jax.numpy as jnp
import numpy as np
from jax import lax
from jax.experimental import pallas as pl
from jax.experimental.pallas import tpu as pltpu
from jax.sharding import PartitionSpec as P

TIME_STEP = 0.05
MAX_STRETCH = 10.0
STRESS_SCALE = 4.0
PRECISE = lax.Precision.HIGHEST
HALO = 4
SUB = 8
MIB = 1024 * 1024
F32 = jnp.float32
BF16 = jnp.bfloat16


def split(value):
    high = value.astype(BF16)
    return high, (value - high.astype(F32)).astype(BF16)


def dot(a, b):
    return jnp.dot(a, b, preferred_element_type=F32)


def dot3(stacked, b_high, b_low):
    rows = stacked.shape[0] // 2
    both = dot(stacked, b_high)
    return both[:rows] + both[rows:] + dot(stacked[:rows], b_low)

def in_hbm(value):
    return pltpu.with_memory_space_constraint(value, pltpu.HBM)


def in_vmem(value):
    return pltpu.with_memory_space_constraint(value, pltpu.VMEM)


def iota(shape, dim):
    return lax.broadcasted_iota(jnp.int32, shape, dim)


def weigh(ids_ref, spring_ref, weight_ref):
    axial = weight_ref.shape[0] // 6
    count = weight_ref.shape[1]
    q = [spring_ref[c, 0] for c in range(3)]
    stretch_sq = q[0] * q[0] + q[1] * q[1] + q[2] * q[2]
    factor = 1.0 / (1.0 - stretch_sq / MAX_STRETCH)
    here = iota((axial, count), 0) == ids_ref[1, 0]
    for c in range(3):
        weight = STRESS_SCALE * factor * q[0] * q[c]
        high = weight.astype(BF16).astype(F32)
        weight_ref[c * axial : (c + 1) * axial, :] = jnp.where(here, high, 0.0).astype(BF16)
        weight_ref[(3 + c) * axial : (4 + c) * axial, :] = jnp.where(
            here, weight - high, 0.0
        ).astype(BF16)


def gather_rows(ids_ref, weight_ref, first_row, rows):
    axial = weight_ref.shape[0] // 6
    count = weight_ref.shape[1]
    hot = jnp.where(iota((rows, count), 0) + first_row == ids_ref[0, 0], 1.0, 0.0).astype(BF16)
    both = lax.dot_general(
        hot, weight_ref[...], (((1,), (1,)), ((), ())), preferred_element_type=F32
    )
    return [
        both[:, c * axial : (c + 1) * axial] + both[:, (3 + c) * axial : (4 + c) * axial]
        for c in range(3)
    ]


def edge_kernel(ids_ref, spring_ref, first_ref, last_ref, low_ref, high_ref, weight_ref, *, radii):
    _, _, _, angles, axial = low_ref.shape
    weigh(ids_ref, spring_ref, weight_ref)
    for field_ref, out_ref, radius in (
        (first_ref, low_ref, 0),
        (last_ref, high_ref, radii - HALO),
    ):
        out_ref[0] = field_ref[...]
        values = gather_rows(ids_ref, weight_ref, radius * angles, HALO * angles)
        for c in range(3):
            out_ref[1, c] = values[c].reshape(HALO, angles, axial)


def middle_kernel(ids_ref, spring_ref, stress_ref, weight_ref):
    step = pl.program_id(0)
    _, radii, angles, axial = stress_ref.shape

    @pl.when(step == 0)
    def _():
        weigh(ids_ref, spring_ref, weight_ref)

    rows = radii * angles
    values = gather_rows(ids_ref, weight_ref, HALO * angles + step * rows, rows)
    for c in range(3):
        stress_ref[c] = values[c].reshape(radii, angles, axial)


def deposit_edges(ids, spring, velocity):
    _, radii, angles, axial = velocity.shape
    count = ids.shape[3]
    edge = (2, 3, HALO, angles, axial)
    edge_block = (3, HALO, angles, axial)
    whole = pl.BlockSpec(memory_space=pltpu.VMEM)
    return pl.pallas_call(
        functools.partial(edge_kernel, radii=radii),
        grid=(1,),
        in_specs=[
            whole,
            whole,
            pl.BlockSpec(edge_block, lambda i: (0, 0, 0, 0)),
            pl.BlockSpec(edge_block, lambda i: (0, radii // HALO - 1, 0, 0)),
        ],
        out_specs=[pl.BlockSpec(edge, lambda i: (0, 0, 0, 0, 0))] * 2,
        out_shape=[pltpu.HBM(edge, F32)] * 2,
        scratch_shapes=[pltpu.VMEM((6 * axial, count), BF16)],
        compiler_params=pltpu.CompilerParams(vmem_limit_bytes=28 * MIB),
        cost_estimate=pl.CostEstimate(
            flops=24 * HALO * angles * count * axial,
            bytes_accessed=96 * HALO * angles * axial,
            transcendentals=0,
        ),
        name="deposit_edges",
    )(ids, spring, in_hbm(velocity), in_hbm(velocity))


def deposit_middle(ids, spring, low_edge, shape):
    _, radii, angles, axial = shape
    count = ids.shape[3]
    inner = radii - 2 * HALO
    part = math.gcd(inner, max(1, 512 // angles))
    whole = pl.BlockSpec(memory_space=pltpu.VMEM)
    return pl.pallas_call(
        lambda ids_ref, spring_ref, _, *refs: middle_kernel(ids_ref, spring_ref, *refs),
        grid=(inner // part,),
        in_specs=[whole, whole, pl.BlockSpec(memory_space=pl.ANY)],
        out_specs=pl.BlockSpec((3, part, angles, axial), lambda i: (0, i, 0, 0)),
        out_shape=pltpu.HBM((3, inner, angles, axial), F32),
        scratch_shapes=[pltpu.VMEM((6 * axial, count), BF16)],
        compiler_params=pltpu.CompilerParams(vmem_limit_bytes=28 * MIB),
        cost_estimate=pl.CostEstimate(
            flops=12 * inner * angles * count * axial,
            bytes_accessed=12 * inner * angles * axial,
            transcendentals=0,
        ),
        name="deposit_middle",
    )(ids, spring, in_hbm(low_edge))


def derivative_matrix(stencil_ref, inverse_ref):
    rows = inverse_ref.shape[1]
    wide = rows + 2 * HALO
    offset = iota((wide, rows), 0) - iota((wide, rows), 1)
    band = jnp.zeros((wide, rows), F32)
    for s in range(2 * HALO + 1):
        band = band + jnp.where(offset == s, stencil_ref[s : s + 1, :], 0.0)
    small = lax.dot_general(
        inverse_ref[...],
        band,
        (((1,), (1,)), ((), ())),
        precision=PRECISE,
        preferred_element_type=F32,
    )
    tall = jnp.where(iota((rows * SUB, rows), 0) // SUB == iota((rows * SUB, rows), 1), 1.0, 0.0)
    flat = jnp.where(iota((wide, wide * SUB), 1) // SUB == iota((wide, wide * SUB), 0), 1.0, 0.0)
    big = (rows * SUB, wide * SUB)
    same = iota(big, 0) % SUB == iota(big, 1) % SUB
    parts = []
    for part in split(small):
        spread = dot(dot(tall.astype(BF16), part).astype(BF16), flat.astype(BF16))
        parts.append(jnp.where(same, spread, 0.0).astype(BF16))
    return jnp.concatenate(parts, axis=0)


def move_kernel(
    stencil_ref,
    inverse_ref,
    low_ref,
    velocity_ref,
    low_edge_ref,
    middle_ref,
    high_edge_ref,
    high_ref,
    ids_ref,
    spring_ref,
    noise_ref,
    moved_ref,
    force_ref,
    grad_ref,
    matrix_ref,
):
    radii, angles, axial = velocity_ref.shape[1:]
    matrix_ref[...] = derivative_matrix(stencil_ref, inverse_ref)
    group = radii * SUB

    def derive(i, carry):
        at = pl.ds(pl.multiple_of(i * SUB, SUB), SUB)
        columns = []
        own = [
            [velocity_ref],
            [low_edge_ref.at[1], middle_ref, high_edge_ref.at[1]],
        ]
        for f in range(2):
            refs = [low_ref.at[f]] + own[f] + [high_ref.at[f]]
            for c in range(3):
                value = jnp.concatenate([ref[c, :, at, :] for ref in refs], axis=0)
                columns.append(value.reshape((radii + 2 * HALO) * SUB, axial))
        field_high, field_low = split(jnp.concatenate(columns, axis=1))
        result = dot3(matrix_ref[...], field_high, field_low)
        for c in range(3):
            force = TIME_STEP * result[:, (3 + c) * axial : (4 + c) * axial]
            force_ref[c, :, at, :] = force.reshape(radii, SUB, axial)
        turned_high, turned_low = split(result[:, : 3 * axial].T)
        cols = pl.ds(pl.multiple_of(i * group, group), group)
        grad_ref[: 3 * axial, cols] = turned_high
        grad_ref[3 * axial :, cols] = turned_low
        return carry

    lax.fori_loop(0, angles // SUB, derive, 0)

    count = spring_ref.shape[3]
    part = min(count, 512)

    def read(i, carry):
        at = pl.ds(pl.multiple_of(i * part, part), part)
        plane = ids_ref[0, 0, :, at]
        radius, angle = plane // angles, plane % angles
        column = (angle // SUB) * group + radius * SUB + angle % SUB
        hot = jnp.where(iota((radii * angles, part), 0) == column, 1.0, 0.0).astype(BF16)
        picked = dot(grad_ref[...], hot)
        here = iota((axial, part), 0) == ids_ref[1, 0, :, at]
        q = [spring_ref[c, 0, :, at] for c in range(3)]
        stretch_sq = q[0] * q[0] + q[1] * q[1] + q[2] * q[2]
        factor = 1.0 / (1.0 - stretch_sq / MAX_STRETCH)
        for c in range(3):
            value = (
                picked[c * axial : (c + 1) * axial] + picked[(3 + c) * axial : (4 + c) * axial]
            )
            shear = jnp.sum(jnp.where(here, value, 0.0), axis=0, keepdims=True)
            moved_ref[c, 0, :, at] = (
                q[c]
                + TIME_STEP * (shear * q[0] - 0.5 * factor * q[c])
                + math.sqrt(TIME_STEP) * noise_ref[c, 0, :, at]
            )
        return carry

    lax.fori_loop(0, count // part, read, 0)


def move(stencil, inverse, low, velocity, stress, high, ids, spring, noise):
    low_edge, middle, high_edge = stress
    radii, angles, axial = velocity.shape[1:]
    whole = pl.BlockSpec(memory_space=pltpu.VMEM)
    return pl.pallas_call(
        move_kernel,
        in_specs=[whole] * 11,
        out_specs=[whole, whole],
        out_shape=[
            jax.ShapeDtypeStruct(spring.shape, F32),
            pltpu.HBM(velocity.shape, F32),
        ],
        scratch_shapes=[
            pltpu.VMEM((6 * axial, radii * angles), BF16),
            pltpu.VMEM((2 * radii * SUB, (radii + 2 * HALO) * SUB), BF16),
        ],
        compiler_params=pltpu.CompilerParams(vmem_limit_bytes=28 * MIB),
        cost_estimate=pl.CostEstimate(
            flops=14 * radii * angles * spring.shape[3] * axial,
            bytes_accessed=40 * radii * angles * axial,
            transcendentals=0,
        ),
        name="move",
    )(
        stencil,
        inverse,
        in_vmem(low),
        in_hbm(velocity),
        in_hbm(low_edge),
        in_hbm(middle),
        in_hbm(high_edge),
        in_vmem(high),
        ids,
        spring,
        noise,
    )


def fourier_tables(all_angles):
    half = all_angles // 2
    row = np.arange(half)
    quarter = half // 2
    waves = [
        np.where(row <= quarter, 2 * row, 2 * (row - quarter)),
        np.where(row < quarter, 2 * row + 1, 2 * (row - quarter) + 1),
    ]
    cosine = [row <= quarter, row < quarter]
    tables = []
    for wave, even in zip(waves, cosine):
        phase = (wave[:, None] * row[None, :]) % all_angles
        angle = phase * (2.0 * math.pi / all_angles)
        table = np.where(even[:, None], np.cos(angle), np.sin(angle))
        weight = np.where((wave == 0) | (wave == half), 1.0, 2.0) / all_angles
        for value in (table, table.T * weight[None, :]):
            value = value.astype(np.float32)
            high = value.astype(BF16)
            low = (value - high.astype(np.float32)).astype(BF16)
            tables.append(np.concatenate([high, low], axis=0))
    return np.stack(tables)


def solve_kernel(coef_ref, first_ref, tables_ref, *refs):
    in_ref, out_ref, table_ref, done_ref, table_sems, out_sems = refs[-6:]
    blocks, rows, angles, axial = in_ref.shape
    half = blocks * angles // 2
    quarter = half // 2
    part = math.gcd(rows, 4)
    loads = [
        pltpu.make_async_copy(tables_ref.at[i], table_ref.at[i], table_sems.at[i])
        for i in range(4)
    ]
    for copy in loads:
        copy.start()

    base = first_ref[0]
    lane = iota((1, axial), 1)
    coef = jnp.zeros((1, axial), F32)
    for q in range(rows):
        coef = jnp.where(lane == q, coef_ref[lax.rem(base + q, coef_ref.shape[0])], coef)
    row = iota((half, axial), 0)
    waves = [
        jnp.where(row <= quarter, 2 * row, 2 * (row - quarter)),
        jnp.where(row < quarter, 2 * row + 1, 2 * (row - quarter) + 1),
    ]
    damping = [1.0 / (1.0 + coef * (wave * wave).astype(F32)) for wave in waves]

    stores = []
    for g in range(rows // part):
        chosen = range(g * part, (g + 1) * part)
        near = [in_ref[: blocks // 2, q].reshape(half, axial) for q in chosen]
        far = [in_ref[blocks // 2 :, q].reshape(half, axial) for q in chosen]
        results = []
        for odd in range(2):
            field = jnp.concatenate([a - b if odd else a + b for a, b in zip(near, far)], axis=1)
            if g == 0:
                loads[2 * odd].wait()
            spectrum = dot3(table_ref[2 * odd], *split(field))
            scale = [
                jnp.broadcast_to(damping[odd][:, q : q + 1], (half, axial)) for q in chosen
            ]
            if g == 0:
                loads[2 * odd + 1].wait()
            damped = spectrum * jnp.concatenate(scale, axis=1)
            results.append(dot3(table_ref[2 * odd + 1], *split(damped)))
        for i, q in enumerate(chosen):
            even, odd = [value[:, i * axial : (i + 1) * axial] for value in results]
            done_ref[: blocks // 2, q] = (even + odd).reshape(blocks // 2, angles, axial)
            done_ref[blocks // 2 :, q] = (even - odd).reshape(blocks // 2, angles, axial)
            stores.append(
                pltpu.make_async_copy(done_ref.at[:, q], out_ref.at[:, q], out_sems.at[q])
            )
            stores[-1].start()
    for copy in stores:
        copy.wait()


def solve(coef, first, field, after):
    blocks, rows, angles, axial = field.shape
    all_angles = blocks * angles
    tables = fourier_tables(all_angles)
    smem = pl.BlockSpec(memory_space=pltpu.SMEM)
    whole = pl.BlockSpec(memory_space=pltpu.VMEM)
    unread = pl.BlockSpec(memory_space=pl.ANY)
    return pl.pallas_call(
        solve_kernel,
        in_specs=[smem, smem, unread] + [unread] * len(after) + [whole],
        out_specs=unread,
        out_shape=pltpu.HBM(field.shape, F32),
        scratch_shapes=[
            pltpu.VMEM(tables.shape, BF16),
            pltpu.VMEM(field.shape, F32),
            pltpu.SemaphoreType.DMA((4,)),
            pltpu.SemaphoreType.DMA((rows,)),
        ],
        compiler_params=pltpu.CompilerParams(vmem_limit_bytes=28 * MIB),
        cost_estimate=pl.CostEstimate(
            flops=12 * all_angles * all_angles * rows * axial,
            bytes_accessed=8 * all_angles * rows * axial,
            transcendentals=0,
        ),
        name="solve",
    )(
        coef,
        first,
        in_hbm(jnp.asarray(tables)),
        *after,
        in_vmem(field),
    )


def join_kernel(force_ref, smooth_ref, out_ref, sum_ref, in_sems, out_sems):
    parts = in_sems.shape[0]
    part = sum_ref.shape[0] // parts
    spans = [pl.ds(i * part, part) for i in range(parts)]
    reads = [
        pltpu.make_async_copy(force_ref.at[at], sum_ref.at[at], in_sems.at[i])
        for i, at in enumerate(spans)
    ]
    writes = [
        pltpu.make_async_copy(sum_ref.at[at], out_ref.at[at], out_sems.at[i])
        for i, at in enumerate(spans)
    ]
    for copy in reads:
        copy.start()
    for i, at in enumerate(spans):
        reads[i].wait()
        sum_ref[at] = sum_ref[at] + smooth_ref[at]
        writes[i].start()
    for copy in writes:
        copy.wait()


def join(force, smooth):
    whole = pl.BlockSpec(memory_space=pltpu.VMEM)
    return pl.pallas_call(
        join_kernel,
        in_specs=[pl.BlockSpec(memory_space=pl.ANY), whole],
        out_specs=pl.BlockSpec(memory_space=pl.ANY),
        out_shape=pltpu.HBM(force.shape, F32),
        scratch_shapes=[
            pltpu.VMEM(force.shape, F32),
            pltpu.SemaphoreType.DMA((math.gcd(force.shape[0], 16),)),
            pltpu.SemaphoreType.DMA((math.gcd(force.shape[0], 16),)),
        ],
        compiler_params=pltpu.CompilerParams(vmem_limit_bytes=14 * MIB),
        cost_estimate=pl.CostEstimate(
            flops=force.size, bytes_accessed=12 * force.size, transcendentals=0
        ),
        name="join",
    )(in_hbm(force), in_vmem(smooth))


def from_neighbours(low_edge, high_edge):
    count = lax.axis_size("rad")
    forward = [(i, i + 1) for i in range(count - 1)]
    backward = [(target, source) for source, target in forward]
    low = lax.ppermute(high_edge, "rad", forward)
    high = lax.ppermute(low_edge, "rad", backward)
    return low, high


def per_device(velocity, dumbbells, cell_ids, brownian, stencil_coef, block_inverse, azim_coef):
    _, radii, angles, axial = velocity.shape
    az = lax.axis_size("az")
    rows = 3 * radii // az
    pieces = velocity.reshape(az, rows, angles, axial)
    gathered = lax.all_to_all(pieces, "az", 0, 0, tiled=True)
    low_edge, high_edge = deposit_edges(cell_ids, dumbbells, velocity)
    low, high = from_neighbours(low_edge, high_edge)
    middle = deposit_middle(cell_ids, dumbbells, low_edge, velocity.shape)
    stress = (low_edge, middle, high_edge)
    first = (lax.axis_index("az") * rows).astype(jnp.int32).reshape(1)
    solved = solve(azim_coef, first, gathered, (in_vmem(low), in_vmem(high), in_hbm(middle)))
    smooth = lax.all_to_all(solved, "az", 0, 0, tiled=True)
    moved, force = move(
        stencil_coef, block_inverse, low, velocity, stress, high, cell_ids, dumbbells, brownian
    )
    lines = (3 * radii, angles, axial)
    result = join(force.reshape(lines), smooth.reshape(lines))
    return result.reshape(velocity.shape), moved


def solution(mesh):
    placed = (
        P(None, "rad", "az", None),
        P(None, "rad", "az", None),
        P(None, "rad", "az", None),
        P(None, "rad", "az", None),
        P(None, "rad"),
        P("rad", None),
        P("rad"),
    )
    return jax.shard_map(
        per_device,
        mesh=mesh,
        in_specs=placed,
        out_specs=(P(None, "rad", "az", None), P(None, "rad", "az", None)),
        check_vma=False,
    )
```

```python
import functools
import functools
import math

import jax
import jax.numpy as jnp
import numpy as np
from jax import lax
from jax.experimental import pallas as pl
from jax.experimental.pallas import tpu as pltpu
from jax.sharding import PartitionSpec as P

TIME_STEP = 0.05
MAX_STRETCH = 10.0
STRESS_SCALE = 4.0
PRECISE = lax.Precision.HIGHEST
HALO = 4
SUB = 8
MIB = 1024 * 1024
F32 = jnp.float32
BF16 = jnp.bfloat16


def split(value):
    high = value.astype(BF16)
    return high, (value - high.astype(F32)).astype(BF16)


def dot(a, b):
    return jnp.dot(a, b, preferred_element_type=F32)


def dot3(stacked, b_high, b_low):
    rows = stacked.shape[0] // 2
    both = dot(stacked, b_high)
    return both[:rows] + both[rows:] + dot(stacked[:rows], b_low)

def in_hbm(value):
    return pltpu.with_memory_space_constraint(value, pltpu.HBM)


def in_vmem(value):
    return pltpu.with_memory_space_constraint(value, pltpu.VMEM)


def iota(shape, dim):
    return lax.broadcasted_iota(jnp.int32, shape, dim)


def weigh(ids_ref, spring_ref, weight_ref):
    axial = weight_ref.shape[0] // 6
    count = weight_ref.shape[1]
    q = [spring_ref[c, 0] for c in range(3)]
    stretch_sq = q[0] * q[0] + q[1] * q[1] + q[2] * q[2]
    factor = 1.0 / (1.0 - stretch_sq / MAX_STRETCH)
    here = iota((axial, count), 0) == ids_ref[1, 0]
    for c in range(3):
        weight = STRESS_SCALE * factor * q[0] * q[c]
        high = weight.astype(BF16).astype(F32)
        weight_ref[c * axial : (c + 1) * axial, :] = jnp.where(here, high, 0.0).astype(BF16)
        weight_ref[(3 + c) * axial : (4 + c) * axial, :] = jnp.where(
            here, weight - high, 0.0
        ).astype(BF16)


def gather_rows(ids_ref, weight_ref, first_row, rows):
    axial = weight_ref.shape[0] // 6
    count = weight_ref.shape[1]
    hot = jnp.where(iota((rows, count), 0) + first_row == ids_ref[0, 0], 1.0, 0.0).astype(BF16)
    both = lax.dot_general(
        hot, weight_ref[...], (((1,), (1,)), ((), ())), preferred_element_type=F32
    )
    return [
        both[:, c * axial : (c + 1) * axial] + both[:, (3 + c) * axial : (4 + c) * axial]
        for c in range(3)
    ]


def edge_kernel(ids_ref, spring_ref, first_ref, last_ref, low_ref, high_ref, weight_ref, *, radii):
    _, _, _, angles, axial = low_ref.shape
    weigh(ids_ref, spring_ref, weight_ref)
    for field_ref, out_ref, radius in (
        (first_ref, low_ref, 0),
        (last_ref, high_ref, radii - HALO),
    ):
        out_ref[0] = field_ref[...]
        values = gather_rows(ids_ref, weight_ref, radius * angles, HALO * angles)
        for c in range(3):
            out_ref[1, c] = values[c].reshape(HALO, angles, axial)


def middle_kernel(ids_ref, spring_ref, stress_ref, weight_ref):
    step = pl.program_id(0)
    _, radii, angles, axial = stress_ref.shape

    @pl.when(step == 0)
    def _():
        weigh(ids_ref, spring_ref, weight_ref)

    rows = radii * angles
    values = gather_rows(ids_ref, weight_ref, HALO * angles + step * rows, rows)
    for c in range(3):
        stress_ref[c] = values[c].reshape(radii, angles, axial)


def deposit_edges(ids, spring, velocity):
    _, radii, angles, axial = velocity.shape
    count = ids.shape[3]
    edge = (2, 3, HALO, angles, axial)
    edge_block = (3, HALO, angles, axial)
    whole = pl.BlockSpec(memory_space=pltpu.VMEM)
    return pl.pallas_call(
        functools.partial(edge_kernel, radii=radii),
        grid=(1,),
        in_specs=[
            whole,
            whole,
            pl.BlockSpec(edge_block, lambda i: (0, 0, 0, 0)),
            pl.BlockSpec(edge_block, lambda i: (0, radii // HALO - 1, 0, 0)),
        ],
        out_specs=[pl.BlockSpec(edge, lambda i: (0, 0, 0, 0, 0))] * 2,
        out_shape=[pltpu.HBM(edge, F32)] * 2,
        scratch_shapes=[pltpu.VMEM((6 * axial, count), BF16)],
        compiler_params=pltpu.CompilerParams(vmem_limit_bytes=28 * MIB),
        cost_estimate=pl.CostEstimate(
            flops=24 * HALO * angles * count * axial,
            bytes_accessed=96 * HALO * angles * axial,
            transcendentals=0,
        ),
        name="deposit_edges",
    )(ids, spring, in_hbm(velocity), in_hbm(velocity))


def deposit_middle(ids, spring, low_edge, shape):
    _, radii, angles, axial = shape
    count = ids.shape[3]
    inner = radii - 2 * HALO
    part = math.gcd(inner, max(1, 512 // angles))
    whole = pl.BlockSpec(memory_space=pltpu.VMEM)
    return pl.pallas_call(
        lambda ids_ref, spring_ref, _, *refs: middle_kernel(ids_ref, spring_ref, *refs),
        grid=(inner // part,),
        in_specs=[whole, whole, pl.BlockSpec(memory_space=pl.ANY)],
        out_specs=pl.BlockSpec((3, part, angles, axial), lambda i: (0, i, 0, 0)),
        out_shape=pltpu.HBM((3, inner, angles, axial), F32),
        scratch_shapes=[pltpu.VMEM((6 * axial, count), BF16)],
        compiler_params=pltpu.CompilerParams(vmem_limit_bytes=28 * MIB),
        cost_estimate=pl.CostEstimate(
            flops=12 * inner * angles * count * axial,
            bytes_accessed=12 * inner * angles * axial,
            transcendentals=0,
        ),
        name="deposit_middle",
    )(ids, spring, in_hbm(low_edge))


def derivative_matrix(stencil_ref, inverse_ref):
    rows = inverse_ref.shape[1]
    wide = rows + 2 * HALO
    offset = iota((wide, rows), 0) - iota((wide, rows), 1)
    band = jnp.zeros((wide, rows), F32)
    for s in range(2 * HALO + 1):
        band = band + jnp.where(offset == s, stencil_ref[s : s + 1, :], 0.0)
    small = lax.dot_general(
        inverse_ref[...],
        band,
        (((1,), (1,)), ((), ())),
        precision=PRECISE,
        preferred_element_type=F32,
    )
    tall = jnp.where(iota((rows * SUB, rows), 0) // SUB == iota((rows * SUB, rows), 1), 1.0, 0.0)
    flat = jnp.where(iota((wide, wide * SUB), 1) // SUB == iota((wide, wide * SUB), 0), 1.0, 0.0)
    big = (rows * SUB, wide * SUB)
    same = iota(big, 0) % SUB == iota(big, 1) % SUB
    parts = []
    for part in split(small):
        spread = dot(dot(tall.astype(BF16), part).astype(BF16), flat.astype(BF16))
        parts.append(jnp.where(same, spread, 0.0).astype(BF16))
    return jnp.concatenate(parts, axis=0)


def move_kernel(
    stencil_ref,
    inverse_ref,
    low_ref,
    velocity_ref,
    low_edge_ref,
    middle_ref,
    high_edge_ref,
    high_ref,
    ids_ref,
    spring_ref,
    noise_ref,
    moved_ref,
    force_ref,
    grad_ref,
    matrix_ref,
):
    radii, angles, axial = velocity_ref.shape[1:]
    matrix_ref[...] = derivative_matrix(stencil_ref, inverse_ref)
    group = radii * SUB

    def derive(i, carry):
        at = pl.ds(pl.multiple_of(i * SUB, SUB), SUB)
        columns = []
        own = [
            [velocity_ref],
            [low_edge_ref.at[1], middle_ref, high_edge_ref.at[1]],
        ]
        for f in range(2):
            refs = [low_ref.at[f]] + own[f] + [high_ref.at[f]]
            for c in range(3):
                value = jnp.concatenate([ref[c, :, at, :] for ref in refs], axis=0)
                columns.append(value.reshape((radii + 2 * HALO) * SUB, axial))
        field_high, field_low = split(jnp.concatenate(columns, axis=1))
        result = dot3(matrix_ref[...], field_high, field_low)
        for c in range(3):
            force = TIME_STEP * result[:, (3 + c) * axial : (4 + c) * axial]
            force_ref[c, :, at, :] = force.reshape(radii, SUB, axial)
        turned_high, turned_low = split(result[:, : 3 * axial].T)
        cols = pl.ds(pl.multiple_of(i * group, group), group)
        grad_ref[: 3 * axial, cols] = turned_high
        grad_ref[3 * axial :, cols] = turned_low
        return carry

    lax.fori_loop(0, angles // SUB, derive, 0)

    count = spring_ref.shape[3]
    part = min(count, 512)

    def read(i, carry):
        at = pl.ds(pl.multiple_of(i * part, part), part)
        plane = ids_ref[0, 0, :, at]
        radius, angle = plane // angles, plane % angles
        column = (angle // SUB) * group + radius * SUB + angle % SUB
        hot = jnp.where(iota((radii * angles, part), 0) == column, 1.0, 0.0).astype(BF16)
        picked = dot(grad_ref[...], hot)
        here = iota((axial, part), 0) == ids_ref[1, 0, :, at]
        q = [spring_ref[c, 0, :, at] for c in range(3)]
        stretch_sq = q[0] * q[0] + q[1] * q[1] + q[2] * q[2]
        factor = 1.0 / (1.0 - stretch_sq / MAX_STRETCH)
        for c in range(3):
            value = (
                picked[c * axial : (c + 1) * axial] + picked[(3 + c) * axial : (4 + c) * axial]
            )
            shear = jnp.sum(jnp.where(here, value, 0.0), axis=0, keepdims=True)
            moved_ref[c, 0, :, at] = (
                q[c]
                + TIME_STEP * (shear * q[0] - 0.5 * factor * q[c])
                + math.sqrt(TIME_STEP) * noise_ref[c, 0, :, at]
            )
        return carry

    lax.fori_loop(0, count // part, read, 0)


def move(stencil, inverse, low, velocity, stress, high, ids, spring, noise):
    low_edge, middle, high_edge = stress
    radii, angles, axial = velocity.shape[1:]
    whole = pl.BlockSpec(memory_space=pltpu.VMEM)
    return pl.pallas_call(
        move_kernel,
        in_specs=[whole] * 11,
        out_specs=[whole, whole],
        out_shape=[
            jax.ShapeDtypeStruct(spring.shape, F32),
            pltpu.HBM(velocity.shape, F32),
        ],
        scratch_shapes=[
            pltpu.VMEM((6 * axial, radii * angles), BF16),
            pltpu.VMEM((2 * radii * SUB, (radii + 2 * HALO) * SUB), BF16),
        ],
        compiler_params=pltpu.CompilerParams(vmem_limit_bytes=28 * MIB),
        cost_estimate=pl.CostEstimate(
            flops=14 * radii * angles * spring.shape[3] * axial,
            bytes_accessed=40 * radii * angles * axial,
            transcendentals=0,
        ),
        name="move",
    )(
        stencil,
        inverse,
        in_vmem(low),
        in_hbm(velocity),
        in_hbm(low_edge),
        in_hbm(middle),
        in_hbm(high_edge),
        in_vmem(high),
        ids,
        spring,
        noise,
    )


def fourier_tables(all_angles):
    half = all_angles // 2
    row = np.arange(half)
    quarter = half // 2
    waves = [
        np.where(row <= quarter, 2 * row, 2 * (row - quarter)),
        np.where(row < quarter, 2 * row + 1, 2 * (row - quarter) + 1),
    ]
    cosine = [row <= quarter, row < quarter]
    tables = []
    for wave, even in zip(waves, cosine):
        phase = (wave[:, None] * row[None, :]) % all_angles
        angle = phase * (2.0 * math.pi / all_angles)
        table = np.where(even[:, None], np.cos(angle), np.sin(angle))
        weight = np.where((wave == 0) | (wave == half), 1.0, 2.0) / all_angles
        for value in (table, table.T * weight[None, :]):
            value = value.astype(np.float32)
            high = value.astype(BF16)
            low = (value - high.astype(np.float32)).astype(BF16)
            tables.append(np.concatenate([high, low], axis=0))
    return np.stack(tables)


def solve_kernel(coef_ref, me_ref, tables_ref, *refs, extra):
    in_ref, refs = refs[extra], refs[extra + 1 :]
    blocks, rows, angles, axial = in_ref.shape
    out_refs = refs[:blocks]
    table_ref, done_ref, table_sems, out_sems = refs[blocks:]
    half = blocks * angles // 2
    quarter = half // 2
    part = math.gcd(rows, 4)
    loads = [
        pltpu.make_async_copy(tables_ref.at[i], table_ref.at[i], table_sems.at[i])
        for i in range(4)
    ]
    for copy in loads:
        copy.start()

    base = me_ref[0] * rows
    lane = iota((1, axial), 1)
    coef = jnp.zeros((1, axial), F32)
    for q in range(rows):
        coef = jnp.where(lane == q, coef_ref[lax.rem(base + q, coef_ref.shape[0])], coef)
    row = iota((half, axial), 0)
    waves = [
        jnp.where(row <= quarter, 2 * row, 2 * (row - quarter)),
        jnp.where(row < quarter, 2 * row + 1, 2 * (row - quarter) + 1),
    ]
    damping = [1.0 / (1.0 + coef * (wave * wave).astype(F32)) for wave in waves]

    stores = []
    for g in range(rows // part):
        chosen = range(g * part, (g + 1) * part)
        near = [in_ref[: blocks // 2, q].reshape(half, axial) for q in chosen]
        far = [in_ref[blocks // 2 :, q].reshape(half, axial) for q in chosen]
        results = []
        for odd in range(2):
            field = jnp.concatenate([a - b if odd else a + b for a, b in zip(near, far)], axis=1)
            if g == 0:
                loads[2 * odd].wait()
            spectrum = dot3(table_ref[2 * odd], *split(field))
            scale = [
                jnp.broadcast_to(damping[odd][:, q : q + 1], (half, axial)) for q in chosen
            ]
            if g == 0:
                loads[2 * odd + 1].wait()
            damped = spectrum * jnp.concatenate(scale, axis=1)
            results.append(dot3(table_ref[2 * odd + 1], *split(damped)))
        for i, q in enumerate(chosen):
            even, odd = [value[:, i * axial : (i + 1) * axial] for value in results]
            done_ref[: blocks // 2, q] = (even + odd).reshape(blocks // 2, angles, axial)
            done_ref[blocks // 2 :, q] = (even - odd).reshape(blocks // 2, angles, axial)
        at = pl.ds(g * part, part)
        for s in range(blocks):
            stores.append(
                pltpu.make_async_copy(
                    done_ref.at[me_ref[0] ^ s, at], out_refs[s].at[at], out_sems.at[g, s]
                )
            )
            stores[-1].start()
    for copy in stores:
        copy.wait()


def solve(coef, me, field, after):
    blocks, rows, angles, axial = field.shape
    all_angles = blocks * angles
    tables = fourier_tables(all_angles)
    smem = pl.BlockSpec(memory_space=pltpu.SMEM)
    whole = pl.BlockSpec(memory_space=pltpu.VMEM)
    unread = pl.BlockSpec(memory_space=pl.ANY)
    return pl.pallas_call(
        functools.partial(solve_kernel, extra=len(after)),
        in_specs=[smem, smem, unread] + [unread] * len(after) + [whole],
        out_specs=[unread] * blocks,
        out_shape=[pltpu.HBM(field.shape[1:], F32)] * blocks,
        scratch_shapes=[
            pltpu.VMEM(tables.shape, BF16),
            pltpu.VMEM(field.shape, F32),
            pltpu.SemaphoreType.DMA((4,)),
            pltpu.SemaphoreType.DMA((rows // math.gcd(rows, 4), blocks)),
        ],
        compiler_params=pltpu.CompilerParams(vmem_limit_bytes=28 * MIB),
        cost_estimate=pl.CostEstimate(
            flops=12 * all_angles * all_angles * rows * axial,
            bytes_accessed=8 * all_angles * rows * axial,
            transcendentals=0,
        ),
        name="solve",
    )(
        coef,
        me,
        in_hbm(jnp.asarray(tables)),
        *after,
        in_vmem(field),
    )


def join_kernel(me_ref, force_ref, own_ref, *refs):
    count = len(refs) - 4
    piece_refs, (out_ref, sum_ref, in_sems, out_sems) = refs[:count], refs[count:]
    blocks, rows = sum_ref.shape[0] - 1, sum_ref.shape[1]
    me = me_ref[0]
    reads, writes = [], []
    for s in range(blocks):
        at = pl.ds((me ^ s) * rows, rows)
        reads.append(
            pltpu.make_async_copy(force_ref.at[at], sum_ref.at[s], in_sems.at[s])
        )
        writes.append(
            pltpu.make_async_copy(sum_ref.at[s], out_ref.at[at], out_sems.at[s])
        )
    own = pltpu.make_async_copy(own_ref, sum_ref.at[blocks], in_sems.at[blocks])
    own.start()
    for copy in reads:
        copy.start()
    own.wait()
    for s in range(blocks):
        reads[s].wait()
        piece = sum_ref[blocks] if s == 0 else piece_refs[s - 1][...]
        sum_ref[s] = sum_ref[s] + piece
        writes[s].start()
    for copy in writes:
        copy.wait()


def join(me, force, pieces):
    rows, angles, axial = pieces[0].shape
    blocks = len(pieces)
    whole = pl.BlockSpec(memory_space=pltpu.VMEM)
    away = pl.BlockSpec(memory_space=pl.ANY)
    return pl.pallas_call(
        join_kernel,
        in_specs=[pl.BlockSpec(memory_space=pltpu.SMEM), away, away] + [whole] * (blocks - 1),
        out_specs=away,
        out_shape=pltpu.HBM(force.shape, F32),
        scratch_shapes=[
            pltpu.VMEM((blocks + 1, rows, angles, axial), F32),
            pltpu.SemaphoreType.DMA((blocks + 1,)),
            pltpu.SemaphoreType.DMA((blocks,)),
        ],
        compiler_params=pltpu.CompilerParams(vmem_limit_bytes=14 * MIB),
        cost_estimate=pl.CostEstimate(
            flops=force.size, bytes_accessed=12 * force.size, transcendentals=0
        ),
        name="join",
    )(me, in_hbm(force), in_hbm(pieces[0]), *[in_vmem(piece) for piece in pieces[1:]])


def exchange(pieces):
    count = len(pieces)
    received = [pieces[0]] + [None] * (count - 1)
    order = list(range(2, count, 2)) + list(range(3, count, 2)) + [1]
    for s in order:
        received[s] = lax.ppermute(pieces[s], "az", [(i, i ^ s) for i in range(count)])
    return received


def from_neighbours(low_edge, high_edge):
    count = lax.axis_size("rad")
    forward = [(i, i + 1) for i in range(count - 1)]
    backward = [(target, source) for source, target in forward]
    low = lax.ppermute(high_edge, "rad", forward)
    high = lax.ppermute(low_edge, "rad", backward)
    return low, high


def per_device(velocity, dumbbells, cell_ids, brownian, stencil_coef, block_inverse, azim_coef):
    _, radii, angles, axial = velocity.shape
    az = lax.axis_size("az")
    rows = 3 * radii // az
    pieces = velocity.reshape(az, rows, angles, axial)
    gathered = lax.all_to_all(pieces, "az", 0, 0, tiled=True)
    low_edge, high_edge = deposit_edges(cell_ids, dumbbells, velocity)
    low, high = from_neighbours(low_edge, high_edge)
    middle = deposit_middle(cell_ids, dumbbells, low_edge, velocity.shape)
    stress = (low_edge, middle, high_edge)
    me = lax.axis_index("az").astype(jnp.int32).reshape(1)
    solved = solve(azim_coef, me, gathered, (in_vmem(low), in_vmem(high), in_hbm(middle)))
    pieces = exchange(solved)
    moved, force = move(
        stencil_coef, block_inverse, low, velocity, stress, high, cell_ids, dumbbells, brownian
    )
    lines = (3 * radii, angles, axial)
    result = join(me, force.reshape(lines), pieces)
    return result.reshape(velocity.shape), moved


def solution(mesh):
    placed = (
        P(None, "rad", "az", None),
        P(None, "rad", "az", None),
        P(None, "rad", "az", None),
        P(None, "rad", "az", None),
        P(None, "rad"),
        P("rad", None),
        P("rad"),
    )
    return jax.shard_map(
        per_device,
        mesh=mesh,
        in_specs=placed,
        out_specs=(P(None, "rad", "az", None), P(None, "rad", "az", None)),
        check_vma=False,
    )
```

```python
import functools
import functools
import math

import jax
import jax.numpy as jnp
import numpy as np
from jax import lax
from jax.experimental import pallas as pl
from jax.experimental.pallas import tpu as pltpu
from jax.sharding import PartitionSpec as P

TIME_STEP = 0.05
MAX_STRETCH = 10.0
STRESS_SCALE = 4.0
PRECISE = lax.Precision.HIGHEST
HALO = 4
SUB = 8
MIB = 1024 * 1024
F32 = jnp.float32
BF16 = jnp.bfloat16


def split(value):
    high = value.astype(BF16)
    return high, (value - high.astype(F32)).astype(BF16)


def dot(a, b):
    return jnp.dot(a, b, preferred_element_type=F32)


def dot3(stacked, b_high, b_low):
    rows = stacked.shape[0] // 2
    both = dot(stacked, b_high)
    return both[:rows] + both[rows:] + dot(stacked[:rows], b_low)

def in_hbm(value):
    return pltpu.with_memory_space_constraint(value, pltpu.HBM)


def in_vmem(value):
    return pltpu.with_memory_space_constraint(value, pltpu.VMEM)


def iota(shape, dim):
    return lax.broadcasted_iota(jnp.int32, shape, dim)


def weigh(ids_ref, spring_ref, weight_ref):
    axial = weight_ref.shape[0] // 6
    count = weight_ref.shape[1]
    q = [spring_ref[c, 0] for c in range(3)]
    stretch_sq = q[0] * q[0] + q[1] * q[1] + q[2] * q[2]
    factor = 1.0 / (1.0 - stretch_sq / MAX_STRETCH)
    here = iota((axial, count), 0) == ids_ref[1, 0]
    for c in range(3):
        weight = STRESS_SCALE * factor * q[0] * q[c]
        high = weight.astype(BF16).astype(F32)
        weight_ref[c * axial : (c + 1) * axial, :] = jnp.where(here, high, 0.0).astype(BF16)
        weight_ref[(3 + c) * axial : (4 + c) * axial, :] = jnp.where(
            here, weight - high, 0.0
        ).astype(BF16)


def gather_rows(ids_ref, weight_ref, first_row, rows):
    axial = weight_ref.shape[0] // 6
    count = weight_ref.shape[1]
    hot = jnp.where(iota((rows, count), 0) + first_row == ids_ref[0, 0], 1.0, 0.0).astype(BF16)
    both = lax.dot_general(
        hot, weight_ref[...], (((1,), (1,)), ((), ())), preferred_element_type=F32
    )
    return [
        both[:, c * axial : (c + 1) * axial] + both[:, (3 + c) * axial : (4 + c) * axial]
        for c in range(3)
    ]


def edge_kernel(ids_ref, spring_ref, first_ref, last_ref, low_ref, high_ref, weight_ref, *, radii):
    _, _, _, angles, axial = low_ref.shape
    weigh(ids_ref, spring_ref, weight_ref)
    for field_ref, out_ref, radius in (
        (first_ref, low_ref, 0),
        (last_ref, high_ref, radii - HALO),
    ):
        out_ref[0] = field_ref[...]
        values = gather_rows(ids_ref, weight_ref, radius * angles, HALO * angles)
        for c in range(3):
            out_ref[1, c] = values[c].reshape(HALO, angles, axial)


def middle_kernel(ids_ref, spring_ref, stress_ref, weight_ref):
    step = pl.program_id(0)
    _, radii, angles, axial = stress_ref.shape

    @pl.when(step == 0)
    def _():
        weigh(ids_ref, spring_ref, weight_ref)

    rows = radii * angles
    values = gather_rows(ids_ref, weight_ref, HALO * angles + step * rows, rows)
    for c in range(3):
        stress_ref[c] = values[c].reshape(radii, angles, axial)


def deposit_edges(ids, spring, velocity):
    _, radii, angles, axial = velocity.shape
    count = ids.shape[3]
    edge = (2, 3, HALO, angles, axial)
    edge_block = (3, HALO, angles, axial)
    whole = pl.BlockSpec(memory_space=pltpu.VMEM)
    return pl.pallas_call(
        functools.partial(edge_kernel, radii=radii),
        grid=(1,),
        in_specs=[
            whole,
            whole,
            pl.BlockSpec(edge_block, lambda i: (0, 0, 0, 0)),
            pl.BlockSpec(edge_block, lambda i: (0, radii // HALO - 1, 0, 0)),
        ],
        out_specs=[pl.BlockSpec(edge, lambda i: (0, 0, 0, 0, 0))] * 2,
        out_shape=[pltpu.HBM(edge, F32)] * 2,
        scratch_shapes=[pltpu.VMEM((6 * axial, count), BF16)],
        compiler_params=pltpu.CompilerParams(vmem_limit_bytes=28 * MIB),
        cost_estimate=pl.CostEstimate(
            flops=24 * HALO * angles * count * axial,
            bytes_accessed=96 * HALO * angles * axial,
            transcendentals=0,
        ),
        name="deposit_edges",
    )(ids, spring, in_hbm(velocity), in_hbm(velocity))


def deposit_middle(ids, spring, low_edge, shape):
    _, radii, angles, axial = shape
    count = ids.shape[3]
    inner = radii - 2 * HALO
    part = math.gcd(inner, max(1, 512 // angles))
    whole = pl.BlockSpec(memory_space=pltpu.VMEM)
    return pl.pallas_call(
        lambda ids_ref, spring_ref, _, *refs: middle_kernel(ids_ref, spring_ref, *refs),
        grid=(inner // part,),
        in_specs=[whole, whole, pl.BlockSpec(memory_space=pl.ANY)],
        out_specs=pl.BlockSpec((3, part, angles, axial), lambda i: (0, i, 0, 0)),
        out_shape=pltpu.HBM((3, inner, angles, axial), F32),
        scratch_shapes=[pltpu.VMEM((6 * axial, count), BF16)],
        compiler_params=pltpu.CompilerParams(vmem_limit_bytes=28 * MIB),
        cost_estimate=pl.CostEstimate(
            flops=12 * inner * angles * count * axial,
            bytes_accessed=12 * inner * angles * axial,
            transcendentals=0,
        ),
        name="deposit_middle",
    )(ids, spring, in_hbm(low_edge))


def derivative_matrix(stencil_ref, inverse_ref):
    rows = inverse_ref.shape[1]
    wide = rows + 2 * HALO
    offset = iota((wide, rows), 0) - iota((wide, rows), 1)
    band = jnp.zeros((wide, rows), F32)
    for s in range(2 * HALO + 1):
        band = band + jnp.where(offset == s, stencil_ref[s : s + 1, :], 0.0)
    small = lax.dot_general(
        inverse_ref[...],
        band,
        (((1,), (1,)), ((), ())),
        precision=PRECISE,
        preferred_element_type=F32,
    )
    tall = jnp.where(iota((rows * SUB, rows), 0) // SUB == iota((rows * SUB, rows), 1), 1.0, 0.0)
    flat = jnp.where(iota((wide, wide * SUB), 1) // SUB == iota((wide, wide * SUB), 0), 1.0, 0.0)
    big = (rows * SUB, wide * SUB)
    same = iota(big, 0) % SUB == iota(big, 1) % SUB
    parts = []
    for part in split(small):
        spread = dot(dot(tall.astype(BF16), part).astype(BF16), flat.astype(BF16))
        parts.append(jnp.where(same, spread, 0.0).astype(BF16))
    return jnp.concatenate(parts, axis=0)


def derive_kernel(
    stencil_ref,
    inverse_ref,
    low_ref,
    velocity_ref,
    low_edge_ref,
    middle_ref,
    high_edge_ref,
    high_ref,
    grad_ref,
    force_ref,
    matrix_ref,
):
    radii, angles, axial = velocity_ref.shape[1:]
    matrix_ref[...] = derivative_matrix(stencil_ref, inverse_ref)
    group = radii * SUB

    def derive(i, carry):
        at = pl.ds(pl.multiple_of(i * SUB, SUB), SUB)
        columns = []
        own = [
            [velocity_ref],
            [low_edge_ref.at[1], middle_ref, high_edge_ref.at[1]],
        ]
        for f in range(2):
            refs = [low_ref.at[f]] + own[f] + [high_ref.at[f]]
            for c in range(3):
                value = jnp.concatenate([ref[c, :, at, :] for ref in refs], axis=0)
                columns.append(value.reshape((radii + 2 * HALO) * SUB, axial))
        field_high, field_low = split(jnp.concatenate(columns, axis=1))
        result = dot3(matrix_ref[...], field_high, field_low)
        for c in range(3):
            force = TIME_STEP * result[:, (3 + c) * axial : (4 + c) * axial]
            force_ref[c, :, at, :] = force.reshape(radii, SUB, axial)
        turned_high, turned_low = split(result[:, : 3 * axial].T)
        cols = pl.ds(pl.multiple_of(i * group, group), group)
        grad_ref[: 3 * axial, cols] = turned_high
        grad_ref[3 * axial :, cols] = turned_low
        return carry

    lax.fori_loop(0, angles // SUB, derive, 0)


def derive(stencil, inverse, low, velocity, stress, high):
    low_edge, middle, high_edge = stress
    radii, angles, axial = velocity.shape[1:]
    whole = pl.BlockSpec(memory_space=pltpu.VMEM)
    return pl.pallas_call(
        derive_kernel,
        in_specs=[whole] * 8,
        out_specs=[whole, whole],
        out_shape=[
            pltpu.HBM((6 * axial, radii * angles), BF16),
            pltpu.HBM(velocity.shape, F32),
        ],
        scratch_shapes=[pltpu.VMEM((2 * radii * SUB, (radii + 2 * HALO) * SUB), BF16)],
        compiler_params=pltpu.CompilerParams(vmem_limit_bytes=28 * MIB),
        cost_estimate=pl.CostEstimate(
            flops=3600 * radii * radii * angles * axial // 8,
            bytes_accessed=40 * radii * angles * axial,
            transcendentals=0,
        ),
        name="derive",
    )(
        stencil,
        inverse,
        in_vmem(low),
        in_hbm(velocity),
        in_hbm(low_edge),
        in_hbm(middle),
        in_hbm(high_edge),
        in_vmem(high),
    )


def move_kernel(grad_ref, ids_ref, spring_ref, noise_ref, moved_ref, *, angles):
    axial, cells = grad_ref.shape[0] // 6, grad_ref.shape[1]
    group = cells // angles * SUB

    count = spring_ref.shape[3]
    part = min(count, 512)

    def read(i, carry):
        at = pl.ds(pl.multiple_of(i * part, part), part)
        plane = ids_ref[0, 0, :, at]
        radius, angle = plane // angles, plane % angles
        column = (angle // SUB) * group + radius * SUB + angle % SUB
        hot = jnp.where(iota((cells, part), 0) == column, 1.0, 0.0).astype(BF16)
        picked = dot(grad_ref[...], hot)
        here = iota((axial, part), 0) == ids_ref[1, 0, :, at]
        q = [spring_ref[c, 0, :, at] for c in range(3)]
        stretch_sq = q[0] * q[0] + q[1] * q[1] + q[2] * q[2]
        factor = 1.0 / (1.0 - stretch_sq / MAX_STRETCH)
        for c in range(3):
            value = (
                picked[c * axial : (c + 1) * axial] + picked[(3 + c) * axial : (4 + c) * axial]
            )
            shear = jnp.sum(jnp.where(here, value, 0.0), axis=0, keepdims=True)
            moved_ref[c, 0, :, at] = (
                q[c]
                + TIME_STEP * (shear * q[0] - 0.5 * factor * q[c])
                + math.sqrt(TIME_STEP) * noise_ref[c, 0, :, at]
            )
        return carry

    lax.fori_loop(0, count // part, read, 0)


def move(grad, ids, spring, noise, angles):
    cells = grad.shape[1]
    whole = pl.BlockSpec(memory_space=pltpu.VMEM)
    return pl.pallas_call(
        functools.partial(move_kernel, angles=angles),
        in_specs=[whole] * 4,
        out_specs=whole,
        out_shape=jax.ShapeDtypeStruct(spring.shape, F32),
        compiler_params=pltpu.CompilerParams(vmem_limit_bytes=24 * MIB),
        cost_estimate=pl.CostEstimate(
            flops=2 * grad.size * spring.shape[3],
            bytes_accessed=2 * grad.size,
            transcendentals=0,
        ),
        name="move",
    )(in_hbm(grad), ids, spring, noise)


def fourier_tables(all_angles):
    half = all_angles // 2
    row = np.arange(half)
    quarter = half // 2
    waves = [
        np.where(row <= quarter, 2 * row, 2 * (row - quarter)),
        np.where(row < quarter, 2 * row + 1, 2 * (row - quarter) + 1),
    ]
    cosine = [row <= quarter, row < quarter]
    tables = []
    for wave, even in zip(waves, cosine):
        phase = (wave[:, None] * row[None, :]) % all_angles
        angle = phase * (2.0 * math.pi / all_angles)
        table = np.where(even[:, None], np.cos(angle), np.sin(angle))
        weight = np.where((wave == 0) | (wave == half), 1.0, 2.0) / all_angles
        for value in (table, table.T * weight[None, :]):
            value = value.astype(np.float32)
            high = value.astype(BF16)
            low = (value - high.astype(np.float32)).astype(BF16)
            tables.append(np.concatenate([high, low], axis=0))
    return np.stack(tables)


def solve_kernel(coef_ref, me_ref, tables_ref, *refs, extra):
    in_ref, refs = refs[extra], refs[extra + 1 :]
    blocks, rows, angles, axial = in_ref.shape
    out_refs = refs[:blocks]
    table_ref, done_ref, table_sems, out_sems = refs[blocks:]
    half = blocks * angles // 2
    quarter = half // 2
    part = math.gcd(rows, 4)
    loads = [
        pltpu.make_async_copy(tables_ref.at[i], table_ref.at[i], table_sems.at[i])
        for i in range(4)
    ]
    for copy in loads:
        copy.start()

    base = me_ref[0] * rows
    lane = iota((1, axial), 1)
    coef = jnp.zeros((1, axial), F32)
    for q in range(rows):
        coef = jnp.where(lane == q, coef_ref[lax.rem(base + q, coef_ref.shape[0])], coef)
    row = iota((half, axial), 0)
    waves = [
        jnp.where(row <= quarter, 2 * row, 2 * (row - quarter)),
        jnp.where(row < quarter, 2 * row + 1, 2 * (row - quarter) + 1),
    ]
    damping = [1.0 / (1.0 + coef * (wave * wave).astype(F32)) for wave in waves]

    stores = []
    for g in range(rows // part):
        chosen = range(g * part, (g + 1) * part)
        near = [in_ref[: blocks // 2, q].reshape(half, axial) for q in chosen]
        far = [in_ref[blocks // 2 :, q].reshape(half, axial) for q in chosen]
        results = []
        for odd in range(2):
            field = jnp.concatenate([a - b if odd else a + b for a, b in zip(near, far)], axis=1)
            if g == 0:
                loads[2 * odd].wait()
            spectrum = dot3(table_ref[2 * odd], *split(field))
            scale = [
                jnp.broadcast_to(damping[odd][:, q : q + 1], (half, axial)) for q in chosen
            ]
            if g == 0:
                loads[2 * odd + 1].wait()
            damped = spectrum * jnp.concatenate(scale, axis=1)
            results.append(dot3(table_ref[2 * odd + 1], *split(damped)))
        for i, q in enumerate(chosen):
            even, odd = [value[:, i * axial : (i + 1) * axial] for value in results]
            done_ref[: blocks // 2, q] = (even + odd).reshape(blocks // 2, angles, axial)
            done_ref[blocks // 2 :, q] = (even - odd).reshape(blocks // 2, angles, axial)
        at = pl.ds(g * part, part)
        for s in range(blocks):
            stores.append(
                pltpu.make_async_copy(
                    done_ref.at[me_ref[0] ^ s, at], out_refs[s].at[at], out_sems.at[g, s]
                )
            )
            stores[-1].start()
    for copy in stores:
        copy.wait()


def solve(coef, me, field, after):
    blocks, rows, angles, axial = field.shape
    all_angles = blocks * angles
    tables = fourier_tables(all_angles)
    smem = pl.BlockSpec(memory_space=pltpu.SMEM)
    whole = pl.BlockSpec(memory_space=pltpu.VMEM)
    unread = pl.BlockSpec(memory_space=pl.ANY)
    return pl.pallas_call(
        functools.partial(solve_kernel, extra=len(after)),
        in_specs=[smem, smem, unread] + [unread] * len(after) + [whole],
        out_specs=[unread] * blocks,
        out_shape=[pltpu.HBM(field.shape[1:], F32)] * blocks,
        scratch_shapes=[
            pltpu.VMEM(tables.shape, BF16),
            pltpu.VMEM(field.shape, F32),
            pltpu.SemaphoreType.DMA((4,)),
            pltpu.SemaphoreType.DMA((rows // math.gcd(rows, 4), blocks)),
        ],
        compiler_params=pltpu.CompilerParams(vmem_limit_bytes=28 * MIB),
        cost_estimate=pl.CostEstimate(
            flops=12 * all_angles * all_angles * rows * axial,
            bytes_accessed=8 * all_angles * rows * axial,
            transcendentals=0,
        ),
        name="solve",
    )(
        coef,
        me,
        in_hbm(jnp.asarray(tables)),
        *after,
        in_vmem(field),
    )


def join_kernel(me_ref, force_ref, own_ref, *refs):
    count = len(refs) - 4
    piece_refs, (out_ref, sum_ref, in_sems, out_sems) = refs[:count], refs[count:]
    blocks, rows = sum_ref.shape[0] - 1, sum_ref.shape[1]
    me = me_ref[0]
    reads, writes = [], []
    for s in range(blocks):
        at = pl.ds((me ^ s) * rows, rows)
        reads.append(
            pltpu.make_async_copy(force_ref.at[at], sum_ref.at[s], in_sems.at[s])
        )
        writes.append(
            pltpu.make_async_copy(sum_ref.at[s], out_ref.at[at], out_sems.at[s])
        )
    own = pltpu.make_async_copy(own_ref, sum_ref.at[blocks], in_sems.at[blocks])
    own.start()
    for copy in reads:
        copy.start()
    own.wait()
    for s in range(blocks):
        reads[s].wait()
        piece = sum_ref[blocks] if s == 0 else piece_refs[s - 1][...]
        sum_ref[s] = sum_ref[s] + piece
        writes[s].start()
    for copy in writes:
        copy.wait()


def join(me, force, pieces):
    rows, angles, axial = pieces[0].shape
    blocks = len(pieces)
    whole = pl.BlockSpec(memory_space=pltpu.VMEM)
    away = pl.BlockSpec(memory_space=pl.ANY)
    return pl.pallas_call(
        join_kernel,
        in_specs=[pl.BlockSpec(memory_space=pltpu.SMEM), away, away] + [whole] * (blocks - 1),
        out_specs=away,
        out_shape=pltpu.HBM(force.shape, F32),
        scratch_shapes=[
            pltpu.VMEM((blocks + 1, rows, angles, axial), F32),
            pltpu.SemaphoreType.DMA((blocks + 1,)),
            pltpu.SemaphoreType.DMA((blocks,)),
        ],
        compiler_params=pltpu.CompilerParams(vmem_limit_bytes=14 * MIB),
        cost_estimate=pl.CostEstimate(
            flops=force.size, bytes_accessed=12 * force.size, transcendentals=0
        ),
        name="join",
    )(me, in_hbm(force), in_hbm(pieces[0]), *[in_vmem(piece) for piece in pieces[1:]])


def exchange(pieces):
    count = len(pieces)
    received = [pieces[0]] + [None] * (count - 1)
    order = list(range(2, count, 2)) + list(range(3, count, 2)) + [1]
    for s in order:
        received[s] = lax.ppermute(pieces[s], "az", [(i, i ^ s) for i in range(count)])
    return received


def from_neighbours(low_edge, high_edge):
    count = lax.axis_size("rad")
    forward = [(i, i + 1) for i in range(count - 1)]
    backward = [(target, source) for source, target in forward]
    low = lax.ppermute(high_edge, "rad", forward)
    high = lax.ppermute(low_edge, "rad", backward)
    return low, high


def per_device(velocity, dumbbells, cell_ids, brownian, stencil_coef, block_inverse, azim_coef):
    _, radii, angles, axial = velocity.shape
    az = lax.axis_size("az")
    rows = 3 * radii // az
    pieces = velocity.reshape(az, rows, angles, axial)
    gathered = lax.all_to_all(pieces, "az", 0, 0, tiled=True)
    low_edge, high_edge = deposit_edges(cell_ids, dumbbells, velocity)
    low, high = from_neighbours(low_edge, high_edge)
    middle = deposit_middle(cell_ids, dumbbells, low_edge, velocity.shape)
    stress = (low_edge, middle, high_edge)
    grad, force = derive(stencil_coef, block_inverse, low, velocity, stress, high)
    me = lax.axis_index("az").astype(jnp.int32).reshape(1)
    solved = solve(azim_coef, me, gathered, (in_hbm(force),))
    pieces = exchange(solved)
    moved = move(grad, cell_ids, dumbbells, brownian, angles)
    lines = (3 * radii, angles, axial)
    result = join(me, force.reshape(lines), pieces)
    return result.reshape(velocity.shape), moved


def solution(mesh):
    placed = (
        P(None, "rad", "az", None),
        P(None, "rad", "az", None),
        P(None, "rad", "az", None),
        P(None, "rad", "az", None),
        P(None, "rad"),
        P("rad", None),
        P("rad"),
    )
    return jax.shard_map(
        per_device,
        mesh=mesh,
        in_specs=placed,
        out_specs=(P(None, "rad", "az", None), P(None, "rad", "az", None)),
        check_vma=False,
    )
```

```python
import functools
import functools
import math

import jax
import jax.numpy as jnp
import numpy as np
from jax import lax
from jax.experimental import pallas as pl
from jax.experimental.pallas import tpu as pltpu
from jax.sharding import PartitionSpec as P

TIME_STEP = 0.05
MAX_STRETCH = 10.0
STRESS_SCALE = 4.0
PRECISE = lax.Precision.HIGHEST
HALO = 4
SUB = 8
MIB = 1024 * 1024
F32 = jnp.float32
BF16 = jnp.bfloat16


def split(value):
    high = value.astype(BF16)
    return high, (value - high.astype(F32)).astype(BF16)


def dot(a, b):
    return jnp.dot(a, b, preferred_element_type=F32)


def dot3(stacked, b_high, b_low):
    rows = stacked.shape[0] // 2
    both = dot(stacked, b_high)
    return both[:rows] + both[rows:] + dot(stacked[:rows], b_low)

def in_hbm(value):
    return pltpu.with_memory_space_constraint(value, pltpu.HBM)


def in_vmem(value):
    return pltpu.with_memory_space_constraint(value, pltpu.VMEM)


def iota(shape, dim):
    return lax.broadcasted_iota(jnp.int32, shape, dim)


def weigh(ids_ref, spring_ref, weight_ref):
    axial = weight_ref.shape[0] // 6
    count = weight_ref.shape[1]
    q = [spring_ref[c, 0] for c in range(3)]
    stretch_sq = q[0] * q[0] + q[1] * q[1] + q[2] * q[2]
    factor = 1.0 / (1.0 - stretch_sq / MAX_STRETCH)
    here = iota((axial, count), 0) == ids_ref[1, 0]
    for c in range(3):
        weight = STRESS_SCALE * factor * q[0] * q[c]
        high = weight.astype(BF16).astype(F32)
        weight_ref[c * axial : (c + 1) * axial, :] = jnp.where(here, high, 0.0).astype(BF16)
        weight_ref[(3 + c) * axial : (4 + c) * axial, :] = jnp.where(
            here, weight - high, 0.0
        ).astype(BF16)


def gather_rows(ids_ref, weight_ref, first_row, rows):
    axial = weight_ref.shape[0] // 6
    count = weight_ref.shape[1]
    hot = jnp.where(iota((rows, count), 0) + first_row == ids_ref[0, 0], 1.0, 0.0).astype(BF16)
    both = lax.dot_general(
        hot, weight_ref[...], (((1,), (1,)), ((), ())), preferred_element_type=F32
    )
    return [
        both[:, c * axial : (c + 1) * axial] + both[:, (3 + c) * axial : (4 + c) * axial]
        for c in range(3)
    ]


def edge_kernel(ids_ref, spring_ref, first_ref, last_ref, low_ref, high_ref, weight_ref, *, radii):
    _, _, _, angles, axial = low_ref.shape
    weigh(ids_ref, spring_ref, weight_ref)
    for field_ref, out_ref, radius in (
        (first_ref, low_ref, 0),
        (last_ref, high_ref, radii - HALO),
    ):
        out_ref[0] = field_ref[...]
        values = gather_rows(ids_ref, weight_ref, radius * angles, HALO * angles)
        for c in range(3):
            out_ref[1, c] = values[c].reshape(HALO, angles, axial)


def middle_kernel(ids_ref, spring_ref, stress_ref, weight_ref):
    step = pl.program_id(0)
    _, radii, angles, axial = stress_ref.shape

    @pl.when(step == 0)
    def _():
        weigh(ids_ref, spring_ref, weight_ref)

    rows = radii * angles
    values = gather_rows(ids_ref, weight_ref, HALO * angles + step * rows, rows)
    for c in range(3):
        stress_ref[c] = values[c].reshape(radii, angles, axial)


def deposit_edges(ids, spring, velocity):
    _, radii, angles, axial = velocity.shape
    count = ids.shape[3]
    edge = (2, 3, HALO, angles, axial)
    edge_block = (3, HALO, angles, axial)
    whole = pl.BlockSpec(memory_space=pltpu.VMEM)
    return pl.pallas_call(
        functools.partial(edge_kernel, radii=radii),
        grid=(1,),
        in_specs=[
            whole,
            whole,
            pl.BlockSpec(edge_block, lambda i: (0, 0, 0, 0)),
            pl.BlockSpec(edge_block, lambda i: (0, radii // HALO - 1, 0, 0)),
        ],
        out_specs=[pl.BlockSpec(edge, lambda i: (0, 0, 0, 0, 0))] * 2,
        out_shape=[pltpu.HBM(edge, F32)] * 2,
        scratch_shapes=[pltpu.VMEM((6 * axial, count), BF16)],
        compiler_params=pltpu.CompilerParams(vmem_limit_bytes=28 * MIB),
        cost_estimate=pl.CostEstimate(
            flops=24 * HALO * angles * count * axial,
            bytes_accessed=96 * HALO * angles * axial,
            transcendentals=0,
        ),
        name="deposit_edges",
    )(ids, spring, in_hbm(velocity), in_hbm(velocity))


def deposit_middle(ids, spring, low_edge, shape):
    _, radii, angles, axial = shape
    count = ids.shape[3]
    inner = radii - 2 * HALO
    part = math.gcd(inner, max(1, 512 // angles))
    whole = pl.BlockSpec(memory_space=pltpu.VMEM)
    return pl.pallas_call(
        lambda ids_ref, spring_ref, _, *refs: middle_kernel(ids_ref, spring_ref, *refs),
        grid=(inner // part,),
        in_specs=[whole, whole, pl.BlockSpec(memory_space=pl.ANY)],
        out_specs=pl.BlockSpec((3, part, angles, axial), lambda i: (0, i, 0, 0)),
        out_shape=pltpu.HBM((3, inner, angles, axial), F32),
        scratch_shapes=[pltpu.VMEM((6 * axial, count), BF16)],
        compiler_params=pltpu.CompilerParams(vmem_limit_bytes=28 * MIB),
        cost_estimate=pl.CostEstimate(
            flops=12 * inner * angles * count * axial,
            bytes_accessed=12 * inner * angles * axial,
            transcendentals=0,
        ),
        name="deposit_middle",
    )(ids, spring, in_hbm(low_edge))


def derivative_matrix(stencil_ref, inverse_ref):
    rows = inverse_ref.shape[1]
    wide = rows + 2 * HALO
    offset = iota((wide, rows), 0) - iota((wide, rows), 1)
    band = jnp.zeros((wide, rows), F32)
    for s in range(2 * HALO + 1):
        band = band + jnp.where(offset == s, stencil_ref[s : s + 1, :], 0.0)
    small = lax.dot_general(
        inverse_ref[...],
        band,
        (((1,), (1,)), ((), ())),
        precision=PRECISE,
        preferred_element_type=F32,
    )
    tall = jnp.where(iota((rows * SUB, rows), 0) // SUB == iota((rows * SUB, rows), 1), 1.0, 0.0)
    flat = jnp.where(iota((wide, wide * SUB), 1) // SUB == iota((wide, wide * SUB), 0), 1.0, 0.0)
    big = (rows * SUB, wide * SUB)
    same = iota(big, 0) % SUB == iota(big, 1) % SUB
    parts = []
    for part in split(small):
        spread = dot(dot(tall.astype(BF16), part).astype(BF16), flat.astype(BF16))
        parts.append(jnp.where(same, spread, 0.0).astype(BF16))
    return jnp.concatenate(parts, axis=0)


def derive_kernel(
    stencil_ref,
    inverse_ref,
    low_ref,
    velocity_ref,
    low_edge_ref,
    middle_ref,
    high_edge_ref,
    high_ref,
    grad_ref,
    force_ref,
    matrix_ref,
):
    radii, angles, axial = velocity_ref.shape[1:]

    @pl.when(pl.program_id(0) == 0)
    def _():
        matrix_ref[...] = derivative_matrix(stencil_ref, inverse_ref)

    group = radii * SUB

    for i in range(angles // SUB):
        at = pl.ds(i * SUB, SUB)
        columns = []
        own = [
            [velocity_ref],
            [low_edge_ref.at[0], middle_ref, high_edge_ref.at[0]],
        ]
        for f in range(2):
            refs = [low_ref.at[f]] + own[f] + [high_ref.at[f]]
            for c in range(3):
                value = jnp.concatenate([ref[c, :, at, :] for ref in refs], axis=0)
                columns.append(value.reshape((radii + 2 * HALO) * SUB, axial))
        field_high, field_low = split(jnp.concatenate(columns, axis=1))
        result = dot3(matrix_ref[...], field_high, field_low)
        for c in range(3):
            force = TIME_STEP * result[:, (3 + c) * axial : (4 + c) * axial]
            force_ref[c, :, at, :] = force.reshape(radii, SUB, axial)
        turned_high, turned_low = split(result[:, : 3 * axial].T)
        cols = pl.ds(i * group, group)
        grad_ref[: 3 * axial, cols] = turned_high
        grad_ref[3 * axial :, cols] = turned_low


def derive(stencil, inverse, low, velocity, stress, high):
    low_edge, middle, high_edge = stress
    radii, angles, axial = velocity.shape[1:]
    part = 2 * SUB

    def block(count, first=None):
        if first is None:
            return pl.BlockSpec((3, count, part, axial), lambda i: (0, 0, i, 0))
        return pl.BlockSpec((2 - first, 3, count, part, axial), lambda i: (first, 0, 0, i, 0))

    return pl.pallas_call(
        derive_kernel,
        grid=(angles // part,),
        in_specs=[
            pl.BlockSpec(stencil.shape, lambda i: (0, 0)),
            pl.BlockSpec(inverse.shape, lambda i: (0, 0)),
            block(HALO, 0),
            block(radii),
            block(HALO, 1),
            block(radii - 2 * HALO),
            block(HALO, 1),
            block(HALO, 0),
        ],
        out_specs=[
            pl.BlockSpec((6 * axial, radii * part), lambda i: (0, i)),
            block(radii),
        ],
        out_shape=[
            pltpu.HBM((6 * axial, radii * angles), BF16),
            pltpu.HBM(velocity.shape, F32),
        ],
        scratch_shapes=[pltpu.VMEM((2 * radii * SUB, (radii + 2 * HALO) * SUB), BF16)],
        compiler_params=pltpu.CompilerParams(vmem_limit_bytes=28 * MIB),
        cost_estimate=pl.CostEstimate(
            flops=3600 * radii * radii * angles * axial // 8,
            bytes_accessed=40 * radii * angles * axial,
            transcendentals=0,
        ),
        name="derive",
    )(
        stencil,
        inverse,
        in_vmem(low),
        in_hbm(velocity),
        in_hbm(low_edge),
        in_hbm(middle),
        in_hbm(high_edge),
        in_vmem(high),
    )


def move_kernel(grad_ref, ids_ref, spring_ref, noise_ref, moved_ref, *, angles):
    axial, cells = grad_ref.shape[0] // 6, grad_ref.shape[1]
    group = cells // angles * SUB

    count = spring_ref.shape[3]
    part = min(count, 512)

    def read(i, carry):
        at = pl.ds(pl.multiple_of(i * part, part), part)
        plane = ids_ref[0, 0, :, at]
        radius, angle = plane // angles, plane % angles
        column = (angle // SUB) * group + radius * SUB + angle % SUB
        hot = jnp.where(iota((cells, part), 0) == column, 1.0, 0.0).astype(BF16)
        picked = dot(grad_ref[...], hot)
        here = iota((axial, part), 0) == ids_ref[1, 0, :, at]
        q = [spring_ref[c, 0, :, at] for c in range(3)]
        stretch_sq = q[0] * q[0] + q[1] * q[1] + q[2] * q[2]
        factor = 1.0 / (1.0 - stretch_sq / MAX_STRETCH)
        for c in range(3):
            value = (
                picked[c * axial : (c + 1) * axial] + picked[(3 + c) * axial : (4 + c) * axial]
            )
            shear = jnp.sum(jnp.where(here, value, 0.0), axis=0, keepdims=True)
            moved_ref[c, 0, :, at] = (
                q[c]
                + TIME_STEP * (shear * q[0] - 0.5 * factor * q[c])
                + math.sqrt(TIME_STEP) * noise_ref[c, 0, :, at]
            )
        return carry

    lax.fori_loop(0, count // part, read, 0)


def move(grad, ids, spring, noise, angles):
    cells = grad.shape[1]
    whole = pl.BlockSpec(memory_space=pltpu.VMEM)
    return pl.pallas_call(
        functools.partial(move_kernel, angles=angles),
        in_specs=[whole] * 4,
        out_specs=whole,
        out_shape=jax.ShapeDtypeStruct(spring.shape, F32),
        compiler_params=pltpu.CompilerParams(vmem_limit_bytes=24 * MIB),
        cost_estimate=pl.CostEstimate(
            flops=2 * grad.size * spring.shape[3],
            bytes_accessed=2 * grad.size,
            transcendentals=0,
        ),
        name="move",
    )(in_hbm(grad), ids, spring, noise)


def fourier_tables(all_angles):
    half = all_angles // 2
    row = np.arange(half)
    quarter = half // 2
    waves = [
        np.where(row <= quarter, 2 * row, 2 * (row - quarter)),
        np.where(row < quarter, 2 * row + 1, 2 * (row - quarter) + 1),
    ]
    cosine = [row <= quarter, row < quarter]
    tables = []
    for wave, even in zip(waves, cosine):
        phase = (wave[:, None] * row[None, :]) % all_angles
        angle = phase * (2.0 * math.pi / all_angles)
        table = np.where(even[:, None], np.cos(angle), np.sin(angle))
        weight = np.where((wave == 0) | (wave == half), 1.0, 2.0) / all_angles
        for value in (table, table.T * weight[None, :]):
            value = value.astype(np.float32)
            high = value.astype(BF16)
            low = (value - high.astype(np.float32)).astype(BF16)
            tables.append(np.concatenate([high, low], axis=0))
    return np.stack(tables)


def solve_kernel(coef_ref, me_ref, tables_ref, *refs, extra):
    in_ref, refs = refs[extra], refs[extra + 1 :]
    blocks, rows, angles, axial = in_ref.shape
    out_refs = refs[:blocks]
    table_ref, done_ref, table_sems, out_sems = refs[blocks:]
    half = blocks * angles // 2
    quarter = half // 2
    part = math.gcd(rows, 2)
    loads = [
        pltpu.make_async_copy(tables_ref.at[i], table_ref.at[i], table_sems.at[i])
        for i in range(4)
    ]
    for copy in loads:
        copy.start()

    base = me_ref[0] * rows
    lane = iota((1, axial), 1)
    coef = jnp.zeros((1, axial), F32)
    for q in range(rows):
        coef = jnp.where(lane == q, coef_ref[lax.rem(base + q, coef_ref.shape[0])], coef)
    row = iota((half, axial), 0)
    waves = [
        jnp.where(row <= quarter, 2 * row, 2 * (row - quarter)),
        jnp.where(row < quarter, 2 * row + 1, 2 * (row - quarter) + 1),
    ]
    damping = [1.0 / (1.0 + coef * (wave * wave).astype(F32)) for wave in waves]

    stores = []
    for g in range(rows // part):
        chosen = range(g * part, (g + 1) * part)
        near = [in_ref[: blocks // 2, q].reshape(half, axial) for q in chosen]
        far = [in_ref[blocks // 2 :, q].reshape(half, axial) for q in chosen]
        results = []
        for odd in range(2):
            field = jnp.concatenate([a - b if odd else a + b for a, b in zip(near, far)], axis=1)
            if g == 0:
                loads[2 * odd].wait()
            spectrum = dot3(table_ref[2 * odd], *split(field))
            scale = [
                jnp.broadcast_to(damping[odd][:, q : q + 1], (half, axial)) for q in chosen
            ]
            if g == 0:
                loads[2 * odd + 1].wait()
            damped = spectrum * jnp.concatenate(scale, axis=1)
            results.append(dot3(table_ref[2 * odd + 1], *split(damped)))
        for i, q in enumerate(chosen):
            even, odd = [value[:, i * axial : (i + 1) * axial] for value in results]
            done_ref[: blocks // 2, q] = (even + odd).reshape(blocks // 2, angles, axial)
            done_ref[blocks // 2 :, q] = (even - odd).reshape(blocks // 2, angles, axial)
        at = pl.ds(g * part, part)
        for s in range(blocks):
            stores.append(
                pltpu.make_async_copy(
                    done_ref.at[me_ref[0] ^ s, at], out_refs[s].at[at], out_sems.at[g, s]
                )
            )
            stores[-1].start()
    for copy in stores:
        copy.wait()


def solve(coef, me, field, after):
    blocks, rows, angles, axial = field.shape
    all_angles = blocks * angles
    tables = fourier_tables(all_angles)
    smem = pl.BlockSpec(memory_space=pltpu.SMEM)
    whole = pl.BlockSpec(memory_space=pltpu.VMEM)
    unread = pl.BlockSpec(memory_space=pl.ANY)
    return pl.pallas_call(
        functools.partial(solve_kernel, extra=len(after)),
        in_specs=[smem, smem, unread] + [unread] * len(after) + [whole],
        out_specs=[unread] * blocks,
        out_shape=[pltpu.HBM(field.shape[1:], F32)] * blocks,
        scratch_shapes=[
            pltpu.VMEM(tables.shape, BF16),
            pltpu.VMEM(field.shape, F32),
            pltpu.SemaphoreType.DMA((4,)),
            pltpu.SemaphoreType.DMA((rows // math.gcd(rows, 2), blocks)),
        ],
        compiler_params=pltpu.CompilerParams(vmem_limit_bytes=28 * MIB),
        cost_estimate=pl.CostEstimate(
            flops=12 * all_angles * all_angles * rows * axial,
            bytes_accessed=8 * all_angles * rows * axial,
            transcendentals=0,
        ),
        name="solve",
    )(
        coef,
        me,
        in_hbm(jnp.asarray(tables)),
        *after,
        in_vmem(field),
    )


def join_kernel(me_ref, force_ref, own_ref, *refs):
    count = len(refs) - 4
    piece_refs, (out_ref, sum_ref, in_sems, out_sems) = refs[:count], refs[count:]
    blocks, rows = sum_ref.shape[0] - 1, sum_ref.shape[1]
    me = me_ref[0]
    reads, writes = [], []
    for s in range(blocks):
        at = pl.ds((me ^ s) * rows, rows)
        reads.append(
            pltpu.make_async_copy(force_ref.at[at], sum_ref.at[s], in_sems.at[s])
        )
        writes.append(
            pltpu.make_async_copy(sum_ref.at[s], out_ref.at[at], out_sems.at[s])
        )
    own = pltpu.make_async_copy(own_ref, sum_ref.at[blocks], in_sems.at[blocks])
    own.start()
    for copy in reads:
        copy.start()
    own.wait()
    for s in range(blocks):
        reads[s].wait()
        piece = sum_ref[blocks] if s == 0 else piece_refs[s - 1][...]
        sum_ref[s] = sum_ref[s] + piece
        writes[s].start()
    for copy in writes:
        copy.wait()


def join(me, force, pieces):
    rows, angles, axial = pieces[0].shape
    blocks = len(pieces)
    whole = pl.BlockSpec(memory_space=pltpu.VMEM)
    away = pl.BlockSpec(memory_space=pl.ANY)
    return pl.pallas_call(
        join_kernel,
        in_specs=[pl.BlockSpec(memory_space=pltpu.SMEM), away, away] + [whole] * (blocks - 1),
        out_specs=away,
        out_shape=pltpu.HBM(force.shape, F32),
        scratch_shapes=[
            pltpu.VMEM((blocks + 1, rows, angles, axial), F32),
            pltpu.SemaphoreType.DMA((blocks + 1,)),
            pltpu.SemaphoreType.DMA((blocks,)),
        ],
        compiler_params=pltpu.CompilerParams(vmem_limit_bytes=14 * MIB),
        cost_estimate=pl.CostEstimate(
            flops=force.size, bytes_accessed=12 * force.size, transcendentals=0
        ),
        name="join",
    )(me, in_hbm(force), in_hbm(pieces[0]), *[in_vmem(piece) for piece in pieces[1:]])


def exchange(pieces):
    count = len(pieces)
    received = [pieces[0]] + [None] * (count - 1)
    order = list(range(2, count, 2)) + list(range(3, count, 2)) + [1]
    for s in order:
        received[s] = lax.ppermute(pieces[s], "az", [(i, i ^ s) for i in range(count)])
    return received


def from_neighbours(low_edge, high_edge):
    count = lax.axis_size("rad")
    forward = [(i, i + 1) for i in range(count - 1)]
    backward = [(target, source) for source, target in forward]
    low = lax.ppermute(high_edge, "rad", forward)
    high = lax.ppermute(low_edge, "rad", backward)
    return low, high


def per_device(velocity, dumbbells, cell_ids, brownian, stencil_coef, block_inverse, azim_coef):
    _, radii, angles, axial = velocity.shape
    az = lax.axis_size("az")
    rows = 3 * radii // az
    pieces = velocity.reshape(az, rows, angles, axial)
    gathered = lax.all_to_all(pieces, "az", 0, 0, tiled=True)
    low_edge, high_edge = deposit_edges(cell_ids, dumbbells, velocity)
    low, high = from_neighbours(low_edge, high_edge)
    middle = deposit_middle(cell_ids, dumbbells, low_edge, velocity.shape)
    stress = (low_edge, middle, high_edge)
    grad, force = derive(stencil_coef, block_inverse, low, velocity, stress, high)
    me = lax.axis_index("az").astype(jnp.int32).reshape(1)
    solved = solve(azim_coef, me, gathered, (in_hbm(force),))
    pieces = exchange(solved)
    moved = move(grad, cell_ids, dumbbells, brownian, angles)
    lines = (3 * radii, angles, axial)
    result = join(me, force.reshape(lines), pieces)
    return result.reshape(velocity.shape), moved


def solution(mesh):
    placed = (
        P(None, "rad", "az", None),
        P(None, "rad", "az", None),
        P(None, "rad", "az", None),
        P(None, "rad", "az", None),
        P(None, "rad"),
        P("rad", None),
        P("rad"),
    )
    return jax.shard_map(
        per_device,
        mesh=mesh,
        in_specs=placed,
        out_specs=(P(None, "rad", "az", None), P(None, "rad", "az", None)),
        check_vma=False,
    )
```

```python
import functools
import functools
import math

import jax
import jax.numpy as jnp
import numpy as np
from jax import lax
from jax.experimental import pallas as pl
from jax.experimental.pallas import tpu as pltpu
from jax.sharding import PartitionSpec as P

TIME_STEP = 0.05
MAX_STRETCH = 10.0
STRESS_SCALE = 4.0
PRECISE = lax.Precision.HIGHEST
HALO = 4
SUB = 8
MIB = 1024 * 1024
F32 = jnp.float32
BF16 = jnp.bfloat16


def split(value):
    high = value.astype(BF16)
    return high, (value - high.astype(F32)).astype(BF16)


def dot(a, b):
    return jnp.dot(a, b, preferred_element_type=F32)


def dot3(stacked, b_high, b_low):
    rows = stacked.shape[0] // 2
    both = dot(stacked, b_high)
    return both[:rows] + both[rows:] + dot(stacked[:rows], b_low)

def in_hbm(value):
    return pltpu.with_memory_space_constraint(value, pltpu.HBM)


def in_vmem(value):
    return pltpu.with_memory_space_constraint(value, pltpu.VMEM)


def iota(shape, dim):
    return lax.broadcasted_iota(jnp.int32, shape, dim)


def weigh(ids_ref, spring_ref, weight_ref):
    axial = weight_ref.shape[0] // 6
    count = weight_ref.shape[1]
    q = [spring_ref[c, 0] for c in range(3)]
    stretch_sq = q[0] * q[0] + q[1] * q[1] + q[2] * q[2]
    factor = 1.0 / (1.0 - stretch_sq / MAX_STRETCH)
    here = iota((axial, count), 0) == ids_ref[1, 0]
    for c in range(3):
        weight = STRESS_SCALE * factor * q[0] * q[c]
        high = weight.astype(BF16).astype(F32)
        weight_ref[c * axial : (c + 1) * axial, :] = jnp.where(here, high, 0.0).astype(BF16)
        weight_ref[(3 + c) * axial : (4 + c) * axial, :] = jnp.where(
            here, weight - high, 0.0
        ).astype(BF16)


def gather_rows(ids_ref, weight_ref, first_row, rows):
    axial = weight_ref.shape[0] // 6
    count = weight_ref.shape[1]
    hot = jnp.where(iota((rows, count), 0) + first_row == ids_ref[0, 0], 1.0, 0.0).astype(BF16)
    both = lax.dot_general(
        hot, weight_ref[...], (((1,), (1,)), ((), ())), preferred_element_type=F32
    )
    return [
        both[:, c * axial : (c + 1) * axial] + both[:, (3 + c) * axial : (4 + c) * axial]
        for c in range(3)
    ]


def edge_kernel(ids_ref, spring_ref, first_ref, last_ref, low_ref, high_ref, weight_ref, *, radii):
    _, _, _, angles, axial = low_ref.shape
    weigh(ids_ref, spring_ref, weight_ref)
    for field_ref, out_ref, radius in (
        (first_ref, low_ref, 0),
        (last_ref, high_ref, radii - HALO),
    ):
        out_ref[0] = field_ref[...]
        values = gather_rows(ids_ref, weight_ref, radius * angles, HALO * angles)
        for c in range(3):
            out_ref[1, c] = values[c].reshape(HALO, angles, axial)


def middle_kernel(ids_ref, spring_ref, stress_ref, weight_ref):
    step = pl.program_id(0)
    _, radii, angles, axial = stress_ref.shape

    @pl.when(step == 0)
    def _():
        weigh(ids_ref, spring_ref, weight_ref)

    rows = radii * angles
    values = gather_rows(ids_ref, weight_ref, HALO * angles + step * rows, rows)
    for c in range(3):
        stress_ref[c] = values[c].reshape(radii, angles, axial)


def deposit_edges(ids, spring, velocity):
    _, radii, angles, axial = velocity.shape
    count = ids.shape[3]
    edge = (2, 3, HALO, angles, axial)
    edge_block = (3, HALO, angles, axial)
    whole = pl.BlockSpec(memory_space=pltpu.VMEM)
    return pl.pallas_call(
        functools.partial(edge_kernel, radii=radii),
        grid=(1,),
        in_specs=[
            whole,
            whole,
            pl.BlockSpec(edge_block, lambda i: (0, 0, 0, 0)),
            pl.BlockSpec(edge_block, lambda i: (0, radii // HALO - 1, 0, 0)),
        ],
        out_specs=[pl.BlockSpec(edge, lambda i: (0, 0, 0, 0, 0))] * 2,
        out_shape=[pltpu.HBM(edge, F32)] * 2,
        scratch_shapes=[pltpu.VMEM((6 * axial, count), BF16)],
        compiler_params=pltpu.CompilerParams(vmem_limit_bytes=28 * MIB),
        cost_estimate=pl.CostEstimate(
            flops=24 * HALO * angles * count * axial,
            bytes_accessed=96 * HALO * angles * axial,
            transcendentals=0,
        ),
        name="deposit_edges",
    )(ids, spring, in_hbm(velocity), in_hbm(velocity))


def deposit_middle(ids, spring, low_edge, shape):
    _, radii, angles, axial = shape
    count = ids.shape[3]
    inner = radii - 2 * HALO
    part = math.gcd(inner, max(1, 512 // angles))
    whole = pl.BlockSpec(memory_space=pltpu.VMEM)
    return pl.pallas_call(
        lambda ids_ref, spring_ref, _, *refs: middle_kernel(ids_ref, spring_ref, *refs),
        grid=(inner // part,),
        in_specs=[whole, whole, pl.BlockSpec(memory_space=pl.ANY)],
        out_specs=pl.BlockSpec((3, part, angles, axial), lambda i: (0, i, 0, 0)),
        out_shape=pltpu.HBM((3, inner, angles, axial), F32),
        scratch_shapes=[pltpu.VMEM((6 * axial, count), BF16)],
        compiler_params=pltpu.CompilerParams(vmem_limit_bytes=28 * MIB),
        cost_estimate=pl.CostEstimate(
            flops=12 * inner * angles * count * axial,
            bytes_accessed=12 * inner * angles * axial,
            transcendentals=0,
        ),
        name="deposit_middle",
    )(ids, spring, in_hbm(low_edge))


def derivative_matrix(stencil_ref, inverse_ref):
    rows = inverse_ref.shape[1]
    wide = rows + 2 * HALO
    offset = iota((wide, rows), 0) - iota((wide, rows), 1)
    band = jnp.zeros((wide, rows), F32)
    for s in range(2 * HALO + 1):
        band = band + jnp.where(offset == s, stencil_ref[s : s + 1, :], 0.0)
    small = lax.dot_general(
        inverse_ref[...],
        band,
        (((1,), (1,)), ((), ())),
        precision=PRECISE,
        preferred_element_type=F32,
    )
    tall = jnp.where(iota((rows * SUB, rows), 0) // SUB == iota((rows * SUB, rows), 1), 1.0, 0.0)
    flat = jnp.where(iota((wide, wide * SUB), 1) // SUB == iota((wide, wide * SUB), 0), 1.0, 0.0)
    big = (rows * SUB, wide * SUB)
    same = iota(big, 0) % SUB == iota(big, 1) % SUB
    parts = []
    for part in split(small):
        spread = dot(dot(tall.astype(BF16), part).astype(BF16), flat.astype(BF16))
        parts.append(jnp.where(same, spread, 0.0).astype(BF16))
    return jnp.concatenate(parts, axis=0)


def derive_kernel(
    stencil_ref,
    inverse_ref,
    low_ref,
    velocity_ref,
    low_edge_ref,
    middle_ref,
    high_edge_ref,
    high_ref,
    grad_ref,
    force_ref,
    matrix_ref,
):
    radii, angles, axial = velocity_ref.shape[1:]

    @pl.when(pl.program_id(0) == 0)
    def _():
        matrix_ref[...] = derivative_matrix(stencil_ref, inverse_ref)

    for i in range(angles // SUB):
        at = pl.ds(i * SUB, SUB)
        columns = []
        own = [
            [velocity_ref],
            [low_edge_ref.at[0], middle_ref, high_edge_ref.at[0]],
        ]
        for f in range(2):
            refs = [low_ref.at[f]] + own[f] + [high_ref.at[f]]
            for c in range(3):
                value = jnp.concatenate([ref[c, :, at, :] for ref in refs], axis=0)
                columns.append(value.reshape((radii + 2 * HALO) * SUB, axial))
        field_high, field_low = split(jnp.concatenate(columns, axis=1))
        result = dot3(matrix_ref[...], field_high, field_low)
        for c in range(3):
            force = TIME_STEP * result[:, (3 + c) * axial : (4 + c) * axial]
            force_ref[c, :, at, :] = force.reshape(radii, SUB, axial)
            grad = result[:, c * axial : (c + 1) * axial]
            grad_ref[c, :, at, :] = grad.reshape(radii, SUB, axial)


def derive(stencil, inverse, low, velocity, stress, high):
    low_edge, middle, high_edge = stress
    radii, angles, axial = velocity.shape[1:]
    part = 2 * SUB

    def block(count, first=None):
        if first is None:
            return pl.BlockSpec((3, count, part, axial), lambda i: (0, 0, i, 0))
        return pl.BlockSpec((2 - first, 3, count, part, axial), lambda i: (first, 0, 0, i, 0))

    return pl.pallas_call(
        derive_kernel,
        grid=(angles // part,),
        in_specs=[
            pl.BlockSpec(stencil.shape, lambda i: (0, 0)),
            pl.BlockSpec(inverse.shape, lambda i: (0, 0)),
            block(HALO, 0),
            block(radii),
            block(HALO, 1),
            block(radii - 2 * HALO),
            block(HALO, 1),
            block(HALO, 0),
        ],
        out_specs=[
            block(radii),
            block(radii),
        ],
        out_shape=[
            pltpu.HBM(velocity.shape, F32),
            pltpu.HBM(velocity.shape, F32),
        ],
        scratch_shapes=[pltpu.VMEM((2 * radii * SUB, (radii + 2 * HALO) * SUB), BF16)],
        compiler_params=pltpu.CompilerParams(vmem_limit_bytes=28 * MIB),
        cost_estimate=pl.CostEstimate(
            flops=3600 * radii * radii * angles * axial // 8,
            bytes_accessed=40 * radii * angles * axial,
            transcendentals=0,
        ),
        name="derive",
    )(
        stencil,
        inverse,
        in_vmem(low),
        in_hbm(velocity),
        in_hbm(low_edge),
        in_hbm(middle),
        in_hbm(high_edge),
        in_vmem(high),
    )


def move_kernel(grad_ref, ids_ref, spring_ref, noise_ref, moved_ref, turned_ref):
    _, radii, angles, axial = grad_ref.shape
    cells = radii * angles
    group = radii * SUB

    def turn(i, carry):
        at = pl.ds(pl.multiple_of(i * SUB, SUB), SUB)
        value = jnp.concatenate(
            [grad_ref[c, :, at, :].reshape(group, axial) for c in range(3)], axis=1
        )
        turned_high, turned_low = split(value.T)
        cols = pl.ds(pl.multiple_of(i * group, group), group)
        turned_ref[: 3 * axial, cols] = turned_high
        turned_ref[3 * axial :, cols] = turned_low
        return carry

    lax.fori_loop(0, angles // SUB, turn, 0)

    count = spring_ref.shape[3]
    part = min(count, 512)

    def read(i, carry):
        at = pl.ds(pl.multiple_of(i * part, part), part)
        plane = ids_ref[0, 0, :, at]
        radius, angle = plane // angles, plane % angles
        column = (angle // SUB) * group + radius * SUB + angle % SUB
        hot = jnp.where(iota((cells, part), 0) == column, 1.0, 0.0).astype(BF16)
        picked = dot(turned_ref[...], hot)
        here = iota((axial, part), 0) == ids_ref[1, 0, :, at]
        q = [spring_ref[c, 0, :, at] for c in range(3)]
        stretch_sq = q[0] * q[0] + q[1] * q[1] + q[2] * q[2]
        factor = 1.0 / (1.0 - stretch_sq / MAX_STRETCH)
        for c in range(3):
            value = (
                picked[c * axial : (c + 1) * axial] + picked[(3 + c) * axial : (4 + c) * axial]
            )
            shear = jnp.sum(jnp.where(here, value, 0.0), axis=0, keepdims=True)
            moved_ref[c, 0, :, at] = (
                q[c]
                + TIME_STEP * (shear * q[0] - 0.5 * factor * q[c])
                + math.sqrt(TIME_STEP) * noise_ref[c, 0, :, at]
            )
        return carry

    lax.fori_loop(0, count // part, read, 0)


def move(grad, ids, spring, noise):
    _, radii, angles, axial = grad.shape
    whole = pl.BlockSpec(memory_space=pltpu.VMEM)
    return pl.pallas_call(
        move_kernel,
        in_specs=[whole] * 4,
        out_specs=whole,
        out_shape=jax.ShapeDtypeStruct(spring.shape, F32),
        scratch_shapes=[pltpu.VMEM((6 * axial, radii * angles), BF16)],
        compiler_params=pltpu.CompilerParams(vmem_limit_bytes=28 * MIB),
        cost_estimate=pl.CostEstimate(
            flops=4 * grad.size * spring.shape[3],
            bytes_accessed=4 * grad.size,
            transcendentals=0,
        ),
        name="move",
    )(in_hbm(grad), ids, spring, noise)


def fourier_tables(all_angles):
    half = all_angles // 2
    row = np.arange(half)
    quarter = half // 2
    waves = [
        np.where(row <= quarter, 2 * row, 2 * (row - quarter)),
        np.where(row < quarter, 2 * row + 1, 2 * (row - quarter) + 1),
    ]
    cosine = [row <= quarter, row < quarter]
    tables = []
    for wave, even in zip(waves, cosine):
        phase = (wave[:, None] * row[None, :]) % all_angles
        angle = phase * (2.0 * math.pi / all_angles)
        table = np.where(even[:, None], np.cos(angle), np.sin(angle))
        weight = np.where((wave == 0) | (wave == half), 1.0, 2.0) / all_angles
        for value in (table, table.T * weight[None, :]):
            value = value.astype(np.float32)
            high = value.astype(BF16)
            low = (value - high.astype(np.float32)).astype(BF16)
            tables.append(np.concatenate([high, low], axis=0))
    return np.stack(tables)


def solve_kernel(coef_ref, me_ref, tables_ref, *refs, extra):
    in_ref, refs = refs[extra], refs[extra + 1 :]
    blocks, rows, angles, axial = in_ref.shape
    out_refs = refs[:blocks]
    table_ref, done_ref, table_sems, out_sems = refs[blocks:]
    half = blocks * angles // 2
    quarter = half // 2
    part = math.gcd(rows, 2)
    loads = [
        pltpu.make_async_copy(tables_ref.at[i], table_ref.at[i], table_sems.at[i])
        for i in range(4)
    ]
    for copy in loads:
        copy.start()

    base = me_ref[0] * rows
    lane = iota((1, axial), 1)
    coef = jnp.zeros((1, axial), F32)
    for q in range(rows):
        coef = jnp.where(lane == q, coef_ref[lax.rem(base + q, coef_ref.shape[0])], coef)
    row = iota((half, axial), 0)
    waves = [
        jnp.where(row <= quarter, 2 * row, 2 * (row - quarter)),
        jnp.where(row < quarter, 2 * row + 1, 2 * (row - quarter) + 1),
    ]
    damping = [1.0 / (1.0 + coef * (wave * wave).astype(F32)) for wave in waves]

    stores = []
    for g in range(rows // part):
        chosen = range(g * part, (g + 1) * part)
        near = [in_ref[: blocks // 2, q].reshape(half, axial) for q in chosen]
        far = [in_ref[blocks // 2 :, q].reshape(half, axial) for q in chosen]
        results = []
        for odd in range(2):
            field = jnp.concatenate([a - b if odd else a + b for a, b in zip(near, far)], axis=1)
            if g == 0:
                loads[2 * odd].wait()
            spectrum = dot3(table_ref[2 * odd], *split(field))
            scale = [
                jnp.broadcast_to(damping[odd][:, q : q + 1], (half, axial)) for q in chosen
            ]
            if g == 0:
                loads[2 * odd + 1].wait()
            damped = spectrum * jnp.concatenate(scale, axis=1)
            results.append(dot3(table_ref[2 * odd + 1], *split(damped)))
        for i, q in enumerate(chosen):
            even, odd = [value[:, i * axial : (i + 1) * axial] for value in results]
            done_ref[: blocks // 2, q] = (even + odd).reshape(blocks // 2, angles, axial)
            done_ref[blocks // 2 :, q] = (even - odd).reshape(blocks // 2, angles, axial)
        at = pl.ds(g * part, part)
        for s in range(blocks):
            stores.append(
                pltpu.make_async_copy(
                    done_ref.at[me_ref[0] ^ s, at], out_refs[s].at[at], out_sems.at[g, s]
                )
            )
            stores[-1].start()
    for copy in stores:
        copy.wait()


def solve(coef, me, field, after):
    blocks, rows, angles, axial = field.shape
    all_angles = blocks * angles
    tables = fourier_tables(all_angles)
    smem = pl.BlockSpec(memory_space=pltpu.SMEM)
    whole = pl.BlockSpec(memory_space=pltpu.VMEM)
    unread = pl.BlockSpec(memory_space=pl.ANY)
    return pl.pallas_call(
        functools.partial(solve_kernel, extra=len(after)),
        in_specs=[smem, smem, unread] + [unread] * len(after) + [whole],
        out_specs=[unread] * blocks,
        out_shape=[pltpu.HBM(field.shape[1:], F32)] * blocks,
        scratch_shapes=[
            pltpu.VMEM(tables.shape, BF16),
            pltpu.VMEM(field.shape, F32),
            pltpu.SemaphoreType.DMA((4,)),
            pltpu.SemaphoreType.DMA((rows // math.gcd(rows, 2), blocks)),
        ],
        compiler_params=pltpu.CompilerParams(vmem_limit_bytes=28 * MIB),
        cost_estimate=pl.CostEstimate(
            flops=12 * all_angles * all_angles * rows * axial,
            bytes_accessed=8 * all_angles * rows * axial,
            transcendentals=0,
        ),
        name="solve",
    )(
        coef,
        me,
        in_hbm(jnp.asarray(tables)),
        *after,
        in_vmem(field),
    )


def join_kernel(me_ref, force_ref, *refs, first, given):
    count = len(refs) - 4 - given
    piece_refs, refs = refs[:count], refs[count + given :]
    out_ref, sum_ref, in_sems, out_sems = refs
    rows = sum_ref.shape[1]
    reads, writes = [], []
    for i in range(count):
        at = pl.ds((me_ref[0] ^ (first + i)) * rows, rows)
        reads.append(pltpu.make_async_copy(force_ref.at[at], sum_ref.at[i], in_sems.at[i]))
        writes.append(pltpu.make_async_copy(sum_ref.at[i], out_ref.at[at], out_sems.at[i]))
    for copy in reads:
        copy.start()
    for i in range(count):
        reads[i].wait()
        sum_ref[i] = sum_ref[i] + piece_refs[i][...]
        writes[i].start()
    for copy in writes:
        copy.wait()


def join(me, force, pieces, first, result=None):
    rows, angles, axial = pieces[0].shape
    count = len(pieces)
    given = [] if result is None else [in_hbm(result)]
    whole = pl.BlockSpec(memory_space=pltpu.VMEM)
    away = pl.BlockSpec(memory_space=pl.ANY)
    return pl.pallas_call(
        functools.partial(join_kernel, first=first, given=len(given)),
        in_specs=[pl.BlockSpec(memory_space=pltpu.SMEM), away]
        + [whole] * count
        + [away] * len(given),
        out_specs=away,
        out_shape=pltpu.HBM(force.shape, F32),
        input_output_aliases={2 + count: 0} if given else {},
        scratch_shapes=[
            pltpu.VMEM((count, rows, angles, axial), F32),
            pltpu.SemaphoreType.DMA((count,)),
            pltpu.SemaphoreType.DMA((count,)),
        ],
        compiler_params=pltpu.CompilerParams(vmem_limit_bytes=14 * MIB),
        cost_estimate=pl.CostEstimate(
            flops=count * rows * angles * axial,
            bytes_accessed=12 * count * rows * angles * axial,
            transcendentals=0,
        ),
        name="join",
    )(me, in_hbm(force), *pieces, *given)


def exchange(pieces):
    count = len(pieces)
    received = [pieces[0]] + [None] * (count - 1)
    order = list(range(2, count, 2)) + list(range(3, count, 2)) + [1]
    for s in order:
        received[s] = lax.ppermute(pieces[s], "az", [(i, i ^ s) for i in range(count)])
    return received


def from_neighbours(low_edge, high_edge):
    count = lax.axis_size("rad")
    forward = [(i, i + 1) for i in range(count - 1)]
    backward = [(target, source) for source, target in forward]
    low = lax.ppermute(high_edge, "rad", forward)
    high = lax.ppermute(low_edge, "rad", backward)
    return low, high


def per_device(velocity, dumbbells, cell_ids, brownian, stencil_coef, block_inverse, azim_coef):
    _, radii, angles, axial = velocity.shape
    az = lax.axis_size("az")
    rows = 3 * radii // az
    pieces = velocity.reshape(az, rows, angles, axial)
    gathered = lax.all_to_all(pieces, "az", 0, 0, tiled=True)
    low_edge, high_edge = deposit_edges(cell_ids, dumbbells, velocity)
    low, high = from_neighbours(low_edge, high_edge)
    middle = deposit_middle(cell_ids, dumbbells, low_edge, velocity.shape)
    stress = (low_edge, middle, high_edge)
    grad, force = derive(stencil_coef, block_inverse, low, velocity, stress, high)
    me = lax.axis_index("az").astype(jnp.int32).reshape(1)
    solved = solve(azim_coef, me, gathered, (in_hbm(force),))
    pieces = exchange(solved)
    moved = move(grad, cell_ids, dumbbells, brownian)
    lines = (3 * radii, angles, axial)
    force = force.reshape(lines)
    early = len(pieces) * 3 // 8
    result = join(me, force, pieces[:early], 0)
    result = join(me, force, [in_vmem(piece) for piece in pieces[early:]], early, result)
    return result.reshape(velocity.shape), moved


def solution(mesh):
    placed = (
        P(None, "rad", "az", None),
        P(None, "rad", "az", None),
        P(None, "rad", "az", None),
        P(None, "rad", "az", None),
        P(None, "rad"),
        P("rad", None),
        P("rad"),
    )
    return jax.shard_map(
        per_device,
        mesh=mesh,
        in_specs=placed,
        out_specs=(P(None, "rad", "az", None), P(None, "rad", "az", None)),
        check_vma=False,
    )
```

```python
import functools
import functools
import math

import jax
import jax.numpy as jnp
import numpy as np
from jax import lax
from jax.experimental import pallas as pl
from jax.experimental.pallas import tpu as pltpu
from jax.sharding import PartitionSpec as P

TIME_STEP = 0.05
MAX_STRETCH = 10.0
STRESS_SCALE = 4.0
PRECISE = lax.Precision.HIGHEST
HALO = 4
SUB = 8
MIB = 1024 * 1024
F32 = jnp.float32
BF16 = jnp.bfloat16


def split(value):
    high = value.astype(BF16)
    return high, (value - high.astype(F32)).astype(BF16)


def dot(a, b):
    return jnp.dot(a, b, preferred_element_type=F32)


def dot3(stacked, b_high, b_low):
    rows = stacked.shape[0] // 2
    both = dot(stacked, b_high)
    return both[:rows] + both[rows:] + dot(stacked[:rows], b_low)

def in_hbm(value):
    return pltpu.with_memory_space_constraint(value, pltpu.HBM)


def in_vmem(value):
    return pltpu.with_memory_space_constraint(value, pltpu.VMEM)


def iota(shape, dim):
    return lax.broadcasted_iota(jnp.int32, shape, dim)


def weigh(ids_ref, spring_ref, weight_ref):
    axial = weight_ref.shape[0] // 6
    count = weight_ref.shape[1]
    q = [spring_ref[c, 0] for c in range(3)]
    stretch_sq = q[0] * q[0] + q[1] * q[1] + q[2] * q[2]
    factor = 1.0 / (1.0 - stretch_sq / MAX_STRETCH)
    here = iota((axial, count), 0) == ids_ref[1, 0]
    for c in range(3):
        weight = STRESS_SCALE * factor * q[0] * q[c]
        high = weight.astype(BF16).astype(F32)
        weight_ref[c * axial : (c + 1) * axial, :] = jnp.where(here, high, 0.0).astype(BF16)
        weight_ref[(3 + c) * axial : (4 + c) * axial, :] = jnp.where(
            here, weight - high, 0.0
        ).astype(BF16)


def gather_rows(ids_ref, weight_ref, first_row, rows):
    axial = weight_ref.shape[0] // 6
    count = weight_ref.shape[1]
    hot = jnp.where(iota((rows, count), 0) + first_row == ids_ref[0, 0], 1.0, 0.0).astype(BF16)
    both = lax.dot_general(
        hot, weight_ref[...], (((1,), (1,)), ((), ())), preferred_element_type=F32
    )
    return [
        both[:, c * axial : (c + 1) * axial] + both[:, (3 + c) * axial : (4 + c) * axial]
        for c in range(3)
    ]


def edge_kernel(ids_ref, spring_ref, first_ref, last_ref, low_ref, high_ref, weight_ref, *, radii):
    _, _, _, angles, axial = low_ref.shape
    weigh(ids_ref, spring_ref, weight_ref)
    for field_ref, out_ref, radius in (
        (first_ref, low_ref, 0),
        (last_ref, high_ref, radii - HALO),
    ):
        out_ref[0] = field_ref[...]
        values = gather_rows(ids_ref, weight_ref, radius * angles, HALO * angles)
        for c in range(3):
            out_ref[1, c] = values[c].reshape(HALO, angles, axial)


def middle_kernel(ids_ref, spring_ref, stress_ref, weight_ref):
    step = pl.program_id(0)
    _, radii, angles, axial = stress_ref.shape

    @pl.when(step == 0)
    def _():
        weigh(ids_ref, spring_ref, weight_ref)

    rows = radii * angles
    values = gather_rows(ids_ref, weight_ref, HALO * angles + step * rows, rows)
    for c in range(3):
        stress_ref[c] = values[c].reshape(radii, angles, axial)


def deposit_edges(ids, spring, velocity):
    _, radii, angles, axial = velocity.shape
    count = ids.shape[3]
    edge = (2, 3, HALO, angles, axial)
    edge_block = (3, HALO, angles, axial)
    whole = pl.BlockSpec(memory_space=pltpu.VMEM)
    return pl.pallas_call(
        functools.partial(edge_kernel, radii=radii),
        grid=(1,),
        in_specs=[
            whole,
            whole,
            pl.BlockSpec(edge_block, lambda i: (0, 0, 0, 0)),
            pl.BlockSpec(edge_block, lambda i: (0, radii // HALO - 1, 0, 0)),
        ],
        out_specs=[pl.BlockSpec(edge, lambda i: (0, 0, 0, 0, 0))] * 2,
        out_shape=[pltpu.HBM(edge, F32)] * 2,
        scratch_shapes=[pltpu.VMEM((6 * axial, count), BF16)],
        compiler_params=pltpu.CompilerParams(vmem_limit_bytes=28 * MIB),
        cost_estimate=pl.CostEstimate(
            flops=24 * HALO * angles * count * axial,
            bytes_accessed=96 * HALO * angles * axial,
            transcendentals=0,
        ),
        name="deposit_edges",
    )(ids, spring, in_hbm(velocity), in_hbm(velocity))


def deposit_middle(ids, spring, low_edge, shape):
    _, radii, angles, axial = shape
    count = ids.shape[3]
    inner = radii - 2 * HALO
    part = math.gcd(inner, max(1, 512 // angles))
    whole = pl.BlockSpec(memory_space=pltpu.VMEM)
    return pl.pallas_call(
        lambda ids_ref, spring_ref, _, *refs: middle_kernel(ids_ref, spring_ref, *refs),
        grid=(inner // part,),
        in_specs=[whole, whole, pl.BlockSpec(memory_space=pl.ANY)],
        out_specs=pl.BlockSpec((3, part, angles, axial), lambda i: (0, i, 0, 0)),
        out_shape=pltpu.HBM((3, inner, angles, axial), F32),
        scratch_shapes=[pltpu.VMEM((6 * axial, count), BF16)],
        compiler_params=pltpu.CompilerParams(vmem_limit_bytes=28 * MIB),
        cost_estimate=pl.CostEstimate(
            flops=12 * inner * angles * count * axial,
            bytes_accessed=12 * inner * angles * axial,
            transcendentals=0,
        ),
        name="deposit_middle",
    )(ids, spring, in_hbm(low_edge))


def derivative_matrix(stencil_ref, inverse_ref):
    rows = inverse_ref.shape[1]
    wide = rows + 2 * HALO
    offset = iota((wide, rows), 0) - iota((wide, rows), 1)
    band = jnp.zeros((wide, rows), F32)
    for s in range(2 * HALO + 1):
        band = band + jnp.where(offset == s, stencil_ref[s : s + 1, :], 0.0)
    small = lax.dot_general(
        inverse_ref[...],
        band,
        (((1,), (1,)), ((), ())),
        precision=PRECISE,
        preferred_element_type=F32,
    )
    tall = jnp.where(iota((rows * SUB, rows), 0) // SUB == iota((rows * SUB, rows), 1), 1.0, 0.0)
    flat = jnp.where(iota((wide, wide * SUB), 1) // SUB == iota((wide, wide * SUB), 0), 1.0, 0.0)
    big = (rows * SUB, wide * SUB)
    same = iota(big, 0) % SUB == iota(big, 1) % SUB
    parts = []
    for part in split(small):
        spread = dot(dot(tall.astype(BF16), part).astype(BF16), flat.astype(BF16))
        parts.append(jnp.where(same, spread, 0.0).astype(BF16))
    return jnp.concatenate(parts, axis=0)


def derive_kernel(
    stencil_ref,
    inverse_ref,
    low_ref,
    velocity_ref,
    low_edge_ref,
    middle_ref,
    high_edge_ref,
    high_ref,
    piece_ref,
    grad_ref,
    force_ref,
    passed_ref,
    matrix_ref,
    sem,
):
    radii, angles, axial = velocity_ref.shape[1:]

    passing = pltpu.make_async_copy(piece_ref, passed_ref, sem.at[0])

    @pl.when(pl.program_id(0) == 0)
    def _():
        passing.start()
        matrix_ref[...] = derivative_matrix(stencil_ref, inverse_ref)

    group = radii * SUB

    for i in range(angles // SUB):
        at = pl.ds(i * SUB, SUB)
        columns = []
        own = [
            [velocity_ref],
            [low_edge_ref.at[0], middle_ref, high_edge_ref.at[0]],
        ]
        for f in range(2):
            refs = [low_ref.at[f]] + own[f] + [high_ref.at[f]]
            for c in range(3):
                value = jnp.concatenate([ref[c, :, at, :] for ref in refs], axis=0)
                columns.append(value.reshape((radii + 2 * HALO) * SUB, axial))
        field_high, field_low = split(jnp.concatenate(columns, axis=1))
        result = dot3(matrix_ref[...], field_high, field_low)
        for c in range(3):
            force = TIME_STEP * result[:, (3 + c) * axial : (4 + c) * axial]
            force_ref[c, :, at, :] = force.reshape(radii, SUB, axial)
        turned_high, turned_low = split(result[:, : 3 * axial].T)
        cols = pl.ds(i * group, group)
        grad_ref[: 3 * axial, cols] = turned_high
        grad_ref[3 * axial :, cols] = turned_low

    @pl.when(pl.program_id(0) == pl.num_programs(0) - 1)
    def _():
        passing.wait()


def derive(stencil, inverse, low, velocity, stress, high, piece):
    low_edge, middle, high_edge = stress
    radii, angles, axial = velocity.shape[1:]
    part = 2 * SUB

    def block(count, first=None):
        if first is None:
            return pl.BlockSpec((3, count, part, axial), lambda i: (0, 0, i, 0))
        return pl.BlockSpec((2 - first, 3, count, part, axial), lambda i: (first, 0, 0, i, 0))

    return pl.pallas_call(
        derive_kernel,
        grid=(angles // part,),
        in_specs=[
            pl.BlockSpec(stencil.shape, lambda i: (0, 0)),
            pl.BlockSpec(inverse.shape, lambda i: (0, 0)),
            block(HALO, 0),
            block(radii),
            block(HALO, 1),
            block(radii - 2 * HALO),
            block(HALO, 1),
            block(HALO, 0),
            pl.BlockSpec(memory_space=pl.ANY),
        ],
        out_specs=[
            pl.BlockSpec((6 * axial, radii * part), lambda i: (0, i)),
            block(radii),
            pl.BlockSpec(memory_space=pl.ANY),
        ],
        out_shape=[
            pltpu.HBM((6 * axial, radii * angles), BF16),
            pltpu.HBM(velocity.shape, F32),
            pltpu.HBM(piece.shape, F32),
        ],
        scratch_shapes=[
            pltpu.VMEM((2 * radii * SUB, (radii + 2 * HALO) * SUB), BF16),
            pltpu.SemaphoreType.DMA((1,)),
        ],
        compiler_params=pltpu.CompilerParams(vmem_limit_bytes=28 * MIB),
        cost_estimate=pl.CostEstimate(
            flops=3600 * radii * radii * angles * axial // 8,
            bytes_accessed=40 * radii * angles * axial,
            transcendentals=0,
        ),
        name="derive",
    )(
        stencil,
        inverse,
        in_vmem(low),
        in_hbm(velocity),
        in_hbm(low_edge),
        in_hbm(middle),
        in_hbm(high_edge),
        in_vmem(high),
        in_hbm(piece),
    )


def move_kernel(grad_ref, ids_ref, spring_ref, noise_ref, moved_ref, *, angles):
    axial, cells = grad_ref.shape[0] // 6, grad_ref.shape[1]
    group = cells // angles * SUB

    count = spring_ref.shape[3]
    part = min(count, 512)

    def read(i, carry):
        at = pl.ds(pl.multiple_of(i * part, part), part)
        plane = ids_ref[0, 0, :, at]
        radius, angle = plane // angles, plane % angles
        column = (angle // SUB) * group + radius * SUB + angle % SUB
        hot = jnp.where(iota((cells, part), 0) == column, 1.0, 0.0).astype(BF16)
        picked = dot(grad_ref[...], hot)
        here = iota((axial, part), 0) == ids_ref[1, 0, :, at]
        q = [spring_ref[c, 0, :, at] for c in range(3)]
        stretch_sq = q[0] * q[0] + q[1] * q[1] + q[2] * q[2]
        factor = 1.0 / (1.0 - stretch_sq / MAX_STRETCH)
        for c in range(3):
            value = (
                picked[c * axial : (c + 1) * axial] + picked[(3 + c) * axial : (4 + c) * axial]
            )
            shear = jnp.sum(jnp.where(here, value, 0.0), axis=0, keepdims=True)
            moved_ref[c, 0, :, at] = (
                q[c]
                + TIME_STEP * (shear * q[0] - 0.5 * factor * q[c])
                + math.sqrt(TIME_STEP) * noise_ref[c, 0, :, at]
            )
        return carry

    lax.fori_loop(0, count // part, read, 0)


def move(grad, ids, spring, noise, angles):
    cells = grad.shape[1]
    whole = pl.BlockSpec(memory_space=pltpu.VMEM)
    return pl.pallas_call(
        functools.partial(move_kernel, angles=angles),
        in_specs=[whole] * 4,
        out_specs=whole,
        out_shape=jax.ShapeDtypeStruct(spring.shape, F32),
        compiler_params=pltpu.CompilerParams(vmem_limit_bytes=24 * MIB),
        cost_estimate=pl.CostEstimate(
            flops=2 * grad.size * spring.shape[3],
            bytes_accessed=2 * grad.size,
            transcendentals=0,
        ),
        name="move",
    )(in_hbm(grad), ids, spring, noise)


def fourier_tables(all_angles):
    half = all_angles // 2
    row = np.arange(half)
    quarter = half // 2
    waves = [
        np.where(row <= quarter, 2 * row, 2 * (row - quarter)),
        np.where(row < quarter, 2 * row + 1, 2 * (row - quarter) + 1),
    ]
    cosine = [row <= quarter, row < quarter]
    tables = []
    for wave, even in zip(waves, cosine):
        phase = (wave[:, None] * row[None, :]) % all_angles
        angle = phase * (2.0 * math.pi / all_angles)
        table = np.where(even[:, None], np.cos(angle), np.sin(angle))
        weight = np.where((wave == 0) | (wave == half), 1.0, 2.0) / all_angles
        for value in (table, table.T * weight[None, :]):
            value = value.astype(np.float32)
            high = value.astype(BF16)
            low = (value - high.astype(np.float32)).astype(BF16)
            tables.append(np.concatenate([high, low], axis=0))
    return np.stack(tables)


def solve_kernel(coef_ref, me_ref, tables_ref, *refs, extra):
    in_ref, refs = refs[extra], refs[extra + 1 :]
    blocks, rows, angles, axial = in_ref.shape
    out_refs = refs[:blocks]
    table_ref, done_ref, table_sems, out_sems = refs[blocks:]
    half = blocks * angles // 2
    quarter = half // 2
    part = math.gcd(rows, 2)
    loads = [
        pltpu.make_async_copy(tables_ref.at[i], table_ref.at[i], table_sems.at[i])
        for i in range(4)
    ]
    for copy in loads:
        copy.start()

    base = me_ref[0] * rows
    lane = iota((1, axial), 1)
    coef = jnp.zeros((1, axial), F32)
    for q in range(rows):
        coef = jnp.where(lane == q, coef_ref[lax.rem(base + q, coef_ref.shape[0])], coef)
    row = iota((half, axial), 0)
    waves = [
        jnp.where(row <= quarter, 2 * row, 2 * (row - quarter)),
        jnp.where(row < quarter, 2 * row + 1, 2 * (row - quarter) + 1),
    ]
    damping = [1.0 / (1.0 + coef * (wave * wave).astype(F32)) for wave in waves]

    stores = []
    for g in range(rows // part):
        chosen = range(g * part, (g + 1) * part)
        near = [in_ref[: blocks // 2, q].reshape(half, axial) for q in chosen]
        far = [in_ref[blocks // 2 :, q].reshape(half, axial) for q in chosen]
        results = []
        for odd in range(2):
            field = jnp.concatenate([a - b if odd else a + b for a, b in zip(near, far)], axis=1)
            if g == 0:
                loads[2 * odd].wait()
            spectrum = dot3(table_ref[2 * odd], *split(field))
            scale = [
                jnp.broadcast_to(damping[odd][:, q : q + 1], (half, axial)) for q in chosen
            ]
            if g == 0:
                loads[2 * odd + 1].wait()
            damped = spectrum * jnp.concatenate(scale, axis=1)
            results.append(dot3(table_ref[2 * odd + 1], *split(damped)))
        for i, q in enumerate(chosen):
            even, odd = [value[:, i * axial : (i + 1) * axial] for value in results]
            done_ref[: blocks // 2, q] = (even + odd).reshape(blocks // 2, angles, axial)
            done_ref[blocks // 2 :, q] = (even - odd).reshape(blocks // 2, angles, axial)
        at = pl.ds(g * part, part)
        for s in range(blocks):
            stores.append(
                pltpu.make_async_copy(
                    done_ref.at[me_ref[0] ^ s, at], out_refs[s].at[at], out_sems.at[g, s]
                )
            )
            stores[-1].start()
    for copy in stores:
        copy.wait()


def solve(coef, me, field, after):
    blocks, rows, angles, axial = field.shape
    all_angles = blocks * angles
    tables = fourier_tables(all_angles)
    smem = pl.BlockSpec(memory_space=pltpu.SMEM)
    whole = pl.BlockSpec(memory_space=pltpu.VMEM)
    unread = pl.BlockSpec(memory_space=pl.ANY)
    return pl.pallas_call(
        functools.partial(solve_kernel, extra=len(after)),
        in_specs=[smem, smem, unread] + [unread] * len(after) + [whole],
        out_specs=[unread] * blocks,
        out_shape=[pltpu.HBM(field.shape[1:], F32)] * blocks,
        scratch_shapes=[
            pltpu.VMEM(tables.shape, BF16),
            pltpu.VMEM(field.shape, F32),
            pltpu.SemaphoreType.DMA((4,)),
            pltpu.SemaphoreType.DMA((rows // math.gcd(rows, 2), blocks)),
        ],
        compiler_params=pltpu.CompilerParams(vmem_limit_bytes=28 * MIB),
        cost_estimate=pl.CostEstimate(
            flops=12 * all_angles * all_angles * rows * axial,
            bytes_accessed=8 * all_angles * rows * axial,
            transcendentals=0,
        ),
        name="solve",
    )(
        coef,
        me,
        in_hbm(jnp.asarray(tables)),
        *after,
        in_vmem(field),
    )


def join_kernel(me_ref, force_ref, *refs, first, given):
    count = len(refs) - 4 - given
    piece_refs, refs = refs[:count], refs[count + given :]
    out_ref, sum_ref, in_sems, out_sems = refs
    rows = sum_ref.shape[1]
    reads, writes = [], []
    for i in range(count):
        at = pl.ds((me_ref[0] ^ (first + i)) * rows, rows)
        reads.append(pltpu.make_async_copy(force_ref.at[at], sum_ref.at[i], in_sems.at[i]))
        writes.append(pltpu.make_async_copy(sum_ref.at[i], out_ref.at[at], out_sems.at[i]))
    for copy in reads:
        copy.start()
    for i in range(count):
        reads[i].wait()
        sum_ref[i] = sum_ref[i] + piece_refs[i][...]
        writes[i].start()
    for copy in writes:
        copy.wait()


def join(me, force, pieces, first, result=None):
    rows, angles, axial = pieces[0].shape
    count = len(pieces)
    given = [] if result is None else [in_hbm(result)]
    whole = pl.BlockSpec(memory_space=pltpu.VMEM)
    away = pl.BlockSpec(memory_space=pl.ANY)
    return pl.pallas_call(
        functools.partial(join_kernel, first=first, given=len(given)),
        in_specs=[pl.BlockSpec(memory_space=pltpu.SMEM), away]
        + [whole] * count
        + [away] * len(given),
        out_specs=away,
        out_shape=pltpu.HBM(force.shape, F32),
        input_output_aliases={2 + count: 0} if given else {},
        scratch_shapes=[
            pltpu.VMEM((count, rows, angles, axial), F32),
            pltpu.SemaphoreType.DMA((count,)),
            pltpu.SemaphoreType.DMA((count,)),
        ],
        compiler_params=pltpu.CompilerParams(vmem_limit_bytes=14 * MIB),
        cost_estimate=pl.CostEstimate(
            flops=count * rows * angles * axial,
            bytes_accessed=12 * count * rows * angles * axial,
            transcendentals=0,
        ),
        name="join",
    )(me, in_hbm(force), *pieces, *given)


def exchange(pieces):
    count = len(pieces)
    received = [pieces[0]] + [None] * (count - 1)
    order = list(range(2, count, 2)) + list(range(3, count, 2)) + [1]
    for s in order:
        received[s] = lax.ppermute(pieces[s], "az", [(i, i ^ s) for i in range(count)])
    return received


def from_neighbours(low_edge, high_edge):
    count = lax.axis_size("rad")
    forward = [(i, i + 1) for i in range(count - 1)]
    backward = [(target, source) for source, target in forward]
    low = lax.ppermute(high_edge, "rad", forward)
    high = lax.ppermute(low_edge, "rad", backward)
    return low, high


def per_device(velocity, dumbbells, cell_ids, brownian, stencil_coef, block_inverse, azim_coef):
    _, radii, angles, axial = velocity.shape
    az = lax.axis_size("az")
    rows = 3 * radii // az
    pieces = velocity.reshape(az, rows, angles, axial)
    gathered = lax.all_to_all(pieces, "az", 0, 0, tiled=True)
    low_edge, high_edge = deposit_edges(cell_ids, dumbbells, velocity)
    low, high = from_neighbours(low_edge, high_edge)
    middle = deposit_middle(cell_ids, dumbbells, low_edge, velocity.shape)
    stress = (low_edge, middle, high_edge)
    me = lax.axis_index("az").astype(jnp.int32).reshape(1)
    solved = solve(azim_coef, me, gathered, (in_vmem(low), in_vmem(high), in_hbm(middle)))
    grad, force, passed = derive(
        stencil_coef, block_inverse, low, velocity, stress, high, solved[-1]
    )
    pieces = exchange(list(solved[:-1]) + [passed])
    moved = move(grad, cell_ids, dumbbells, brownian, angles)
    lines = (3 * radii, angles, axial)
    force = force.reshape(lines)
    early = len(pieces) * 3 // 8
    result = join(me, force, pieces[:early], 0)
    result = join(me, force, [in_vmem(piece) for piece in pieces[early:]], early, result)
    return result.reshape(velocity.shape), moved


def solution(mesh):
    placed = (
        P(None, "rad", "az", None),
        P(None, "rad", "az", None),
        P(None, "rad", "az", None),
        P(None, "rad", "az", None),
        P(None, "rad"),
        P("rad", None),
        P("rad"),
    )
    return jax.shard_map(
        per_device,
        mesh=mesh,
        in_specs=placed,
        out_specs=(P(None, "rad", "az", None), P(None, "rad", "az", None)),
        check_vma=False,
    )
```

```python
import functools
import functools
import math

import jax
import jax.numpy as jnp
import numpy as np
from jax import lax
from jax.experimental import pallas as pl
from jax.experimental.pallas import tpu as pltpu
from jax.sharding import PartitionSpec as P

TIME_STEP = 0.05
MAX_STRETCH = 10.0
STRESS_SCALE = 4.0
PRECISE = lax.Precision.HIGHEST
HALO = 4
SUB = 8
MIB = 1024 * 1024
F32 = jnp.float32
BF16 = jnp.bfloat16


def split(value):
    high = value.astype(BF16)
    return high, (value - high.astype(F32)).astype(BF16)


def dot(a, b):
    return jnp.dot(a, b, preferred_element_type=F32)


def dot3(stacked, b_high, b_low):
    rows = stacked.shape[0] // 2
    both = dot(stacked, b_high)
    return both[:rows] + both[rows:] + dot(stacked[:rows], b_low)

def in_hbm(value):
    return pltpu.with_memory_space_constraint(value, pltpu.HBM)


def in_vmem(value):
    return pltpu.with_memory_space_constraint(value, pltpu.VMEM)


def iota(shape, dim):
    return lax.broadcasted_iota(jnp.int32, shape, dim)


def weigh(ids_ref, spring_ref, weight_ref):
    axial = weight_ref.shape[0] // 6
    count = weight_ref.shape[1]
    q = [spring_ref[c, 0] for c in range(3)]
    stretch_sq = q[0] * q[0] + q[1] * q[1] + q[2] * q[2]
    factor = 1.0 / (1.0 - stretch_sq / MAX_STRETCH)
    here = iota((axial, count), 0) == ids_ref[1, 0]
    for c in range(3):
        weight = STRESS_SCALE * factor * q[0] * q[c]
        high = weight.astype(BF16).astype(F32)
        weight_ref[c * axial : (c + 1) * axial, :] = jnp.where(here, high, 0.0).astype(BF16)
        weight_ref[(3 + c) * axial : (4 + c) * axial, :] = jnp.where(
            here, weight - high, 0.0
        ).astype(BF16)


def gather_rows(ids_ref, weight_ref, first_row, rows):
    axial = weight_ref.shape[0] // 6
    count = weight_ref.shape[1]
    hot = jnp.where(iota((rows, count), 0) + first_row == ids_ref[0, 0], 1.0, 0.0).astype(BF16)
    both = lax.dot_general(
        hot, weight_ref[...], (((1,), (1,)), ((), ())), preferred_element_type=F32
    )
    return [
        both[:, c * axial : (c + 1) * axial] + both[:, (3 + c) * axial : (4 + c) * axial]
        for c in range(3)
    ]


def edge_kernel(ids_ref, spring_ref, first_ref, last_ref, low_ref, high_ref, weight_ref, *, radii):
    _, _, _, angles, axial = low_ref.shape
    weigh(ids_ref, spring_ref, weight_ref)
    for field_ref, out_ref, radius in (
        (first_ref, low_ref, 0),
        (last_ref, high_ref, radii - HALO),
    ):
        out_ref[0] = field_ref[...]
        values = gather_rows(ids_ref, weight_ref, radius * angles, HALO * angles)
        for c in range(3):
            out_ref[1, c] = values[c].reshape(HALO, angles, axial)


def middle_kernel(ids_ref, spring_ref, stress_ref, weight_ref):
    step = pl.program_id(0)
    _, radii, angles, axial = stress_ref.shape

    @pl.when(step == 0)
    def _():
        weigh(ids_ref, spring_ref, weight_ref)

    rows = radii * angles
    values = gather_rows(ids_ref, weight_ref, HALO * angles + step * rows, rows)
    for c in range(3):
        stress_ref[c] = values[c].reshape(radii, angles, axial)


def deposit_edges(ids, spring, velocity):
    _, radii, angles, axial = velocity.shape
    count = ids.shape[3]
    edge = (2, 3, HALO, angles, axial)
    edge_block = (3, HALO, angles, axial)
    whole = pl.BlockSpec(memory_space=pltpu.VMEM)
    return pl.pallas_call(
        functools.partial(edge_kernel, radii=radii),
        grid=(1,),
        in_specs=[
            whole,
            whole,
            pl.BlockSpec(edge_block, lambda i: (0, 0, 0, 0)),
            pl.BlockSpec(edge_block, lambda i: (0, radii // HALO - 1, 0, 0)),
        ],
        out_specs=[pl.BlockSpec(edge, lambda i: (0, 0, 0, 0, 0))] * 2,
        out_shape=[pltpu.HBM(edge, F32)] * 2,
        scratch_shapes=[pltpu.VMEM((6 * axial, count), BF16)],
        compiler_params=pltpu.CompilerParams(vmem_limit_bytes=28 * MIB),
        cost_estimate=pl.CostEstimate(
            flops=24 * HALO * angles * count * axial,
            bytes_accessed=96 * HALO * angles * axial,
            transcendentals=0,
        ),
        name="deposit_edges",
    )(ids, spring, in_hbm(velocity), in_hbm(velocity))


def deposit_middle(ids, spring, low_edge, shape):
    _, radii, angles, axial = shape
    count = ids.shape[3]
    inner = radii - 2 * HALO
    part = math.gcd(inner, max(1, 512 // angles))
    whole = pl.BlockSpec(memory_space=pltpu.VMEM)
    return pl.pallas_call(
        lambda ids_ref, spring_ref, _, *refs: middle_kernel(ids_ref, spring_ref, *refs),
        grid=(inner // part,),
        in_specs=[whole, whole, pl.BlockSpec(memory_space=pl.ANY)],
        out_specs=pl.BlockSpec((3, part, angles, axial), lambda i: (0, i, 0, 0)),
        out_shape=pltpu.HBM((3, inner, angles, axial), F32),
        scratch_shapes=[pltpu.VMEM((6 * axial, count), BF16)],
        compiler_params=pltpu.CompilerParams(vmem_limit_bytes=28 * MIB),
        cost_estimate=pl.CostEstimate(
            flops=12 * inner * angles * count * axial,
            bytes_accessed=12 * inner * angles * axial,
            transcendentals=0,
        ),
        name="deposit_middle",
    )(ids, spring, in_hbm(low_edge))


def derivative_matrix(stencil_ref, inverse_ref):
    rows = inverse_ref.shape[1]
    wide = rows + 2 * HALO
    offset = iota((wide, rows), 0) - iota((wide, rows), 1)
    band = jnp.zeros((wide, rows), F32)
    for s in range(2 * HALO + 1):
        band = band + jnp.where(offset == s, stencil_ref[s : s + 1, :], 0.0)
    small = lax.dot_general(
        inverse_ref[...],
        band,
        (((1,), (1,)), ((), ())),
        precision=PRECISE,
        preferred_element_type=F32,
    )
    tall = jnp.where(iota((rows * SUB, rows), 0) // SUB == iota((rows * SUB, rows), 1), 1.0, 0.0)
    flat = jnp.where(iota((wide, wide * SUB), 1) // SUB == iota((wide, wide * SUB), 0), 1.0, 0.0)
    big = (rows * SUB, wide * SUB)
    same = iota(big, 0) % SUB == iota(big, 1) % SUB
    parts = []
    for part in split(small):
        spread = dot(dot(tall.astype(BF16), part).astype(BF16), flat.astype(BF16))
        parts.append(jnp.where(same, spread, 0.0).astype(BF16))
    return jnp.concatenate(parts, axis=0)


def derive_kernel(
    stencil_ref,
    inverse_ref,
    low_ref,
    velocity_ref,
    low_edge_ref,
    middle_ref,
    high_edge_ref,
    high_ref,
    piece_ref,
    grad_ref,
    force_ref,
    passed_ref,
    matrix_ref,
):
    radii, angles, axial = velocity_ref.shape[1:]

    passed_ref[...] = piece_ref[...]

    @pl.when(pl.program_id(0) == 0)
    def _():
        matrix_ref[...] = derivative_matrix(stencil_ref, inverse_ref)

    group = radii * SUB

    for i in range(angles // SUB):
        at = pl.ds(i * SUB, SUB)
        columns = []
        own = [
            [velocity_ref],
            [low_edge_ref.at[0], middle_ref, high_edge_ref.at[0]],
        ]
        for f in range(2):
            refs = [low_ref.at[f]] + own[f] + [high_ref.at[f]]
            for c in range(3):
                value = jnp.concatenate([ref[c, :, at, :] for ref in refs], axis=0)
                columns.append(value.reshape((radii + 2 * HALO) * SUB, axial))
        field_high, field_low = split(jnp.concatenate(columns, axis=1))
        result = dot3(matrix_ref[...], field_high, field_low)
        for c in range(3):
            force = TIME_STEP * result[:, (3 + c) * axial : (4 + c) * axial]
            force_ref[c, :, at, :] = force.reshape(radii, SUB, axial)
        turned_high, turned_low = split(result[:, : 3 * axial].T)
        cols = pl.ds(i * group, group)
        grad_ref[: 3 * axial, cols] = turned_high
        grad_ref[3 * axial :, cols] = turned_low

def derive(stencil, inverse, low, velocity, stress, high, piece):
    low_edge, middle, high_edge = stress
    radii, angles, axial = velocity.shape[1:]
    part = 2 * SUB
    steps = angles // part
    assert piece.shape[0] % steps == 0
    piece_block = pl.BlockSpec((piece.shape[0] // steps, angles, axial), lambda i: (i, 0, 0))

    def block(count, first=None):
        if first is None:
            return pl.BlockSpec((3, count, part, axial), lambda i: (0, 0, i, 0))
        return pl.BlockSpec((2 - first, 3, count, part, axial), lambda i: (first, 0, 0, i, 0))

    return pl.pallas_call(
        derive_kernel,
        grid=(steps,),
        in_specs=[
            pl.BlockSpec(stencil.shape, lambda i: (0, 0)),
            pl.BlockSpec(inverse.shape, lambda i: (0, 0)),
            block(HALO, 0),
            block(radii),
            block(HALO, 1),
            block(radii - 2 * HALO),
            block(HALO, 1),
            block(HALO, 0),
            piece_block,
        ],
        out_specs=[
            pl.BlockSpec((6 * axial, radii * part), lambda i: (0, i)),
            block(radii),
            piece_block,
        ],
        out_shape=[
            pltpu.HBM((6 * axial, radii * angles), BF16),
            pltpu.HBM(velocity.shape, F32),
            pltpu.HBM(piece.shape, F32),
        ],
        scratch_shapes=[
            pltpu.VMEM((2 * radii * SUB, (radii + 2 * HALO) * SUB), BF16),
        ],
        compiler_params=pltpu.CompilerParams(vmem_limit_bytes=28 * MIB),
        cost_estimate=pl.CostEstimate(
            flops=3600 * radii * radii * angles * axial // 8,
            bytes_accessed=40 * radii * angles * axial,
            transcendentals=0,
        ),
        name="derive",
    )(
        stencil,
        inverse,
        in_vmem(low),
        in_hbm(velocity),
        in_hbm(low_edge),
        in_hbm(middle),
        in_hbm(high_edge),
        in_vmem(high),
        in_hbm(piece),
    )


def move_kernel(grad_ref, ids_ref, spring_ref, noise_ref, moved_ref, *, angles):
    axial, cells = grad_ref.shape[0] // 6, grad_ref.shape[1]
    group = cells // angles * SUB

    count = spring_ref.shape[3]
    part = min(count, 512)

    def read(i, carry):
        at = pl.ds(pl.multiple_of(i * part, part), part)
        plane = ids_ref[0, 0, :, at]
        radius, angle = plane // angles, plane % angles
        column = (angle // SUB) * group + radius * SUB + angle % SUB
        hot = jnp.where(iota((cells, part), 0) == column, 1.0, 0.0).astype(BF16)
        picked = dot(grad_ref[...], hot)
        here = iota((axial, part), 0) == ids_ref[1, 0, :, at]
        q = [spring_ref[c, 0, :, at] for c in range(3)]
        stretch_sq = q[0] * q[0] + q[1] * q[1] + q[2] * q[2]
        factor = 1.0 / (1.0 - stretch_sq / MAX_STRETCH)
        for c in range(3):
            value = (
                picked[c * axial : (c + 1) * axial] + picked[(3 + c) * axial : (4 + c) * axial]
            )
            shear = jnp.sum(jnp.where(here, value, 0.0), axis=0, keepdims=True)
            moved_ref[c, 0, :, at] = (
                q[c]
                + TIME_STEP * (shear * q[0] - 0.5 * factor * q[c])
                + math.sqrt(TIME_STEP) * noise_ref[c, 0, :, at]
            )
        return carry

    lax.fori_loop(0, count // part, read, 0)


def move(grad, ids, spring, noise, angles):
    cells = grad.shape[1]
    whole = pl.BlockSpec(memory_space=pltpu.VMEM)
    return pl.pallas_call(
        functools.partial(move_kernel, angles=angles),
        in_specs=[whole] * 4,
        out_specs=whole,
        out_shape=jax.ShapeDtypeStruct(spring.shape, F32),
        compiler_params=pltpu.CompilerParams(vmem_limit_bytes=24 * MIB),
        cost_estimate=pl.CostEstimate(
            flops=2 * grad.size * spring.shape[3],
            bytes_accessed=2 * grad.size,
            transcendentals=0,
        ),
        name="move",
    )(in_hbm(grad), ids, spring, noise)


def fourier_tables(all_angles):
    half = all_angles // 2
    row = np.arange(half)
    quarter = half // 2
    waves = [
        np.where(row <= quarter, 2 * row, 2 * (row - quarter)),
        np.where(row < quarter, 2 * row + 1, 2 * (row - quarter) + 1),
    ]
    cosine = [row <= quarter, row < quarter]
    tables = []
    for wave, even in zip(waves, cosine):
        phase = (wave[:, None] * row[None, :]) % all_angles
        angle = phase * (2.0 * math.pi / all_angles)
        table = np.where(even[:, None], np.cos(angle), np.sin(angle))
        weight = np.where((wave == 0) | (wave == half), 1.0, 2.0) / all_angles
        for value in (table, table.T * weight[None, :]):
            value = value.astype(np.float32)
            high = value.astype(BF16)
            low = (value - high.astype(np.float32)).astype(BF16)
            tables.append(np.concatenate([high, low], axis=0))
    return np.stack(tables)


def solve_kernel(coef_ref, me_ref, tables_ref, *refs, extra):
    in_ref, refs = refs[extra], refs[extra + 1 :]
    blocks, rows, angles, axial = in_ref.shape
    out_refs = refs[:blocks]
    table_ref, done_ref, table_sems, out_sems = refs[blocks:]
    half = blocks * angles // 2
    quarter = half // 2
    part = math.gcd(rows, 2)
    loads = [
        pltpu.make_async_copy(tables_ref.at[i], table_ref.at[i], table_sems.at[i])
        for i in range(4)
    ]
    for copy in loads:
        copy.start()

    base = me_ref[0] * rows
    lane = iota((1, axial), 1)
    coef = jnp.zeros((1, axial), F32)
    for q in range(rows):
        coef = jnp.where(lane == q, coef_ref[lax.rem(base + q, coef_ref.shape[0])], coef)
    row = iota((half, axial), 0)
    waves = [
        jnp.where(row <= quarter, 2 * row, 2 * (row - quarter)),
        jnp.where(row < quarter, 2 * row + 1, 2 * (row - quarter) + 1),
    ]
    damping = [1.0 / (1.0 + coef * (wave * wave).astype(F32)) for wave in waves]

    stores = []
    for g in range(rows // part):
        chosen = range(g * part, (g + 1) * part)
        near = [in_ref[: blocks // 2, q].reshape(half, axial) for q in chosen]
        far = [in_ref[blocks // 2 :, q].reshape(half, axial) for q in chosen]
        results = []
        for odd in range(2):
            field = jnp.concatenate([a - b if odd else a + b for a, b in zip(near, far)], axis=1)
            if g == 0:
                loads[2 * odd].wait()
            spectrum = dot3(table_ref[2 * odd], *split(field))
            scale = [
                jnp.broadcast_to(damping[odd][:, q : q + 1], (half, axial)) for q in chosen
            ]
            if g == 0:
                loads[2 * odd + 1].wait()
            damped = spectrum * jnp.concatenate(scale, axis=1)
            results.append(dot3(table_ref[2 * odd + 1], *split(damped)))
        for i, q in enumerate(chosen):
            even, odd = [value[:, i * axial : (i + 1) * axial] for value in results]
            done_ref[: blocks // 2, q] = (even + odd).reshape(blocks // 2, angles, axial)
            done_ref[blocks // 2 :, q] = (even - odd).reshape(blocks // 2, angles, axial)
        at = pl.ds(g * part, part)
        for s in range(blocks):
            stores.append(
                pltpu.make_async_copy(
                    done_ref.at[me_ref[0] ^ s, at], out_refs[s].at[at], out_sems.at[g, s]
                )
            )
            stores[-1].start()
    for copy in stores:
        copy.wait()


def solve(coef, me, field, after):
    blocks, rows, angles, axial = field.shape
    all_angles = blocks * angles
    tables = fourier_tables(all_angles)
    smem = pl.BlockSpec(memory_space=pltpu.SMEM)
    whole = pl.BlockSpec(memory_space=pltpu.VMEM)
    unread = pl.BlockSpec(memory_space=pl.ANY)
    return pl.pallas_call(
        functools.partial(solve_kernel, extra=len(after)),
        in_specs=[smem, smem, unread] + [unread] * len(after) + [whole],
        out_specs=[unread] * blocks,
        out_shape=[pltpu.HBM(field.shape[1:], F32)] * blocks,
        scratch_shapes=[
            pltpu.VMEM(tables.shape, BF16),
            pltpu.VMEM(field.shape, F32),
            pltpu.SemaphoreType.DMA((4,)),
            pltpu.SemaphoreType.DMA((rows // math.gcd(rows, 2), blocks)),
        ],
        compiler_params=pltpu.CompilerParams(vmem_limit_bytes=28 * MIB),
        cost_estimate=pl.CostEstimate(
            flops=12 * all_angles * all_angles * rows * axial,
            bytes_accessed=8 * all_angles * rows * axial,
            transcendentals=0,
        ),
        name="solve",
    )(
        coef,
        me,
        in_hbm(jnp.asarray(tables)),
        *after,
        in_vmem(field),
    )


def join_kernel(me_ref, force_ref, *refs, first, given):
    count = len(refs) - 4 - given
    piece_refs, refs = refs[:count], refs[count + given :]
    out_ref, sum_ref, in_sems, out_sems = refs
    rows = sum_ref.shape[1]
    reads, writes = [], []
    for i in range(count):
        at = pl.ds((me_ref[0] ^ (first + i)) * rows, rows)
        reads.append(pltpu.make_async_copy(force_ref.at[at], sum_ref.at[i], in_sems.at[i]))
        writes.append(pltpu.make_async_copy(sum_ref.at[i], out_ref.at[at], out_sems.at[i]))
    for copy in reads:
        copy.start()
    for i in range(count):
        reads[i].wait()
        sum_ref[i] = sum_ref[i] + piece_refs[i][...]
        writes[i].start()
    for copy in writes:
        copy.wait()


def join(me, force, pieces, first, result=None):
    rows, angles, axial = pieces[0].shape
    count = len(pieces)
    given = [] if result is None else [in_hbm(result)]
    whole = pl.BlockSpec(memory_space=pltpu.VMEM)
    away = pl.BlockSpec(memory_space=pl.ANY)
    return pl.pallas_call(
        functools.partial(join_kernel, first=first, given=len(given)),
        in_specs=[pl.BlockSpec(memory_space=pltpu.SMEM), away]
        + [whole] * count
        + [away] * len(given),
        out_specs=away,
        out_shape=pltpu.HBM(force.shape, F32),
        input_output_aliases={2 + count: 0} if given else {},
        scratch_shapes=[
            pltpu.VMEM((count, rows, angles, axial), F32),
            pltpu.SemaphoreType.DMA((count,)),
            pltpu.SemaphoreType.DMA((count,)),
        ],
        compiler_params=pltpu.CompilerParams(vmem_limit_bytes=14 * MIB),
        cost_estimate=pl.CostEstimate(
            flops=count * rows * angles * axial,
            bytes_accessed=12 * count * rows * angles * axial,
            transcendentals=0,
        ),
        name="join",
    )(me, in_hbm(force), *pieces, *given)


def exchange(pieces):
    count = len(pieces)
    received = [pieces[0]] + [None] * (count - 1)
    order = list(range(2, count, 2)) + list(range(3, count, 2)) + [1]
    for s in order:
        received[s] = lax.ppermute(pieces[s], "az", [(i, i ^ s) for i in range(count)])
    return received


def from_neighbours(low_edge, high_edge):
    count = lax.axis_size("rad")
    forward = [(i, i + 1) for i in range(count - 1)]
    backward = [(target, source) for source, target in forward]
    low = lax.ppermute(high_edge, "rad", forward)
    high = lax.ppermute(low_edge, "rad", backward)
    return low, high


def per_device(velocity, dumbbells, cell_ids, brownian, stencil_coef, block_inverse, azim_coef):
    _, radii, angles, axial = velocity.shape
    az = lax.axis_size("az")
    rows = 3 * radii // az
    pieces = velocity.reshape(az, rows, angles, axial)
    gathered = lax.all_to_all(pieces, "az", 0, 0, tiled=True)
    low_edge, high_edge = deposit_edges(cell_ids, dumbbells, velocity)
    low, high = from_neighbours(low_edge, high_edge)
    middle = deposit_middle(cell_ids, dumbbells, low_edge, velocity.shape)
    stress = (low_edge, middle, high_edge)
    me = lax.axis_index("az").astype(jnp.int32).reshape(1)
    solved = solve(azim_coef, me, gathered, (in_vmem(low), in_vmem(high), in_hbm(middle)))
    grad, force, passed = derive(
        stencil_coef, block_inverse, low, velocity, stress, high, solved[-1]
    )
    pieces = exchange(list(solved[:-1]) + [passed])
    moved = move(grad, cell_ids, dumbbells, brownian, angles)
    lines = (3 * radii, angles, axial)
    force = force.reshape(lines)
    early = len(pieces) * 3 // 8
    result = join(me, force, pieces[:early], 0)
    result = join(me, force, [in_vmem(piece) for piece in pieces[early:]], early, result)
    return result.reshape(velocity.shape), moved


def solution(mesh):
    placed = (
        P(None, "rad", "az", None),
        P(None, "rad", "az", None),
        P(None, "rad", "az", None),
        P(None, "rad", "az", None),
        P(None, "rad"),
        P("rad", None),
        P("rad"),
    )
    return jax.shard_map(
        per_device,
        mesh=mesh,
        in_specs=placed,
        out_specs=(P(None, "rad", "az", None), P(None, "rad", "az", None)),
        check_vma=False,
    )
```

```python
import functools
import functools
import math

import jax
import jax.numpy as jnp
import numpy as np
from jax import lax
from jax.experimental import pallas as pl
from jax.experimental.pallas import tpu as pltpu
from jax.sharding import PartitionSpec as P

TIME_STEP = 0.05
MAX_STRETCH = 10.0
STRESS_SCALE = 4.0
PRECISE = lax.Precision.HIGHEST
HALO = 4
SUB = 8
MIB = 1024 * 1024
F32 = jnp.float32
BF16 = jnp.bfloat16


def split(value):
    high = value.astype(BF16)
    return high, (value - high.astype(F32)).astype(BF16)


def dot(a, b):
    return jnp.dot(a, b, preferred_element_type=F32)


def dot3(stacked, b_high, b_low):
    rows = stacked.shape[0] // 2
    both = dot(stacked, b_high)
    return both[:rows] + both[rows:] + dot(stacked[:rows], b_low)

def partners(count):
    return [s for s in (0, 1, 2, 4, 6, 5, 7, 3) if s < count] + list(range(8, count))


def in_hbm(value):
    return pltpu.with_memory_space_constraint(value, pltpu.HBM)


def in_vmem(value):
    return pltpu.with_memory_space_constraint(value, pltpu.VMEM)


def iota(shape, dim):
    return lax.broadcasted_iota(jnp.int32, shape, dim)


def weigh(ids_ref, spring_ref, weight_ref):
    axial = weight_ref.shape[0] // 6
    count = weight_ref.shape[1]
    q = [spring_ref[c, 0] for c in range(3)]
    stretch_sq = q[0] * q[0] + q[1] * q[1] + q[2] * q[2]
    factor = 1.0 / (1.0 - stretch_sq / MAX_STRETCH)
    here = iota((axial, count), 0) == ids_ref[1, 0]
    for c in range(3):
        weight = STRESS_SCALE * factor * q[0] * q[c]
        high = weight.astype(BF16).astype(F32)
        weight_ref[c * axial : (c + 1) * axial, :] = jnp.where(here, high, 0.0).astype(BF16)
        weight_ref[(3 + c) * axial : (4 + c) * axial, :] = jnp.where(
            here, weight - high, 0.0
        ).astype(BF16)


def gather_rows(ids_ref, weight_ref, first_row, rows):
    axial = weight_ref.shape[0] // 6
    count = weight_ref.shape[1]
    hot = jnp.where(iota((rows, count), 0) + first_row == ids_ref[0, 0], 1.0, 0.0).astype(BF16)
    both = lax.dot_general(
        hot, weight_ref[...], (((1,), (1,)), ((), ())), preferred_element_type=F32
    )
    return [
        both[:, c * axial : (c + 1) * axial] + both[:, (3 + c) * axial : (4 + c) * axial]
        for c in range(3)
    ]


def edge_kernel(ids_ref, spring_ref, first_ref, last_ref, low_ref, high_ref, weight_ref, *, radii):
    _, _, _, angles, axial = low_ref.shape
    weigh(ids_ref, spring_ref, weight_ref)
    for field_ref, out_ref, radius in (
        (first_ref, low_ref, 0),
        (last_ref, high_ref, radii - HALO),
    ):
        out_ref[0] = field_ref[...]
        values = gather_rows(ids_ref, weight_ref, radius * angles, HALO * angles)
        for c in range(3):
            out_ref[1, c] = values[c].reshape(HALO, angles, axial)


def middle_kernel(ids_ref, spring_ref, stress_ref, weight_ref):
    step = pl.program_id(0)
    _, radii, angles, axial = stress_ref.shape

    @pl.when(step == 0)
    def _():
        weigh(ids_ref, spring_ref, weight_ref)

    rows = radii * angles
    values = gather_rows(ids_ref, weight_ref, HALO * angles + step * rows, rows)
    for c in range(3):
        stress_ref[c] = values[c].reshape(radii, angles, axial)


def deposit_edges(ids, spring, velocity):
    _, radii, angles, axial = velocity.shape
    count = ids.shape[3]
    edge = (2, 3, HALO, angles, axial)
    edge_block = (3, HALO, angles, axial)
    whole = pl.BlockSpec(memory_space=pltpu.VMEM)
    return pl.pallas_call(
        functools.partial(edge_kernel, radii=radii),
        grid=(1,),
        in_specs=[
            whole,
            whole,
            pl.BlockSpec(edge_block, lambda i: (0, 0, 0, 0)),
            pl.BlockSpec(edge_block, lambda i: (0, radii // HALO - 1, 0, 0)),
        ],
        out_specs=[pl.BlockSpec(edge, lambda i: (0, 0, 0, 0, 0))] * 2,
        out_shape=[pltpu.HBM(edge, F32)] * 2,
        scratch_shapes=[pltpu.VMEM((6 * axial, count), BF16)],
        compiler_params=pltpu.CompilerParams(vmem_limit_bytes=28 * MIB),
        cost_estimate=pl.CostEstimate(
            flops=24 * HALO * angles * count * axial,
            bytes_accessed=96 * HALO * angles * axial,
            transcendentals=0,
        ),
        name="deposit_edges",
    )(ids, spring, in_hbm(velocity), in_hbm(velocity))


def deposit_middle(ids, spring, low_edge, shape):
    _, radii, angles, axial = shape
    count = ids.shape[3]
    inner = radii - 2 * HALO
    part = math.gcd(inner, max(1, 512 // angles))
    whole = pl.BlockSpec(memory_space=pltpu.VMEM)
    return pl.pallas_call(
        lambda ids_ref, spring_ref, _, *refs: middle_kernel(ids_ref, spring_ref, *refs),
        grid=(inner // part,),
        in_specs=[whole, whole, pl.BlockSpec(memory_space=pl.ANY)],
        out_specs=pl.BlockSpec((3, part, angles, axial), lambda i: (0, i, 0, 0)),
        out_shape=pltpu.HBM((3, inner, angles, axial), F32),
        scratch_shapes=[pltpu.VMEM((6 * axial, count), BF16)],
        compiler_params=pltpu.CompilerParams(vmem_limit_bytes=28 * MIB),
        cost_estimate=pl.CostEstimate(
            flops=12 * inner * angles * count * axial,
            bytes_accessed=12 * inner * angles * axial,
            transcendentals=0,
        ),
        name="deposit_middle",
    )(ids, spring, in_hbm(low_edge))


def derivative_matrix(stencil_ref, inverse_ref):
    rows = inverse_ref.shape[1]
    wide = rows + 2 * HALO
    offset = iota((wide, rows), 0) - iota((wide, rows), 1)
    band = jnp.zeros((wide, rows), F32)
    for s in range(2 * HALO + 1):
        band = band + jnp.where(offset == s, stencil_ref[s : s + 1, :], 0.0)
    small = lax.dot_general(
        inverse_ref[...],
        band,
        (((1,), (1,)), ((), ())),
        precision=PRECISE,
        preferred_element_type=F32,
    )
    tall = jnp.where(iota((rows * SUB, rows), 0) // SUB == iota((rows * SUB, rows), 1), 1.0, 0.0)
    flat = jnp.where(iota((wide, wide * SUB), 1) // SUB == iota((wide, wide * SUB), 0), 1.0, 0.0)
    big = (rows * SUB, wide * SUB)
    same = iota(big, 0) % SUB == iota(big, 1) % SUB
    parts = []
    for part in split(small):
        spread = dot(dot(tall.astype(BF16), part).astype(BF16), flat.astype(BF16))
        parts.append(jnp.where(same, spread, 0.0).astype(BF16))
    return jnp.concatenate(parts, axis=0)


def derive_kernel(
    stencil_ref,
    inverse_ref,
    low_ref,
    velocity_ref,
    low_edge_ref,
    middle_ref,
    high_edge_ref,
    high_ref,
    piece_ref,
    grad_ref,
    force_ref,
    passed_ref,
    matrix_ref,
):
    radii, angles, axial = velocity_ref.shape[1:]

    passed_ref[...] = piece_ref[...]

    @pl.when(pl.program_id(0) == 0)
    def _():
        matrix_ref[...] = derivative_matrix(stencil_ref, inverse_ref)

    group = radii * SUB

    for i in range(angles // SUB):
        at = pl.ds(i * SUB, SUB)
        columns = []
        own = [
            [velocity_ref],
            [low_edge_ref.at[0], middle_ref, high_edge_ref.at[0]],
        ]
        for f in range(2):
            refs = [low_ref.at[f]] + own[f] + [high_ref.at[f]]
            for c in range(3):
                value = jnp.concatenate([ref[c, :, at, :] for ref in refs], axis=0)
                columns.append(value.reshape((radii + 2 * HALO) * SUB, axial))
        field_high, field_low = split(jnp.concatenate(columns, axis=1))
        result = dot3(matrix_ref[...], field_high, field_low)
        for c in range(3):
            force = TIME_STEP * result[:, (3 + c) * axial : (4 + c) * axial]
            force_ref[c, :, at, :] = force.reshape(radii, SUB, axial)
        turned_high, turned_low = split(result[:, : 3 * axial].T)
        cols = pl.ds(i * group, group)
        grad_ref[: 3 * axial, cols] = turned_high
        grad_ref[3 * axial :, cols] = turned_low

def derive(stencil, inverse, low, velocity, stress, high, piece):
    low_edge, middle, high_edge = stress
    radii, angles, axial = velocity.shape[1:]
    part = 2 * SUB
    steps = angles // part
    assert piece.shape[0] % steps == 0
    piece_block = pl.BlockSpec((piece.shape[0] // steps, angles, axial), lambda i: (i, 0, 0))

    def block(count, first=None):
        if first is None:
            return pl.BlockSpec((3, count, part, axial), lambda i: (0, 0, i, 0))
        return pl.BlockSpec((2 - first, 3, count, part, axial), lambda i: (first, 0, 0, i, 0))

    return pl.pallas_call(
        derive_kernel,
        grid=(steps,),
        in_specs=[
            pl.BlockSpec(stencil.shape, lambda i: (0, 0)),
            pl.BlockSpec(inverse.shape, lambda i: (0, 0)),
            block(HALO, 0),
            block(radii),
            block(HALO, 1),
            block(radii - 2 * HALO),
            block(HALO, 1),
            block(HALO, 0),
            piece_block,
        ],
        out_specs=[
            pl.BlockSpec((6 * axial, radii * part), lambda i: (0, i)),
            block(radii),
            piece_block,
        ],
        out_shape=[
            pltpu.HBM((6 * axial, radii * angles), BF16),
            pltpu.HBM(velocity.shape, F32),
            pltpu.HBM(piece.shape, F32),
        ],
        scratch_shapes=[
            pltpu.VMEM((2 * radii * SUB, (radii + 2 * HALO) * SUB), BF16),
        ],
        compiler_params=pltpu.CompilerParams(vmem_limit_bytes=28 * MIB),
        cost_estimate=pl.CostEstimate(
            flops=3600 * radii * radii * angles * axial // 8,
            bytes_accessed=40 * radii * angles * axial,
            transcendentals=0,
        ),
        name="derive",
    )(
        stencil,
        inverse,
        in_vmem(low),
        in_hbm(velocity),
        in_hbm(low_edge),
        in_hbm(middle),
        in_hbm(high_edge),
        in_vmem(high),
        in_hbm(piece),
    )


def move_kernel(grad_ref, ids_ref, spring_ref, noise_ref, moved_ref, *, angles):
    axial, cells = grad_ref.shape[0] // 6, grad_ref.shape[1]
    group = cells // angles * SUB

    count = spring_ref.shape[3]
    part = min(count, 512)

    def read(i, carry):
        at = pl.ds(pl.multiple_of(i * part, part), part)
        plane = ids_ref[0, 0, :, at]
        radius, angle = plane // angles, plane % angles
        column = (angle // SUB) * group + radius * SUB + angle % SUB
        hot = jnp.where(iota((cells, part), 0) == column, 1.0, 0.0).astype(BF16)
        picked = dot(grad_ref[...], hot)
        here = iota((axial, part), 0) == ids_ref[1, 0, :, at]
        q = [spring_ref[c, 0, :, at] for c in range(3)]
        stretch_sq = q[0] * q[0] + q[1] * q[1] + q[2] * q[2]
        factor = 1.0 / (1.0 - stretch_sq / MAX_STRETCH)
        for c in range(3):
            value = (
                picked[c * axial : (c + 1) * axial] + picked[(3 + c) * axial : (4 + c) * axial]
            )
            shear = jnp.sum(jnp.where(here, value, 0.0), axis=0, keepdims=True)
            moved_ref[c, 0, :, at] = (
                q[c]
                + TIME_STEP * (shear * q[0] - 0.5 * factor * q[c])
                + math.sqrt(TIME_STEP) * noise_ref[c, 0, :, at]
            )
        return carry

    lax.fori_loop(0, count // part, read, 0)


def move(grad, ids, spring, noise, angles):
    cells = grad.shape[1]
    whole = pl.BlockSpec(memory_space=pltpu.VMEM)
    return pl.pallas_call(
        functools.partial(move_kernel, angles=angles),
        in_specs=[whole] * 4,
        out_specs=whole,
        out_shape=jax.ShapeDtypeStruct(spring.shape, F32),
        compiler_params=pltpu.CompilerParams(vmem_limit_bytes=24 * MIB),
        cost_estimate=pl.CostEstimate(
            flops=2 * grad.size * spring.shape[3],
            bytes_accessed=2 * grad.size,
            transcendentals=0,
        ),
        name="move",
    )(in_hbm(grad), ids, spring, noise)


def fourier_tables(all_angles):
    half = all_angles // 2
    row = np.arange(half)
    quarter = half // 2
    waves = [
        np.where(row <= quarter, 2 * row, 2 * (row - quarter)),
        np.where(row < quarter, 2 * row + 1, 2 * (row - quarter) + 1),
    ]
    cosine = [row <= quarter, row < quarter]
    tables = []
    for wave, even in zip(waves, cosine):
        phase = (wave[:, None] * row[None, :]) % all_angles
        angle = phase * (2.0 * math.pi / all_angles)
        table = np.where(even[:, None], np.cos(angle), np.sin(angle))
        weight = np.where((wave == 0) | (wave == half), 1.0, 2.0) / all_angles
        for value in (table, table.T * weight[None, :]):
            value = value.astype(np.float32)
            high = value.astype(BF16)
            low = (value - high.astype(np.float32)).astype(BF16)
            tables.append(np.concatenate([high, low], axis=0))
    return np.stack(tables)


def solve_kernel(coef_ref, me_ref, tables_ref, *refs, extra):
    in_ref, refs = refs[extra], refs[extra + 1 :]
    blocks, rows, angles, axial = in_ref.shape
    out_refs = refs[:blocks]
    table_ref, done_ref, table_sems, out_sems = refs[blocks:]
    half = blocks * angles // 2
    quarter = half // 2
    part = math.gcd(rows, 2)
    loads = [
        pltpu.make_async_copy(tables_ref.at[i], table_ref.at[i], table_sems.at[i])
        for i in range(4)
    ]
    for copy in loads:
        copy.start()

    base = me_ref[0] * rows
    lane = iota((1, axial), 1)
    coef = jnp.zeros((1, axial), F32)
    for q in range(rows):
        coef = jnp.where(lane == q, coef_ref[lax.rem(base + q, coef_ref.shape[0])], coef)
    row = iota((half, axial), 0)
    waves = [
        jnp.where(row <= quarter, 2 * row, 2 * (row - quarter)),
        jnp.where(row < quarter, 2 * row + 1, 2 * (row - quarter) + 1),
    ]
    damping = [1.0 / (1.0 + coef * (wave * wave).astype(F32)) for wave in waves]

    stores = []
    for g in range(rows // part):
        chosen = range(g * part, (g + 1) * part)
        near = [in_ref[: blocks // 2, q].reshape(half, axial) for q in chosen]
        far = [in_ref[blocks // 2 :, q].reshape(half, axial) for q in chosen]
        results = []
        for odd in range(2):
            field = jnp.concatenate([a - b if odd else a + b for a, b in zip(near, far)], axis=1)
            if g == 0:
                loads[2 * odd].wait()
            spectrum = dot3(table_ref[2 * odd], *split(field))
            scale = [
                jnp.broadcast_to(damping[odd][:, q : q + 1], (half, axial)) for q in chosen
            ]
            if g == 0:
                loads[2 * odd + 1].wait()
            damped = spectrum * jnp.concatenate(scale, axis=1)
            results.append(dot3(table_ref[2 * odd + 1], *split(damped)))
        for i, q in enumerate(chosen):
            even, odd = [value[:, i * axial : (i + 1) * axial] for value in results]
            done_ref[: blocks // 2, q] = (even + odd).reshape(blocks // 2, angles, axial)
            done_ref[blocks // 2 :, q] = (even - odd).reshape(blocks // 2, angles, axial)
        at = pl.ds(g * part, part)
        for s, partner in enumerate(partners(blocks)):
            stores.append(
                pltpu.make_async_copy(
                    done_ref.at[me_ref[0] ^ partner, at], out_refs[s].at[at], out_sems.at[g, s]
                )
            )
            stores[-1].start()
    for copy in stores:
        copy.wait()


def solve(coef, me, field, after):
    blocks, rows, angles, axial = field.shape
    all_angles = blocks * angles
    tables = fourier_tables(all_angles)
    smem = pl.BlockSpec(memory_space=pltpu.SMEM)
    whole = pl.BlockSpec(memory_space=pltpu.VMEM)
    unread = pl.BlockSpec(memory_space=pl.ANY)
    return pl.pallas_call(
        functools.partial(solve_kernel, extra=len(after)),
        in_specs=[smem, smem, unread] + [unread] * len(after) + [whole],
        out_specs=[unread] * blocks,
        out_shape=[pltpu.HBM(field.shape[1:], F32)] * blocks,
        scratch_shapes=[
            pltpu.VMEM(tables.shape, BF16),
            pltpu.VMEM(field.shape, F32),
            pltpu.SemaphoreType.DMA((4,)),
            pltpu.SemaphoreType.DMA((rows // math.gcd(rows, 2), blocks)),
        ],
        compiler_params=pltpu.CompilerParams(vmem_limit_bytes=28 * MIB),
        cost_estimate=pl.CostEstimate(
            flops=12 * all_angles * all_angles * rows * axial,
            bytes_accessed=8 * all_angles * rows * axial,
            transcendentals=0,
        ),
        name="solve",
    )(
        coef,
        me,
        in_hbm(jnp.asarray(tables)),
        *after,
        in_vmem(field),
    )


def join_kernel(me_ref, force_ref, *refs, first, given):
    count = len(refs) - 4 - given
    piece_refs, refs = refs[:count], refs[count + given :]
    out_ref, sum_ref, in_sems, out_sems = refs
    rows = sum_ref.shape[1]
    order = partners(force_ref.shape[0] // rows)
    reads, writes = [], []
    for i in range(count):
        at = pl.ds((me_ref[0] ^ order[first + i]) * rows, rows)
        reads.append(pltpu.make_async_copy(force_ref.at[at], sum_ref.at[i], in_sems.at[i]))
        writes.append(pltpu.make_async_copy(sum_ref.at[i], out_ref.at[at], out_sems.at[i]))
    for copy in reads:
        copy.start()
    for i in range(count):
        reads[i].wait()
        sum_ref[i] = sum_ref[i] + piece_refs[i][...]
        writes[i].start()
    for copy in writes:
        copy.wait()


def join(me, force, pieces, first, result=None):
    rows, angles, axial = pieces[0].shape
    count = len(pieces)
    given = [] if result is None else [in_hbm(result)]
    whole = pl.BlockSpec(memory_space=pltpu.VMEM)
    away = pl.BlockSpec(memory_space=pl.ANY)
    return pl.pallas_call(
        functools.partial(join_kernel, first=first, given=len(given)),
        in_specs=[pl.BlockSpec(memory_space=pltpu.SMEM), away]
        + [whole] * count
        + [away] * len(given),
        out_specs=away,
        out_shape=pltpu.HBM(force.shape, F32),
        input_output_aliases={2 + count: 0} if given else {},
        scratch_shapes=[
            pltpu.VMEM((count, rows, angles, axial), F32),
            pltpu.SemaphoreType.DMA((count,)),
            pltpu.SemaphoreType.DMA((count,)),
        ],
        compiler_params=pltpu.CompilerParams(vmem_limit_bytes=14 * MIB),
        cost_estimate=pl.CostEstimate(
            flops=count * rows * angles * axial,
            bytes_accessed=12 * count * rows * angles * axial,
            transcendentals=0,
        ),
        name="join",
    )(me, in_hbm(force), *pieces, *given)


def exchange(pieces):
    count = len(pieces)
    received = [pieces[0]]
    for piece, partner in list(zip(pieces, partners(count)))[1:]:
        received.append(lax.ppermute(piece, "az", [(i, i ^ partner) for i in range(count)]))
    return received


def from_neighbours(low_edge, high_edge):
    count = lax.axis_size("rad")
    forward = [(i, i + 1) for i in range(count - 1)]
    backward = [(target, source) for source, target in forward]
    low = lax.ppermute(high_edge, "rad", forward)
    high = lax.ppermute(low_edge, "rad", backward)
    return low, high


def per_device(velocity, dumbbells, cell_ids, brownian, stencil_coef, block_inverse, azim_coef):
    _, radii, angles, axial = velocity.shape
    az = lax.axis_size("az")
    rows = 3 * radii // az
    pieces = velocity.reshape(az, rows, angles, axial)
    gathered = lax.all_to_all(pieces, "az", 0, 0, tiled=True)
    low_edge, high_edge = deposit_edges(cell_ids, dumbbells, velocity)
    low, high = from_neighbours(low_edge, high_edge)
    middle = deposit_middle(cell_ids, dumbbells, low_edge, velocity.shape)
    stress = (low_edge, middle, high_edge)
    me = lax.axis_index("az").astype(jnp.int32).reshape(1)
    solved = solve(azim_coef, me, gathered, (in_vmem(low), in_vmem(high), in_hbm(middle)))
    grad, force, passed = derive(
        stencil_coef, block_inverse, low, velocity, stress, high, solved[-1]
    )
    pieces = exchange(list(solved[:-1]) + [passed])
    moved = move(grad, cell_ids, dumbbells, brownian, angles)
    lines = (3 * radii, angles, axial)
    force = force.reshape(lines)
    early = len(pieces) * 3 // 8
    result = join(me, force, pieces[:early], 0)
    result = join(me, force, [in_vmem(piece) for piece in pieces[early:]], early, result)
    return result.reshape(velocity.shape), moved


def solution(mesh):
    placed = (
        P(None, "rad", "az", None),
        P(None, "rad", "az", None),
        P(None, "rad", "az", None),
        P(None, "rad", "az", None),
        P(None, "rad"),
        P("rad", None),
        P("rad"),
    )
    return jax.shard_map(
        per_device,
        mesh=mesh,
        in_specs=placed,
        out_specs=(P(None, "rad", "az", None), P(None, "rad", "az", None)),
        check_vma=False,
    )
```

```python
import functools
import functools
import math

import jax
import jax.numpy as jnp
import numpy as np
from jax import lax
from jax.experimental import pallas as pl
from jax.experimental.pallas import tpu as pltpu
from jax.sharding import PartitionSpec as P

TIME_STEP = 0.05
MAX_STRETCH = 10.0
STRESS_SCALE = 4.0
PRECISE = lax.Precision.HIGHEST
HALO = 4
SUB = 8
MIB = 1024 * 1024
F32 = jnp.float32
BF16 = jnp.bfloat16


def split(value):
    high = value.astype(BF16)
    return high, (value - high.astype(F32)).astype(BF16)


def dot(a, b):
    return jnp.dot(a, b, preferred_element_type=F32)


def dot3(stacked, b_high, b_low):
    rows = stacked.shape[0] // 2
    both = dot(stacked, b_high)
    return both[:rows] + both[rows:] + dot(stacked[:rows], b_low)

def partners(count):
    return [s for s in (0, 1, 2, 4, 6, 5, 7, 3) if s < count] + list(range(8, count))


def in_hbm(value):
    return pltpu.with_memory_space_constraint(value, pltpu.HBM)


def in_vmem(value):
    return pltpu.with_memory_space_constraint(value, pltpu.VMEM)


def iota(shape, dim):
    return lax.broadcasted_iota(jnp.int32, shape, dim)


def weigh(ids_ref, spring_ref, weight_ref):
    axial = weight_ref.shape[0] // 6
    count = weight_ref.shape[1]
    q = [spring_ref[c, 0] for c in range(3)]
    stretch_sq = q[0] * q[0] + q[1] * q[1] + q[2] * q[2]
    factor = 1.0 / (1.0 - stretch_sq / MAX_STRETCH)
    here = iota((axial, count), 0) == ids_ref[1, 0]
    for c in range(3):
        weight = STRESS_SCALE * factor * q[0] * q[c]
        high = weight.astype(BF16).astype(F32)
        weight_ref[c * axial : (c + 1) * axial, :] = jnp.where(here, high, 0.0).astype(BF16)
        weight_ref[(3 + c) * axial : (4 + c) * axial, :] = jnp.where(
            here, weight - high, 0.0
        ).astype(BF16)


def gather_rows(ids_ref, weight_ref, first_row, rows):
    axial = weight_ref.shape[0] // 6
    count = weight_ref.shape[1]
    hot = jnp.where(iota((rows, count), 0) + first_row == ids_ref[0, 0], 1.0, 0.0).astype(BF16)
    both = lax.dot_general(
        hot, weight_ref[...], (((1,), (1,)), ((), ())), preferred_element_type=F32
    )
    return [
        both[:, c * axial : (c + 1) * axial] + both[:, (3 + c) * axial : (4 + c) * axial]
        for c in range(3)
    ]


def edge_kernel(ids_ref, spring_ref, first_ref, last_ref, low_ref, high_ref, weight_ref, *, radii):
    _, _, _, angles, axial = low_ref.shape
    weigh(ids_ref, spring_ref, weight_ref)
    for field_ref, out_ref, radius in (
        (first_ref, low_ref, 0),
        (last_ref, high_ref, radii - HALO),
    ):
        out_ref[0] = field_ref[...]
        values = gather_rows(ids_ref, weight_ref, radius * angles, HALO * angles)
        for c in range(3):
            out_ref[1, c] = values[c].reshape(HALO, angles, axial)


def middle_kernel(ids_ref, spring_ref, stress_ref, weight_ref):
    step = pl.program_id(0)
    _, radii, angles, axial = stress_ref.shape

    @pl.when(step == 0)
    def _():
        weigh(ids_ref, spring_ref, weight_ref)

    rows = radii * angles
    values = gather_rows(ids_ref, weight_ref, HALO * angles + step * rows, rows)
    for c in range(3):
        stress_ref[c] = values[c].reshape(radii, angles, axial)


def deposit_edges(ids, spring, velocity):
    _, radii, angles, axial = velocity.shape
    count = ids.shape[3]
    edge = (2, 3, HALO, angles, axial)
    edge_block = (3, HALO, angles, axial)
    whole = pl.BlockSpec(memory_space=pltpu.VMEM)
    return pl.pallas_call(
        functools.partial(edge_kernel, radii=radii),
        grid=(1,),
        in_specs=[
            whole,
            whole,
            pl.BlockSpec(edge_block, lambda i: (0, 0, 0, 0)),
            pl.BlockSpec(edge_block, lambda i: (0, radii // HALO - 1, 0, 0)),
        ],
        out_specs=[pl.BlockSpec(edge, lambda i: (0, 0, 0, 0, 0))] * 2,
        out_shape=[pltpu.HBM(edge, F32)] * 2,
        scratch_shapes=[pltpu.VMEM((6 * axial, count), BF16)],
        compiler_params=pltpu.CompilerParams(vmem_limit_bytes=28 * MIB),
        cost_estimate=pl.CostEstimate(
            flops=24 * HALO * angles * count * axial,
            bytes_accessed=96 * HALO * angles * axial,
            transcendentals=0,
        ),
        name="deposit_edges",
    )(ids, spring, in_hbm(velocity), in_hbm(velocity))


def deposit_middle(ids, spring, low_edge, shape):
    _, radii, angles, axial = shape
    count = ids.shape[3]
    inner = radii - 2 * HALO
    part = math.gcd(inner, max(1, 512 // angles))
    whole = pl.BlockSpec(memory_space=pltpu.VMEM)
    return pl.pallas_call(
        lambda ids_ref, spring_ref, _, *refs: middle_kernel(ids_ref, spring_ref, *refs),
        grid=(inner // part,),
        in_specs=[whole, whole, pl.BlockSpec(memory_space=pl.ANY)],
        out_specs=pl.BlockSpec((3, part, angles, axial), lambda i: (0, i, 0, 0)),
        out_shape=pltpu.HBM((3, inner, angles, axial), F32),
        scratch_shapes=[pltpu.VMEM((6 * axial, count), BF16)],
        compiler_params=pltpu.CompilerParams(vmem_limit_bytes=28 * MIB),
        cost_estimate=pl.CostEstimate(
            flops=12 * inner * angles * count * axial,
            bytes_accessed=12 * inner * angles * axial,
            transcendentals=0,
        ),
        name="deposit_middle",
    )(ids, spring, in_hbm(low_edge))


def derivative_matrix(stencil_ref, inverse_ref):
    rows = inverse_ref.shape[1]
    wide = rows + 2 * HALO
    offset = iota((wide, rows), 0) - iota((wide, rows), 1)
    band = jnp.zeros((wide, rows), F32)
    for s in range(2 * HALO + 1):
        band = band + jnp.where(offset == s, stencil_ref[s : s + 1, :], 0.0)
    small = lax.dot_general(
        inverse_ref[...],
        band,
        (((1,), (1,)), ((), ())),
        precision=PRECISE,
        preferred_element_type=F32,
    )
    tall = jnp.where(iota((rows * SUB, rows), 0) // SUB == iota((rows * SUB, rows), 1), 1.0, 0.0)
    flat = jnp.where(iota((wide, wide * SUB), 1) // SUB == iota((wide, wide * SUB), 0), 1.0, 0.0)
    big = (rows * SUB, wide * SUB)
    same = iota(big, 0) % SUB == iota(big, 1) % SUB
    parts = []
    for part in split(small):
        spread = dot(dot(tall.astype(BF16), part).astype(BF16), flat.astype(BF16))
        parts.append(jnp.where(same, spread, 0.0).astype(BF16))
    return jnp.concatenate(parts, axis=0)


def derive_kernel(
    stencil_ref,
    inverse_ref,
    low_ref,
    velocity_ref,
    low_edge_ref,
    middle_ref,
    high_edge_ref,
    high_ref,
    piece_ref,
    grad_ref,
    force_ref,
    passed_ref,
    matrix_ref,
):
    radii, angles, axial = velocity_ref.shape[1:]

    passed_ref[...] = piece_ref[...]

    @pl.when(pl.program_id(0) == 0)
    def _():
        matrix_ref[...] = derivative_matrix(stencil_ref, inverse_ref)

    group = radii * SUB

    for i in range(angles // SUB):
        at = pl.ds(i * SUB, SUB)
        columns = []
        own = [
            [velocity_ref],
            [low_edge_ref.at[0], middle_ref, high_edge_ref.at[0]],
        ]
        for f in range(2):
            refs = [low_ref.at[f]] + own[f] + [high_ref.at[f]]
            for c in range(3):
                value = jnp.concatenate([ref[c, :, at, :] for ref in refs], axis=0)
                columns.append(value.reshape((radii + 2 * HALO) * SUB, axial))
        field_high, field_low = split(jnp.concatenate(columns, axis=1))
        result = dot3(matrix_ref[...], field_high, field_low)
        for c in range(3):
            force = TIME_STEP * result[:, (3 + c) * axial : (4 + c) * axial]
            force_ref[c, :, at, :] = force.reshape(radii, SUB, axial)
        turned_high, turned_low = split(result[:, : 3 * axial].T)
        cols = pl.ds(i * group, group)
        grad_ref[: 3 * axial, cols] = turned_high
        grad_ref[3 * axial :, cols] = turned_low

def derive(stencil, inverse, low, velocity, stress, high, piece):
    low_edge, middle, high_edge = stress
    radii, angles, axial = velocity.shape[1:]
    part = 2 * SUB
    steps = angles // part
    assert piece.shape[0] % steps == 0
    piece_block = pl.BlockSpec((piece.shape[0] // steps, angles, axial), lambda i: (i, 0, 0))

    def block(count, first=None):
        if first is None:
            return pl.BlockSpec((3, count, part, axial), lambda i: (0, 0, i, 0))
        return pl.BlockSpec((2 - first, 3, count, part, axial), lambda i: (first, 0, 0, i, 0))

    return pl.pallas_call(
        derive_kernel,
        grid=(steps,),
        in_specs=[
            pl.BlockSpec(stencil.shape, lambda i: (0, 0)),
            pl.BlockSpec(inverse.shape, lambda i: (0, 0)),
            block(HALO, 0),
            block(radii),
            block(HALO, 1),
            block(radii - 2 * HALO),
            block(HALO, 1),
            block(HALO, 0),
            piece_block,
        ],
        out_specs=[
            pl.BlockSpec((6 * axial, radii * part), lambda i: (0, i)),
            block(radii),
            piece_block,
        ],
        out_shape=[
            pltpu.HBM((6 * axial, radii * angles), BF16),
            pltpu.HBM(velocity.shape, F32),
            pltpu.HBM(piece.shape, F32),
        ],
        scratch_shapes=[
            pltpu.VMEM((2 * radii * SUB, (radii + 2 * HALO) * SUB), BF16),
        ],
        compiler_params=pltpu.CompilerParams(vmem_limit_bytes=28 * MIB),
        cost_estimate=pl.CostEstimate(
            flops=3600 * radii * radii * angles * axial // 8,
            bytes_accessed=40 * radii * angles * axial,
            transcendentals=0,
        ),
        name="derive",
    )(
        stencil,
        inverse,
        in_vmem(low),
        in_hbm(velocity),
        in_hbm(low_edge),
        in_hbm(middle),
        in_hbm(high_edge),
        in_vmem(high),
        in_hbm(piece),
    )


def move_kernel(grad_ref, ids_ref, spring_ref, noise_ref, moved_ref, *, angles):
    axial, cells = grad_ref.shape[0] // 6, grad_ref.shape[1]
    group = cells // angles * SUB

    count = spring_ref.shape[3]
    part = min(count, 1024)

    def read(i, carry):
        at = pl.ds(pl.multiple_of(i * part, part), part)
        plane = ids_ref[0, 0, :, at]
        radius, angle = plane // angles, plane % angles
        column = (angle // SUB) * group + radius * SUB + angle % SUB
        hot = jnp.where(iota((cells, part), 0) == column, 1.0, 0.0).astype(BF16)
        picked = dot(grad_ref[...], hot)
        here = iota((axial, part), 0) == ids_ref[1, 0, :, at]
        q = [spring_ref[c, 0, :, at] for c in range(3)]
        stretch_sq = q[0] * q[0] + q[1] * q[1] + q[2] * q[2]
        factor = 1.0 / (1.0 - stretch_sq / MAX_STRETCH)
        for c in range(3):
            value = (
                picked[c * axial : (c + 1) * axial] + picked[(3 + c) * axial : (4 + c) * axial]
            )
            shear = jnp.sum(jnp.where(here, value, 0.0), axis=0, keepdims=True)
            moved_ref[c, 0, :, at] = (
                q[c]
                + TIME_STEP * (shear * q[0] - 0.5 * factor * q[c])
                + math.sqrt(TIME_STEP) * noise_ref[c, 0, :, at]
            )
        return carry

    lax.fori_loop(0, count // part, read, 0)


def move(grad, ids, spring, noise, angles):
    cells = grad.shape[1]
    whole = pl.BlockSpec(memory_space=pltpu.VMEM)
    return pl.pallas_call(
        functools.partial(move_kernel, angles=angles),
        in_specs=[whole] * 4,
        out_specs=whole,
        out_shape=jax.ShapeDtypeStruct(spring.shape, F32),
        compiler_params=pltpu.CompilerParams(vmem_limit_bytes=24 * MIB),
        cost_estimate=pl.CostEstimate(
            flops=2 * grad.size * spring.shape[3],
            bytes_accessed=2 * grad.size,
            transcendentals=0,
        ),
        name="move",
    )(in_hbm(grad), ids, spring, noise)


def fourier_tables(all_angles):
    half = all_angles // 2
    row = np.arange(half)
    quarter = half // 2
    waves = [
        np.where(row <= quarter, 2 * row, 2 * (row - quarter)),
        np.where(row < quarter, 2 * row + 1, 2 * (row - quarter) + 1),
    ]
    cosine = [row <= quarter, row < quarter]
    tables = []
    for wave, even in zip(waves, cosine):
        phase = (wave[:, None] * row[None, :]) % all_angles
        angle = phase * (2.0 * math.pi / all_angles)
        table = np.where(even[:, None], np.cos(angle), np.sin(angle))
        weight = np.where((wave == 0) | (wave == half), 1.0, 2.0) / all_angles
        for value in (table, table.T * weight[None, :]):
            value = value.astype(np.float32)
            high = value.astype(BF16)
            low = (value - high.astype(np.float32)).astype(BF16)
            tables.append(np.concatenate([high, low], axis=0))
    return np.stack(tables)


def solve_kernel(coef_ref, me_ref, tables_ref, *refs, extra):
    in_ref, refs = refs[extra], refs[extra + 1 :]
    blocks, rows, angles, axial = in_ref.shape
    out_refs = refs[:blocks]
    table_ref, done_ref, table_sems, out_sems = refs[blocks:]
    half = blocks * angles // 2
    quarter = half // 2
    part = math.gcd(rows, 2)
    loads = [
        pltpu.make_async_copy(tables_ref.at[i], table_ref.at[i], table_sems.at[i])
        for i in range(4)
    ]
    for copy in loads:
        copy.start()

    base = me_ref[0] * rows
    lane = iota((1, axial), 1)
    coef = jnp.zeros((1, axial), F32)
    for q in range(rows):
        coef = jnp.where(lane == q, coef_ref[lax.rem(base + q, coef_ref.shape[0])], coef)
    row = iota((half, axial), 0)
    waves = [
        jnp.where(row <= quarter, 2 * row, 2 * (row - quarter)),
        jnp.where(row < quarter, 2 * row + 1, 2 * (row - quarter) + 1),
    ]
    damping = [1.0 / (1.0 + coef * (wave * wave).astype(F32)) for wave in waves]

    stores = []
    for g in range(rows // part):
        chosen = range(g * part, (g + 1) * part)
        near = [in_ref[: blocks // 2, q].reshape(half, axial) for q in chosen]
        far = [in_ref[blocks // 2 :, q].reshape(half, axial) for q in chosen]
        results = []
        for odd in range(2):
            field = jnp.concatenate([a - b if odd else a + b for a, b in zip(near, far)], axis=1)
            if g == 0:
                loads[2 * odd].wait()
            spectrum = dot3(table_ref[2 * odd], *split(field))
            scale = [
                jnp.broadcast_to(damping[odd][:, q : q + 1], (half, axial)) for q in chosen
            ]
            if g == 0:
                loads[2 * odd + 1].wait()
            damped = spectrum * jnp.concatenate(scale, axis=1)
            results.append(dot3(table_ref[2 * odd + 1], *split(damped)))
        for i, q in enumerate(chosen):
            even, odd = [value[:, i * axial : (i + 1) * axial] for value in results]
            done_ref[: blocks // 2, q] = (even + odd).reshape(blocks // 2, angles, axial)
            done_ref[blocks // 2 :, q] = (even - odd).reshape(blocks // 2, angles, axial)
        at = pl.ds(g * part, part)
        for s, partner in enumerate(partners(blocks)):
            stores.append(
                pltpu.make_async_copy(
                    done_ref.at[me_ref[0] ^ partner, at], out_refs[s].at[at], out_sems.at[g, s]
                )
            )
            stores[-1].start()
    for copy in stores:
        copy.wait()


def solve(coef, me, field, after):
    blocks, rows, angles, axial = field.shape
    all_angles = blocks * angles
    tables = fourier_tables(all_angles)
    smem = pl.BlockSpec(memory_space=pltpu.SMEM)
    whole = pl.BlockSpec(memory_space=pltpu.VMEM)
    unread = pl.BlockSpec(memory_space=pl.ANY)
    return pl.pallas_call(
        functools.partial(solve_kernel, extra=len(after)),
        in_specs=[smem, smem, unread] + [unread] * len(after) + [whole],
        out_specs=[unread] * blocks,
        out_shape=[pltpu.HBM(field.shape[1:], F32)] * blocks,
        scratch_shapes=[
            pltpu.VMEM(tables.shape, BF16),
            pltpu.VMEM(field.shape, F32),
            pltpu.SemaphoreType.DMA((4,)),
            pltpu.SemaphoreType.DMA((rows // math.gcd(rows, 2), blocks)),
        ],
        compiler_params=pltpu.CompilerParams(vmem_limit_bytes=28 * MIB),
        cost_estimate=pl.CostEstimate(
            flops=12 * all_angles * all_angles * rows * axial,
            bytes_accessed=8 * all_angles * rows * axial,
            transcendentals=0,
        ),
        name="solve",
    )(
        coef,
        me,
        in_hbm(jnp.asarray(tables)),
        *after,
        in_vmem(field),
    )


def join_kernel(me_ref, force_ref, *refs, first, given):
    count = len(refs) - 4 - given
    piece_refs, refs = refs[:count], refs[count + given :]
    out_ref, sum_ref, in_sems, out_sems = refs
    rows = sum_ref.shape[1]
    order = partners(force_ref.shape[0] // rows)
    reads, writes = [], []
    for i in range(count):
        at = pl.ds((me_ref[0] ^ order[first + i]) * rows, rows)
        reads.append(pltpu.make_async_copy(force_ref.at[at], sum_ref.at[i], in_sems.at[i]))
        writes.append(pltpu.make_async_copy(sum_ref.at[i], out_ref.at[at], out_sems.at[i]))
    for copy in reads:
        copy.start()
    for i in range(count):
        reads[i].wait()
        sum_ref[i] = sum_ref[i] + piece_refs[i][...]
        writes[i].start()
    for copy in writes:
        copy.wait()


def join(me, force, pieces, first, result=None):
    rows, angles, axial = pieces[0].shape
    count = len(pieces)
    given = [] if result is None else [in_hbm(result)]
    whole = pl.BlockSpec(memory_space=pltpu.VMEM)
    away = pl.BlockSpec(memory_space=pl.ANY)
    return pl.pallas_call(
        functools.partial(join_kernel, first=first, given=len(given)),
        in_specs=[pl.BlockSpec(memory_space=pltpu.SMEM), away]
        + [whole] * count
        + [away] * len(given),
        out_specs=away,
        out_shape=pltpu.HBM(force.shape, F32),
        input_output_aliases={2 + count: 0} if given else {},
        scratch_shapes=[
            pltpu.VMEM((count, rows, angles, axial), F32),
            pltpu.SemaphoreType.DMA((count,)),
            pltpu.SemaphoreType.DMA((count,)),
        ],
        compiler_params=pltpu.CompilerParams(vmem_limit_bytes=14 * MIB),
        cost_estimate=pl.CostEstimate(
            flops=count * rows * angles * axial,
            bytes_accessed=12 * count * rows * angles * axial,
            transcendentals=0,
        ),
        name="join",
    )(me, in_hbm(force), *pieces, *given)


def exchange(pieces):
    count = len(pieces)
    received = [pieces[0]]
    for piece, partner in list(zip(pieces, partners(count)))[1:]:
        received.append(lax.ppermute(piece, "az", [(i, i ^ partner) for i in range(count)]))
    return received


def from_neighbours(low_edge, high_edge):
    count = lax.axis_size("rad")
    forward = [(i, i + 1) for i in range(count - 1)]
    backward = [(target, source) for source, target in forward]
    low = lax.ppermute(high_edge, "rad", forward)
    high = lax.ppermute(low_edge, "rad", backward)
    return low, high


def per_device(velocity, dumbbells, cell_ids, brownian, stencil_coef, block_inverse, azim_coef):
    _, radii, angles, axial = velocity.shape
    az = lax.axis_size("az")
    rows = 3 * radii // az
    pieces = velocity.reshape(az, rows, angles, axial)
    gathered = lax.all_to_all(pieces, "az", 0, 0, tiled=True)
    low_edge, high_edge = deposit_edges(cell_ids, dumbbells, velocity)
    low, high = from_neighbours(low_edge, high_edge)
    middle = deposit_middle(cell_ids, dumbbells, low_edge, velocity.shape)
    stress = (low_edge, middle, high_edge)
    me = lax.axis_index("az").astype(jnp.int32).reshape(1)
    solved = solve(azim_coef, me, gathered, (in_vmem(low), in_vmem(high), in_hbm(middle)))
    grad, force, passed = derive(
        stencil_coef, block_inverse, low, velocity, stress, high, solved[-1]
    )
    pieces = exchange(list(solved[:-1]) + [passed])
    moved = move(grad, cell_ids, dumbbells, brownian, angles)
    lines = (3 * radii, angles, axial)
    force = force.reshape(lines)
    early = len(pieces) * 3 // 8
    result = join(me, force, pieces[:early], 0)
    result = join(me, force, [in_vmem(piece) for piece in pieces[early:]], early, result)
    return result.reshape(velocity.shape), moved


def solution(mesh):
    placed = (
        P(None, "rad", "az", None),
        P(None, "rad", "az", None),
        P(None, "rad", "az", None),
        P(None, "rad", "az", None),
        P(None, "rad"),
        P("rad", None),
        P("rad"),
    )
    return jax.shard_map(
        per_device,
        mesh=mesh,
        in_specs=placed,
        out_specs=(P(None, "rad", "az", None), P(None, "rad", "az", None)),
        check_vma=False,
    )
```
